32 devices in a mesh: fsdp: 16 (over z, x, core), seq: 2 (over y).
Axes of the slice: x: 2, y: 2, z: 4, core: 2. Of those that a mesh axis runs over, the one named last changes fastest.
Arguments:
- tokens: bfloat16 [32, 1024, 1152], P('fsdp', 'seq'), may hold values from -6 to 6
- condition: float32 [32, 1152], P('fsdp'), may hold values from -6 to 6
- adapter: int32 [32], P('fsdp'), may hold values from 0 to 7, as said below
- cotangent: bfloat16 [32, 1024, 1152], P('fsdp', 'seq'), may hold values from -6 to 6
- modulation_weight: bfloat16 [1152, 6912], P('fsdp', 'seq'), may hold values from -0.1875 to 0.1875
- modulation_bias: float32 [6912], replicated, may hold values from -3 to 3
- query_key_value_weight: bfloat16 [1152, 3456], P('fsdp', 'seq'), may hold values from -0.1875 to 0.1875
- attention_out_weight: bfloat16 [1152, 1152], P('fsdp', 'seq'), may hold values from -0.75 to 0.75
- attention_out_bias: float32 [1152], replicated, may hold values from -1.75 to 1.75
- widen_weight: bfloat16 [1152, 4608], P('fsdp', 'seq'), may hold values from -0.1875 to 0.1875
- widen_bias: float32 [4608], replicated, may hold values from -3 to 3
- narrow_weight: bfloat16 [4608, 1152], P('fsdp', 'seq'), may hold values from -0.09375 to 0.09375
- narrow_bias: float32 [1152], replicated, may hold values from -1.75 to 1.75
- lowrank_down: float32 [8, 16, 9216], P('seq', None, 'fsdp'), may hold values from -0.1875 to 0.1875
- lowrank_up: float32 [8, 16, 17280], P('seq', None, 'fsdp'), may hold values from -0.5 to 0.5
- first_moment_down: float32 [8, 16, 9216], P('seq', None, 'fsdp'), may hold values from -0.00036621094 to 0.00036621094
- first_moment_up: float32 [8, 16, 17280], P('seq', None, 'fsdp'), may hold values from -0.00036621094 to 0.00036621094
- second_moment_down: float32 [8, 16, 9216], P('seq', None, 'fsdp'), may hold values from 1.4742791e-09 to 1.4742791e-08
- second_moment_up: float32 [8, 16, 17280], P('seq', None, 'fsdp'), may hold values from 8.845675e-11 to 8.845675e-10
Outputs:
- block_out: bfloat16 [32, 1024, 1152], P('fsdp', 'seq')
- token_grad: float32 [32, 1024, 1152], P('fsdp', 'seq')
- cond_grad: float32 [32, 1152], P('fsdp')
- grad_norm: float32 [], replicated
- stepped_down: float32 [8, 16, 9216], P('seq', None, 'fsdp')
- stepped_up: float32 [8, 16, 17280], P('seq', None, 'fsdp')
- next_first_down: float32 [8, 16, 9216], P('seq', None, 'fsdp')
- next_first_up: float32 [8, 16, 17280], P('seq', None, 'fsdp')
- next_second_down: float32 [8, 16, 9216], P('seq', None, 'fsdp')
- next_second_up: float32 [8, 16, 17280], P('seq', None, 'fsdp')
The draws below stay inside these ranges and needn't reach their ends.
Inputs may be any that keep to these rules, and one draw needn't show every extreme that they name: Sequence s uses adapter[s]; the values never fall from one sequence to the next, and each of the 8 adapters is used by at least one sequence.
All inputs are finite; a program needn't handle non-finite values.
Results may differ from the reference program's by a relative error of at most 0.025.
The reference program's roundings to bfloat16 on the way count: a program that leaves them out, or rounds other values in their place, can miss the bound.
Values may be sent and summed in bfloat16 or wider, within the bound.
No kernel may reach another device: no remote copies, remote signals or barrier semaphores. Data moves between devices by JAX's collectives and lax.ppermute only.
A program may use at most 256 MiB of HBM per device.

```python
import math
import jax
import jax.numpy as jnp
from jax import lax

MODEL_WIDTH = 1152
HEADS = 16
HD = 72
FF = 4608
ADAPTER_RANK = 16
ADAPTER_COUNT = 8
LEN = 1024
STEP = 10
SEQS = 32
DOWN_COLUMNS = 9216
UP_COLUMNS = 17280
NPAR = 3391488


def draw_adapter(key, part):
    extra_ids = jax.random.randint(key, (SEQS - ADAPTER_COUNT,), 0, ADAPTER_COUNT).astype(jnp.int32)
    every_id = jnp.arange(ADAPTER_COUNT, dtype=jnp.int32)
    return jnp.sort(jnp.concatenate([every_id, extra_ids]))


def levels(rng, dims, shards, low, high):
    def one(position, blocks):
        draws = jax.random.uniform(jax.random.fold_in(jax.random.fold_in(rng, 6), position), (blocks,), jnp.float32, low / len(shards), high / len(shards))
        return jnp.repeat(jnp.exp(draws), dims[position] // blocks).reshape((-1,) + (1,) * (len(dims) - position - 1))

    gain = one(*shards[0])
    for cut in shards[1:]:
        gain = gain * one(*cut)
    return gain


def gaussian(own_key, dims, scale, reach, pieces=(), kind=jnp.bfloat16):
    drawn = jax.random.normal(own_key, dims, jnp.float32) * scale
    if len(pieces) > 0:
        drawn = levels(own_key, dims, pieces, -0.22, 0.18) * drawn
    return jnp.clip(drawn, min=-reach, max=reach).astype(kind)


def setup_inputs(seed: int = 0) -> dict:
    key_list = jax.random.split(jax.random.key(seed), 20)
    return {
        "tokens": gaussian(key_list[0], (SEQS, LEN, MODEL_WIDTH), 1.0, 6.0, ((0, 16), (1, 2))),
        "condition": gaussian(key_list[1], (SEQS, MODEL_WIDTH), 1.0, 6.0, ((0, 16),), jnp.float32),
        "adapter": draw_adapter(jax.random.fold_in(key_list[19], 71), 0),
        "cotangent": gaussian(key_list[3], (SEQS, LEN, MODEL_WIDTH), 1.0, 6.0, ((0, 16), (1, 2))),
        "modulation_weight": gaussian(key_list[4], (MODEL_WIDTH, 6 * MODEL_WIDTH), MODEL_WIDTH ** -0.5, 0.1875, ((0, 16), (1, 2))),
        "modulation_bias": gaussian(key_list[5], (6 * MODEL_WIDTH,), 0.5, 3.0, (), jnp.float32),
        "query_key_value_weight": gaussian(key_list[6], (MODEL_WIDTH, 3 * MODEL_WIDTH), MODEL_WIDTH ** -0.5, 0.1875, ((0, 16), (1, 2))),
        "attention_out_weight": gaussian(key_list[7], (MODEL_WIDTH, MODEL_WIDTH), (MODEL_WIDTH // 16) ** -0.5, 0.75, ((0, 16), (1, 2))),
        "attention_out_bias": gaussian(key_list[8], (MODEL_WIDTH,), 0.3, 1.75, (), jnp.float32),
        "widen_weight": gaussian(key_list[9], (MODEL_WIDTH, FF), MODEL_WIDTH ** -0.5, 0.1875, ((0, 16), (1, 2))),
        "widen_bias": gaussian(key_list[10], (FF,), 0.5, 3.0, (), jnp.float32),
        "narrow_weight": gaussian(key_list[11], (FF, MODEL_WIDTH), FF ** -0.5, 0.09375, ((0, 16), (1, 2))),
        "narrow_bias": gaussian(key_list[12], (MODEL_WIDTH,), 0.3, 1.75, (), jnp.float32),
        "lowrank_down": gaussian(key_list[13], (ADAPTER_COUNT, ADAPTER_RANK, DOWN_COLUMNS), MODEL_WIDTH ** -0.5, 0.1875, ((0, 2), (2, 16)), jnp.float32),
        "lowrank_up": gaussian(key_list[14], (ADAPTER_COUNT, ADAPTER_RANK, UP_COLUMNS), 0.08, 0.5, ((0, 2), (2, 16)), jnp.float32),
        "first_moment_down": gaussian(key_list[15], (ADAPTER_COUNT, ADAPTER_RANK, DOWN_COLUMNS), (0.11 * NPAR ** -0.5), 0.00036621094, ((0, 2), (2, 16)), jnp.float32),
        "first_moment_up": gaussian(key_list[16], (ADAPTER_COUNT, ADAPTER_RANK, UP_COLUMNS), (0.11 * NPAR ** -0.5), 0.00036621094, ((0, 2), (2, 16)), jnp.float32),
        "second_moment_down": jnp.clip(jnp.exp(math.log(1.4742790988009347e-08) - 2.3025851 * jax.random.uniform(key_list[17], (ADAPTER_COUNT, ADAPTER_RANK, DOWN_COLUMNS), jnp.float32) ** levels(key_list[17], (ADAPTER_COUNT, ADAPTER_RANK, DOWN_COLUMNS), ((0, 2), (2, 16)), -0.2, 0.2)), 1.4742791432098556e-09, 1.4742790988009347e-08),
        "second_moment_up": jnp.clip(jnp.exp(math.log(8.845674748236831e-10) - 2.3025851 * jax.random.uniform(key_list[18], (ADAPTER_COUNT, ADAPTER_RANK, UP_COLUMNS), jnp.float32) ** levels(key_list[18], (ADAPTER_COUNT, ADAPTER_RANK, UP_COLUMNS), ((0, 2), (2, 16)), -0.2, 0.2)), 8.84567488701471e-11, 8.845674748236831e-10),
    }


@jax.custom_vjp
def low(v):
    return lax.optimization_barrier(v.astype(jnp.bfloat16)).astype(jnp.float32)

@jax.custom_vjp
def low_back(v):
    return v

def low_keep(v):
    return (low(v), None)

def low_pass(kept, grad):
    return (grad,)

def back_keep(v):
    return (v, None)

def back_low(kept, grad):
    return (low(grad),)
low.defvjp(low_keep, low_pass)
low_back.defvjp(back_keep, back_low)
beta_first = 0.9
beta_second = 0.999
learn_rate = 0.05
decay_rate = 0.1
adam_eps = 1e-08
clip_limit = 1.0
norm_eps = 1e-06
highest = lax.Precision.HIGHEST

def matmul(left_side, right_side):
    return jnp.dot(left_side, right_side, precision=highest, preferred_element_type=jnp.float32)

def normalize(stream):
    center = stream - lax.optimization_barrier(jnp.mean(stream, -1, keepdims=True))
    return center * lax.rsqrt(lax.optimization_barrier(jnp.mean(center * center, -1, keepdims=True)) + norm_eps)

def adapted(inputs, down_all, up_all, down_from, down_to, up_from, up_to):
    middle = low(low_back(matmul(inputs, down_all[:, down_from:down_to].T)))
    return matmul(middle, up_all[:, up_from:up_to])

def attention(queries, key_rows, value_rows):
    length = queries.shape[0]

    def split_heads(matrix):
        return matrix.reshape(length, HEADS, HD).transpose(1, 0, 2)
    raw_scores = low_back(jnp.einsum('hqd,hkd->hqk', split_heads(queries), split_heads(key_rows), precision=highest))
    weights = low(jax.nn.softmax(raw_scores * HD ** (-0.5), axis=-1))
    mixed_heads = jnp.einsum('hqk,hkd->hqd', weights, split_heads(value_rows), precision=highest)
    return mixed_heads.transpose(1, 0, 2).reshape(length, HEADS * HD)

def block(token_rows, cond_row, down_all, up_all, frozen_set):
    modulation_weight, modulation_bias, query_key_value_weight, attention_out_weight, attention_out_bias, widen_weight, widen_bias, narrow_weight, narrow_bias = frozen_set
    down_all = low(down_all)
    up_all = low(up_all)
    cond_act = low(jax.nn.silu(cond_row))[None, :]
    modulation = low_back(matmul(cond_act, modulation_weight) + modulation_bias + adapted(cond_act, down_all, up_all, 0, MODEL_WIDTH, 0, 6 * MODEL_WIDTH))[0]
    shift_first, scale_first, gate_first, shift_second, scale_second, gate_second = jnp.split(modulation, 6)
    hidden = low(normalize(token_rows) * (1.0 + scale_first) + shift_first)
    packed = matmul(hidden, query_key_value_weight) + adapted(hidden, down_all, up_all, MODEL_WIDTH, 2 * MODEL_WIDTH, 6 * MODEL_WIDTH, 9 * MODEL_WIDTH)
    queries = low(low_back(packed[:, :MODEL_WIDTH]))
    key_rows = low(low_back(packed[:, MODEL_WIDTH:2 * MODEL_WIDTH]))
    value_rows = low(low_back(packed[:, 2 * MODEL_WIDTH:]))
    mixed = low(low_back(attention(queries, key_rows, value_rows)))
    branch = low_back(matmul(mixed, attention_out_weight) + attention_out_bias + adapted(mixed, down_all, up_all, 2 * MODEL_WIDTH, 3 * MODEL_WIDTH, 9 * MODEL_WIDTH, 10 * MODEL_WIDTH))
    residual = token_rows + gate_first * branch
    second = low(normalize(residual) * (1.0 + scale_second) + shift_second)
    inner_act = low_back(matmul(second, widen_weight) + widen_bias + adapted(second, down_all, up_all, 3 * MODEL_WIDTH, 4 * MODEL_WIDTH, 10 * MODEL_WIDTH, 10 * MODEL_WIDTH + FF))
    active = low(jax.nn.gelu(inner_act, approximate=True))
    final_out = low_back(matmul(active, narrow_weight) + narrow_bias + adapted(active, down_all, up_all, 4 * MODEL_WIDTH, 4 * MODEL_WIDTH + FF, 10 * MODEL_WIDTH + FF, 11 * MODEL_WIDTH + FF))
    return residual + gate_second * final_out

def reference(tokens, condition, adapter, cotangent, modulation_weight, modulation_bias, query_key_value_weight, attention_out_weight, attention_out_bias, widen_weight, widen_bias, narrow_weight, narrow_bias, lowrank_down, lowrank_up, first_moment_down, first_moment_up, second_moment_down, second_moment_up):
    frozen_set = tuple((weight.astype(jnp.float32) for weight in (modulation_weight, modulation_bias, query_key_value_weight, attention_out_weight, attention_out_bias, widen_weight, widen_bias, narrow_weight, narrow_bias)))

    def per_sequence(running, seq_item):
        down_gradient, up_gradient = running
        sequence_token_rows, sequence_condition, picked_adapter, seq_cot = seq_item

        def forward_pass(token_rows, cond_row, down_rows, up_rows):
            return block(token_rows, cond_row, down_rows, up_rows, frozen_set)
        outcome_value, backward_function = jax.vjp(forward_pass, sequence_token_rows.astype(jnp.float32), sequence_condition, lowrank_down[picked_adapter], lowrank_up[picked_adapter])
        token_grad, cond_grad, down_grad, up_grad = backward_function(seq_cot.astype(jnp.float32))
        updated = (down_gradient.at[picked_adapter].add(down_grad), up_gradient.at[picked_adapter].add(up_grad))
        return (updated, (outcome_value.astype(jnp.bfloat16), token_grad, cond_grad))
    offset_index = (jnp.zeros(lowrank_down.shape, jnp.float32), jnp.zeros(lowrank_up.shape, jnp.float32))
    (down_gradient, up_gradient), (block_out, token_grad, cond_grad) = lax.scan(per_sequence, offset_index, (tokens, condition, adapter, cotangent))
    grad_norm = jnp.sqrt(jnp.sum(down_gradient * down_gradient) + jnp.sum(up_gradient * up_gradient))
    clip_factor = jnp.minimum(1.0, clip_limit / (grad_norm + norm_eps))

    def optimizer_update(params, gradient, moment, square):
        gradient = gradient * clip_factor
        moment_new = beta_first * moment + (1.0 - beta_first) * gradient
        square_new = beta_second * square + (1.0 - beta_second) * gradient * gradient
        direction = moment_new / (1.0 - beta_first ** STEP) / (jnp.sqrt(square_new / (1.0 - beta_second ** STEP)) + adam_eps)
        return (params - learn_rate * (direction + decay_rate * params), moment_new, square_new)
    stepped_down, next_first_down, next_second_down = optimizer_update(lowrank_down, down_gradient, first_moment_down, second_moment_down)
    stepped_up, next_first_up, next_second_up = optimizer_update(lowrank_up, up_gradient, first_moment_up, second_moment_up)
    return (block_out, token_grad, cond_grad, grad_norm, stepped_down, stepped_up, next_first_down, next_first_up, next_second_down, next_second_up)
```

```python
import functools

import jax
import jax.numpy as jnp
from jax import lax
from jax.experimental import pallas as pl
from jax.experimental.pallas import tpu as pltpu
from jax.sharding import PartitionSpec as P

MODEL_WIDTH = 1152
HD = 72
FF = 4608
ADAPTER_RANK = 16
ADAPTER_COUNT = 8
MB = 2
SEQ_MB = 1
STEP = 10


beta_first = 0.9
beta_second = 0.999
learn_rate = 0.05
decay_rate = 0.1
adam_eps = 1e-08
clip_limit = 1.0
norm_eps = 1e-06
pair_heads = 2
highest = lax.Precision.HIGHEST


def linear(inputs, weight):
    return jnp.einsum("sti,io->sto", inputs, weight, preferred_element_type=jnp.float32)


def linear_back(gradient, weight):
    return jnp.einsum("sto,io->sti", gradient, weight, preferred_element_type=jnp.float32)


def normalize(stream):
    center = stream - jnp.mean(stream, -1, keepdims=True)
    inverse = lax.rsqrt(jnp.mean(center * center, -1, keepdims=True) + norm_eps)
    return (center * inverse, inverse)


def normalize_back(gradient, normed, inverse):
    return inverse * (
        gradient
        - jnp.mean(gradient, -1, keepdims=True)
        - normed * jnp.mean(gradient * normed, -1, keepdims=True)
    )


def adapt_forward(inputs, down_part, up_part):
    middle = jnp.einsum(
        "sti,sri->str", inputs, down_part, preferred_element_type=jnp.float32
    ).astype(jnp.bfloat16)
    return (middle, jnp.einsum("str,sro->sto", middle, up_part, preferred_element_type=jnp.float32))


def adapt_backward(inputs, middle, gradient, down_part, up_part):
    up_grad = jnp.einsum("str,sto->sro", middle, gradient, preferred_element_type=jnp.float32)
    middle_grad = jnp.einsum(
        "sto,sro->str", gradient, up_part, preferred_element_type=jnp.float32
    ).astype(jnp.bfloat16)
    down_grad = jnp.einsum("str,sti->sri", middle_grad, inputs, preferred_element_type=jnp.float32)
    input_grad = jnp.einsum(
        "str,sri->sti", middle_grad, down_part, preferred_element_type=jnp.float32
    )
    return (input_grad, down_grad, up_grad)


def grouped(matrix):
    seq_count, row_count, col_count = matrix.shape
    return jnp.moveaxis(
        matrix.reshape(seq_count, row_count, col_count // (pair_heads * HD), pair_heads, HD), 2, 0
    )


def ungrouped(stacked):
    moved = jnp.moveaxis(stacked, 0, 2)
    return moved.reshape(moved.shape[0], moved.shape[1], -1)


def attend_group(group_inputs):
    queries, all_keys, all_values = group_inputs
    factor = queries.shape[-1] ** (-0.5)
    scores = (
        jnp.einsum("sqhd,skhd->shqk", queries, all_keys, preferred_element_type=jnp.float32)
        * factor
    )
    row_max = jnp.max(scores, -1, keepdims=True)
    exponent = jnp.exp(scores - row_max)
    row_total = jnp.sum(exponent, -1, keepdims=True)
    weights = (exponent / row_total).astype(jnp.bfloat16)
    mixed_heads = jnp.einsum(
        "shqk,skhd->sqhd", weights, all_values, preferred_element_type=jnp.float32
    )
    return (mixed_heads, row_max + jnp.log(row_total))


def attend_back(group_inputs):
    queries, all_keys, all_values, d_mixed, log_total = group_inputs
    factor = queries.shape[-1] ** (-0.5)
    scores = (
        jnp.einsum("sqhd,skhd->shqk", queries, all_keys, preferred_element_type=jnp.float32)
        * factor
    )
    probable = jnp.exp(scores - log_total)
    d_values = jnp.einsum(
        "shqk,sqhd->skhd",
        probable.astype(jnp.bfloat16),
        d_mixed,
        preferred_element_type=jnp.float32,
    )
    d_weights = jnp.einsum(
        "sqhd,skhd->shqk", d_mixed, all_values, preferred_element_type=jnp.float32
    )
    inner_sum = jnp.sum(d_weights * probable, -1, keepdims=True)
    d_scores = (probable * (d_weights - inner_sum) * factor).astype(jnp.bfloat16)
    d_queries = jnp.einsum(
        "shqk,skhd->sqhd", d_scores, all_keys, preferred_element_type=jnp.float32
    )
    d_keys = jnp.einsum("shqk,sqhd->skhd", d_scores, queries, preferred_element_type=jnp.float32)
    return (d_queries, d_keys, d_values)


def gelu_tanh(inner_act):
    return jax.nn.gelu(inner_act, approximate=True)


def shards(
    tokens,
    condition,
    adapter,
    cotangent,
    modulation_weight,
    modulation_bias,
    query_key_value_weight,
    attention_out_weight,
    attention_out_bias,
    widen_weight,
    widen_bias,
    narrow_weight,
    narrow_bias,
    lowrank_down,
    lowrank_up,
    first_moment_down,
    first_moment_up,
    second_moment_down,
    second_moment_up,
):
    seq_count_axis = lax.axis_size("seq")
    seq_share = 1.0 / seq_count_axis
    down_portion = lowrank_down.astype(jnp.bfloat16)
    up_portion = lowrank_up.astype(jnp.bfloat16)
    down_edges = (
        0,
        MODEL_WIDTH,
        2 * MODEL_WIDTH,
        3 * MODEL_WIDTH,
        4 * MODEL_WIDTH,
        4 * MODEL_WIDTH + FF,
    )
    up_edges = (
        0,
        6 * MODEL_WIDTH,
        9 * MODEL_WIDTH,
        10 * MODEL_WIDTH,
        10 * MODEL_WIDTH + FF,
        11 * MODEL_WIDTH + FF,
    )

    def fetch():
        across = (
            lax.all_gather(modulation_weight, "seq", axis=1, tiled=True),
            lax.all_gather(query_key_value_weight, "seq", axis=1, tiled=True),
            lax.all_gather(attention_out_weight, "seq", axis=1, tiled=True),
            lax.all_gather(widen_weight, "seq", axis=1, tiled=True),
            lax.all_gather(narrow_weight, "seq", axis=1, tiled=True),
            lax.all_gather(down_portion, "seq", axis=0, tiled=True),
            lax.all_gather(up_portion, "seq", axis=0, tiled=True),
        )
        return (
            lax.all_gather(across[0], "fsdp", axis=0, tiled=True),
            lax.all_gather(across[1], "fsdp", axis=0, tiled=True),
            lax.all_gather(across[2], "fsdp", axis=0, tiled=True),
            lax.all_gather(across[3], "fsdp", axis=0, tiled=True),
            lax.all_gather(across[4], "fsdp", axis=0, tiled=True),
            lax.all_gather(across[5], "fsdp", axis=2, tiled=True),
            lax.all_gather(across[6], "fsdp", axis=2, tiled=True),
        )

    def select(gathered_now, picked_adapter):
        down_sel = gathered_now[5][picked_adapter]
        up_sel = gathered_now[6][picked_adapter]
        down_blocks = [
            down_sel[:, :, down_edges[target] : down_edges[target + 1]] for target in range(5)
        ]
        up_blocks = [up_sel[:, :, up_edges[target] : up_edges[target + 1]] for target in range(5)]
        return (
            gathered_now[0],
            gathered_now[1],
            gathered_now[2],
            gathered_now[3],
            gathered_now[4],
            down_blocks,
            up_blocks,
        )

    down_gradient = jnp.zeros((ADAPTER_COUNT, ADAPTER_RANK, down_edges[5]), jnp.float32)
    up_gradient = jnp.zeros((ADAPTER_COUNT, ADAPTER_RANK, up_edges[5]), jnp.float32)
    output_list, token_list, cond_list = ([], [], [])
    for micro_batch in range(MB):
        first_seq = micro_batch * SEQ_MB
        token_rows = tokens[first_seq : first_seq + SEQ_MB].astype(jnp.float32)
        cond_rows = condition[first_seq : first_seq + SEQ_MB]
        picked_adapter = adapter[first_seq : first_seq + SEQ_MB]
        cot_rows = cotangent[first_seq : first_seq + SEQ_MB].astype(jnp.float32)
        batch_seqs = token_rows.shape[0]
        local_rows = token_rows.shape[1]
        gathered = fetch()
        full_ada, full_qkv, full_proj, full_expand, full_shrink, down_blocks, up_blocks = select(
            gathered, picked_adapter
        )
        cond_act = jax.nn.silu(cond_rows).astype(jnp.bfloat16)[:, None, :]
        middle_ada, extra_ada = adapt_forward(cond_act, down_blocks[0], up_blocks[0])
        modulation = linear(cond_act, full_ada) + modulation_bias + extra_ada
        shift_first, scale_first, gate_first, shift_second, scale_second, gate_second = jnp.split(
            modulation, 6, axis=-1
        )
        normed_first, inverse_first = normalize(token_rows)
        hidden = (normed_first * (1.0 + scale_first) + shift_first).astype(jnp.bfloat16)
        middle_qkv, extra_qkv = adapt_forward(hidden, down_blocks[1], up_blocks[1])
        packed = (linear(hidden, full_qkv) + extra_qkv).astype(jnp.bfloat16)
        head_blocks = packed.reshape(
            batch_seqs, local_rows, 3, seq_count_axis, MODEL_WIDTH // seq_count_axis
        )
        by_heads = lax.all_to_all(head_blocks, "seq", split_axis=3, concat_axis=1, tiled=True)
        query_groups = grouped(by_heads[:, :, 0, 0])
        key_groups = grouped(by_heads[:, :, 1, 0])
        value_groups = grouped(by_heads[:, :, 2, 0])
        mixed_groups, log_total = lax.map(attend_group, (query_groups, key_groups, value_groups))
        mixed = lax.all_to_all(
            ungrouped(mixed_groups).astype(jnp.bfloat16),
            "seq",
            split_axis=1,
            concat_axis=2,
            tiled=True,
        )
        middle_proj, extra_proj = adapt_forward(mixed, down_blocks[2], up_blocks[2])
        branch = linear(mixed, full_proj) + attention_out_bias + extra_proj
        residual = token_rows + gate_first * branch
        normed_second, inverse_second = normalize(residual)
        second = (normed_second * (1.0 + scale_second) + shift_second).astype(jnp.bfloat16)
        middle_expand, extra_expand = adapt_forward(second, down_blocks[3], up_blocks[3])
        inner_act = linear(second, full_expand) + widen_bias + extra_expand
        active = gelu_tanh(inner_act).astype(jnp.bfloat16)
        middle_shrink, extra_shrink = adapt_forward(active, down_blocks[4], up_blocks[4])
        final_out = linear(active, full_shrink) + narrow_bias + extra_shrink
        output_list.append((residual + gate_second * final_out).astype(jnp.bfloat16))
        gathered = fetch()
        full_ada, full_qkv, full_proj, full_expand, full_shrink, down_blocks, up_blocks = select(
            gathered, picked_adapter
        )
        d_final = (gate_second * cot_rows).astype(jnp.bfloat16)
        d_gate_second = jnp.sum(cot_rows * final_out, axis=1, keepdims=True)
        d_active, down_shrink, up_shrink = adapt_backward(
            active, middle_shrink, d_final, down_blocks[4], up_blocks[4]
        )
        d_active = d_active + linear_back(d_final, full_shrink)
        d_inner = jax.vjp(gelu_tanh, inner_act)[1](d_active)[0].astype(jnp.bfloat16)
        d_second, down_expand, up_expand = adapt_backward(
            second, middle_expand, d_inner, down_blocks[3], up_blocks[3]
        )
        d_second = d_second + linear_back(d_inner, full_expand)
        d_shift_second = jnp.sum(d_second, axis=1, keepdims=True)
        d_scale_second = jnp.sum(d_second * normed_second, axis=1, keepdims=True)
        d_residual = cot_rows + normalize_back(
            d_second * (1.0 + scale_second), normed_second, inverse_second
        )
        d_branch = (gate_first * d_residual).astype(jnp.bfloat16)
        d_gate_first = jnp.sum(d_residual * branch, axis=1, keepdims=True)
        d_mixed, down_proj, up_proj = adapt_backward(
            mixed, middle_proj, d_branch, down_blocks[2], up_blocks[2]
        )
        d_mixed = (d_mixed + linear_back(d_branch, full_proj)).astype(jnp.bfloat16)
        d_by_heads = lax.all_to_all(d_mixed, "seq", split_axis=2, concat_axis=1, tiled=True)
        dquery_groups, dkey_groups, dvalue_groups = lax.map(
            attend_back, (query_groups, key_groups, value_groups, grouped(d_by_heads), log_total)
        )
        stacked = jnp.stack(
            [
                ungrouped(dquery_groups).astype(jnp.bfloat16),
                ungrouped(dkey_groups).astype(jnp.bfloat16),
                ungrouped(dvalue_groups).astype(jnp.bfloat16),
            ],
            2,
        )[:, :, :, None, :]
        returned = lax.all_to_all(stacked, "seq", split_axis=1, concat_axis=3, tiled=True)
        d_packed = returned.reshape(batch_seqs, local_rows, 3 * MODEL_WIDTH)
        d_hidden, down_qkv, up_qkv = adapt_backward(
            hidden, middle_qkv, d_packed, down_blocks[1], up_blocks[1]
        )
        d_hidden = d_hidden + linear_back(d_packed, full_qkv)
        d_shift_first = jnp.sum(d_hidden, axis=1, keepdims=True)
        d_scale_first = jnp.sum(d_hidden * normed_first, axis=1, keepdims=True)
        token_list.append(
            d_residual + normalize_back(d_hidden * (1.0 + scale_first), normed_first, inverse_first)
        )
        partial_mod = jnp.concatenate(
            [
                d_shift_first,
                d_scale_first,
                d_gate_first,
                d_shift_second,
                d_scale_second,
                d_gate_second,
            ],
            -1,
        )
        d_modulation = lax.psum(partial_mod, "seq").astype(jnp.bfloat16)
        d_cond_act, down_ada, up_ada = adapt_backward(
            cond_act, middle_ada, d_modulation, down_blocks[0], up_blocks[0]
        )
        d_cond_act = d_cond_act + linear_back(d_modulation, full_ada)
        cond_list.append(jax.vjp(jax.nn.silu, cond_rows)[1](d_cond_act[:, 0, :])[0])
        seq_down = jnp.concatenate(
            [down_ada * seq_share, down_qkv, down_proj, down_expand, down_shrink], -1
        )
        seq_up = jnp.concatenate([up_ada * seq_share, up_qkv, up_proj, up_expand, up_shrink], -1)
        selector = jax.nn.one_hot(picked_adapter, ADAPTER_COUNT, dtype=jnp.float32)
        down_gradient = down_gradient + jnp.einsum(
            "sa,src->arc", selector, seq_down, precision=highest
        )
        up_gradient = up_gradient + jnp.einsum("sa,src->arc", selector, seq_up, precision=highest)
    part_down, part_up = (
        lax.psum_scatter(down_gradient, "fsdp", scatter_dimension=2, tiled=True),
        lax.psum_scatter(up_gradient, "fsdp", scatter_dimension=2, tiled=True),
    )
    sequence_down, sequence_up = (
        lax.psum_scatter(
            part_down.astype(jnp.bfloat16), "seq", scatter_dimension=0, tiled=True
        ).astype(jnp.float32),
        lax.psum_scatter(
            part_up.astype(jnp.bfloat16), "seq", scatter_dimension=0, tiled=True
        ).astype(jnp.float32),
    )
    squared = lax.psum(
        jnp.sum(sequence_down * sequence_down) + jnp.sum(sequence_up * sequence_up), ("fsdp", "seq")
    )
    grad_norm = jnp.sqrt(squared)
    clip_factor = jnp.minimum(1.0, clip_limit / (grad_norm + norm_eps))

    def optimizer_update(params, gradient, moment, square):
        gradient = gradient * clip_factor
        moment_new = beta_first * moment + (1.0 - beta_first) * gradient
        square_new = beta_second * square + (1.0 - beta_second) * gradient * gradient
        direction = (
            moment_new
            / (1.0 - beta_first**STEP)
            / (jnp.sqrt(square_new / (1.0 - beta_second**STEP)) + adam_eps)
        )
        return (params - learn_rate * (direction + decay_rate * params), moment_new, square_new)

    stepped_down, next_first_down, next_second_down = optimizer_update(
        lowrank_down, sequence_down, first_moment_down, second_moment_down
    )
    stepped_up, next_first_up, next_second_up = optimizer_update(
        lowrank_up, sequence_up, first_moment_up, second_moment_up
    )
    block_out = jnp.concatenate(output_list, 0)
    token_grad = jnp.concatenate(token_list, 0)
    cond_grad = jnp.concatenate(cond_list, 0)
    return (
        block_out,
        token_grad,
        cond_grad,
        grad_norm,
        stepped_down,
        stepped_up,
        next_first_down,
        next_first_up,
        next_second_down,
        next_second_up,
    )


HEADS = 16
LOG2E = 1.4426950408889634
SCORE_SCALE = HD ** (-0.5)


def tn(left, right):
    return lax.dot_general(left, right, (((0,), (0,)), ((), ())), preferred_element_type=jnp.float32)


def nn(left, right):
    return lax.dot_general(left, right, (((1,), (0,)), ((), ())), preferred_element_type=jnp.float32)


def nt(left, right):
    return lax.dot_general(left, right, (((1,), (1,)), ((), ())), preferred_element_type=jnp.float32)


def heads_kernel(qkv_ref, mixed_ref, log_ref, *, step):
    length = qkv_ref.shape[-1]
    keys = qkv_ref[1, 0].astype(jnp.float32).T.astype(jnp.bfloat16)
    values_t = qkv_ref[2, 0]
    for start in range(0, length, step):
        queries_t = qkv_ref[0, 0, :, start : start + step]
        scores = nn(keys, queries_t) * (SCORE_SCALE * LOG2E)
        top = jnp.max(scores, axis=0, keepdims=True)
        exponent = jnp.exp2(scores - top)
        total = jnp.sum(exponent, axis=0, keepdims=True)
        weights = (exponent * (1.0 / total)).astype(jnp.bfloat16)
        mixed_ref[0, :, start : start + step] = nn(values_t, weights).astype(jnp.bfloat16)
        log_ref[0, :, start : start + step] = top + jnp.log2(total)


def heads_forward(qkv, step=256):
    _, heads, width, length = qkv.shape
    return pl.pallas_call(
        functools.partial(heads_kernel, step=step),
        grid=(heads,),
        in_specs=[pl.BlockSpec((3, 1, width, length), lambda h: (0, h, 0, 0))],
        out_specs=[
            pl.BlockSpec((1, width, length), lambda h: (h, 0, 0)),
            pl.BlockSpec((1, 1, length), lambda h: (h, 0, 0)),
        ],
        out_shape=[
            jax.ShapeDtypeStruct((heads, width, length), jnp.bfloat16),
            jax.ShapeDtypeStruct((heads, 1, length), jnp.float32),
        ],
        cost_estimate=pl.CostEstimate(
            flops=4 * heads * length * length * 256,
            bytes_accessed=10 * heads * width * length,
            transcendentals=heads * length * length,
        ),
        compiler_params=pltpu.CompilerParams(vmem_limit_bytes=48 * 1024 * 1024),
        name="heads_forward",
    )(qkv)


def heads_back_kernel(qkv_ref, grad_ref, log_ref, out_ref, key_acc, value_acc, *, step):
    length = qkv_ref.shape[-1]
    keys_t = qkv_ref[1, 0]
    keys = keys_t.astype(jnp.float32).T.astype(jnp.bfloat16)
    values = qkv_ref[2, 0].astype(jnp.float32).T.astype(jnp.bfloat16)
    for start in range(0, length, step):
        queries_t = qkv_ref[0, 0, :, start : start + step]
        grad_t = grad_ref[0, :, start : start + step]
        queries = queries_t.astype(jnp.float32).T.astype(jnp.bfloat16)
        grad = grad_t.astype(jnp.float32).T.astype(jnp.bfloat16)
        scores = nn(keys, queries_t) * (SCORE_SCALE * LOG2E)
        probable = jnp.exp2(scores - log_ref[0, :, start : start + step])
        d_weights = nn(values, grad_t)
        inner_sum = jnp.sum(d_weights * probable, axis=0, keepdims=True)
        d_scores = (probable * (d_weights - inner_sum)).astype(jnp.bfloat16)
        d_values = nn(probable.astype(jnp.bfloat16), grad)
        d_keys = nn(d_scores, queries)
        if start == 0:
            value_acc[...] = d_values
            key_acc[...] = d_keys
        else:
            value_acc[...] += d_values
            key_acc[...] += d_keys
        out_ref[0, 0, :, start : start + step] = (nn(keys_t, d_scores) * SCORE_SCALE).astype(
            jnp.bfloat16
        )
    out_ref[1, 0] = (key_acc[...] * SCORE_SCALE).T.astype(jnp.bfloat16)
    out_ref[2, 0] = value_acc[...].T.astype(jnp.bfloat16)


def heads_back(qkv, grad, log_total, step=256):
    _, heads, width, length = qkv.shape
    return pl.pallas_call(
        functools.partial(heads_back_kernel, step=step),
        grid=(heads,),
        in_specs=[
            pl.BlockSpec((3, 1, width, length), lambda h: (0, h, 0, 0)),
            pl.BlockSpec((1, width, length), lambda h: (h, 0, 0)),
            pl.BlockSpec((1, 1, length), lambda h: (h, 0, 0)),
        ],
        out_specs=pl.BlockSpec((3, 1, width, length), lambda h: (0, h, 0, 0)),
        out_shape=jax.ShapeDtypeStruct((3, heads, width, length), jnp.bfloat16),
        scratch_shapes=[
            pltpu.VMEM((length, width), jnp.float32),
            pltpu.VMEM((length, width), jnp.float32),
        ],
        cost_estimate=pl.CostEstimate(
            flops=10 * heads * length * length * 256,
            bytes_accessed=16 * heads * width * length,
            transcendentals=heads * length * length,
        ),
        compiler_params=pltpu.CompilerParams(vmem_limit_bytes=48 * 1024 * 1024),
        name="heads_back",
    )(qkv, grad, log_total)


GELU_RATE = 0.7978845608
GELU_CUBE = 0.044715


def feed_kernel(
    second_ref,
    dfinal_ref,
    middle_ref,
    dmiddle_ref,
    widen_ref,
    narrow_ref,
    up_ref,
    down_ref,
    bias_ref,
    final_ref,
    dsecond_ref,
    up_grad_ref,
    down_grad_ref,
    widen_aug,
    narrow_aug,
    *,
    rows,
):
    chunk = pl.program_id(0)
    width = widen_ref.shape[0]
    widen_aug[:width] = widen_ref[...]
    widen_aug[width:] = up_ref[...]
    narrow_aug[:, :width] = narrow_ref[...]
    narrow_aug[:, width:] = down_ref[...]

    @pl.when(chunk == 0)
    def _():
        final_ref[...] = jnp.zeros_like(final_ref)
        dsecond_ref[...] = jnp.zeros_like(dsecond_ref)

    up_grad_ref[...] = jnp.zeros_like(up_grad_ref)
    down_grad_ref[...] = jnp.zeros_like(down_grad_ref)

    def body(index, carry):
        at = pl.ds(pl.multiple_of(index * rows, rows), rows)
        inner = nn(second_ref[at, :], widen_aug[...]) + bias_ref[...]
        square = inner * inner
        tanh = jnp.tanh(GELU_RATE * inner * (1.0 + GELU_CUBE * square))
        half = 0.5 * (1.0 + tanh)
        active = (inner * half).astype(jnp.bfloat16)
        slope = half + inner * (half * (1.0 - tanh)) * (
            GELU_RATE * (1.0 + (3.0 * GELU_CUBE) * square)
        )
        final_ref[at, :] += nn(active, narrow_aug[...])
        d_inner = (nt(dfinal_ref[at, :], narrow_aug[...]) * slope).astype(jnp.bfloat16)
        dsecond_ref[at, :] += nt(d_inner, widen_aug[...])
        up_grad_ref[...] += nn(middle_ref[:, at], d_inner)
        down_grad_ref[...] += nn(dmiddle_ref[:, at], active)
        return carry

    lax.fori_loop(0, second_ref.shape[0] // rows, body, 0)


def feed(second, dfinal, middle, dmiddle, widen, narrow, up, down, bias, chunk=768, rows=256):
    length, padded = second.shape
    width, hidden = widen.shape
    rank = middle.shape[0]
    whole = lambda j: (0, 0)
    columns = lambda j: (0, j)
    return pl.pallas_call(
        functools.partial(feed_kernel, rows=rows),
        grid=(hidden // chunk,),
        in_specs=[
            pl.BlockSpec((length, padded), whole),
            pl.BlockSpec((length, padded), whole),
            pl.BlockSpec((rank, length), whole),
            pl.BlockSpec((rank, length), whole),
            pl.BlockSpec((width, chunk), columns),
            pl.BlockSpec((chunk, width), lambda j: (j, 0)),
            pl.BlockSpec((padded - width, chunk), columns),
            pl.BlockSpec((chunk, padded - width), lambda j: (j, 0)),
            pl.BlockSpec((1, chunk), columns),
        ],
        out_specs=[
            pl.BlockSpec((length, padded), whole),
            pl.BlockSpec((length, padded), whole),
            pl.BlockSpec((rank, chunk), columns),
            pl.BlockSpec((rank, chunk), columns),
        ],
        out_shape=[
            jax.ShapeDtypeStruct((length, padded), jnp.float32),
            jax.ShapeDtypeStruct((length, padded), jnp.float32),
            jax.ShapeDtypeStruct((rank, hidden), jnp.float32),
            jax.ShapeDtypeStruct((rank, hidden), jnp.float32),
        ],
        scratch_shapes=[
            pltpu.VMEM((padded, chunk), jnp.bfloat16),
            pltpu.VMEM((chunk, padded), jnp.bfloat16),
        ],
        cost_estimate=pl.CostEstimate(
            flops=8 * length * padded * hidden,
            bytes_accessed=4 * width * hidden + 12 * length * padded,
            transcendentals=length * hidden,
        ),
        compiler_params=pltpu.CompilerParams(vmem_limit_bytes=60 * 1024 * 1024),
        name="feed",
    )(second, dfinal, middle, dmiddle, widen, narrow, up, down, bias)


RANK = ADAPTER_RANK
DOWN_EDGES = (0, 1152, 2304, 3456, 4608, 9216)
UP_EDGES = (0, 6912, 10368, 11520, 16128, 17280)
PADDED = MODEL_WIDTH + 128


def fits(mesh):
    return mesh.shape["seq"] == MB and mesh.shape["fsdp"] == 16


def dot(equation, left, right):
    return jnp.einsum(equation, left, right, preferred_element_type=jnp.float32)


def swap(block):
    return lax.ppermute(block, "seq", [(0, 1), (1, 0)])


def join(own, other, mine, axis):
    first = mine == 0
    return jnp.concatenate(
        [jnp.where(first, own, other), jnp.where(first, other, own)], axis
    )


def fast_shards(
    tokens,
    condition,
    adapter,
    cotangent,
    modulation_weight,
    modulation_bias,
    query_key_value_weight,
    attention_out_weight,
    attention_out_bias,
    widen_weight,
    widen_bias,
    narrow_weight,
    narrow_bias,
    lowrank_down,
    lowrank_up,
    first_moment_down,
    first_moment_up,
    second_moment_down,
    second_moment_up,
):
    bf16 = jnp.bfloat16
    n_fsdp = lax.axis_size("fsdp")
    mine = lax.axis_index("seq")
    row = lax.axis_index("fsdp")

    def gather(weight):
        return lax.all_gather(
            join(weight, swap(weight), mine, 1), "fsdp", axis=0, tiled=True
        )

    full_qkv = gather(query_key_value_weight)
    full_proj = gather(attention_out_weight)
    full_widen = gather(widen_weight)
    full_narrow = gather(narrow_weight)

    token_rows = lax.all_to_all(tokens, "seq", split_axis=0, concat_axis=1, tiled=True)[0]
    cot_rows = lax.all_to_all(cotangent, "seq", split_axis=0, concat_axis=1, tiled=True)[0]
    token_rows = token_rows.astype(jnp.float32)
    cot_rows = cot_rows.astype(jnp.float32)

    every_adapter = lax.all_gather(adapter, "fsdp", axis=0, tiled=True)
    own_ids = lax.dynamic_index_in_dim(every_adapter.reshape(n_fsdp, MB), mine, 1, False)
    portions = jnp.concatenate([lowrank_down.astype(bf16), lowrank_up.astype(bf16)], -1)
    table = join(portions, swap(portions), mine, 0)
    picks = jax.nn.one_hot(own_ids, ADAPTER_COUNT, dtype=bf16)
    chosen = dot("fa,arc->frc", picks, table).astype(bf16)
    chosen = lax.all_to_all(chosen, "fsdp", split_axis=0, concat_axis=0, tiled=True)
    down_chunk = lowrank_down.shape[-1]
    up_chunk = lowrank_up.shape[-1]
    down_all = jnp.moveaxis(chosen[:, :, :down_chunk], 0, 1).reshape(RANK, -1)
    up_all = jnp.moveaxis(chosen[:, :, down_chunk:], 0, 1).reshape(RANK, -1)
    downs = [down_all[:, DOWN_EDGES[i] : DOWN_EDGES[i + 1]] for i in range(5)]
    ups = [up_all[:, UP_EDGES[i] : UP_EDGES[i + 1]] for i in range(5)]

    cond_act_pair = jax.nn.silu(condition).astype(bf16)
    every_cond = lax.all_gather(cond_act_pair, "fsdp", axis=0, tiled=True)
    depth = modulation_weight.shape[0]
    cond_slice = lax.dynamic_slice_in_dim(every_cond, row * depth, depth, 1)
    part = dot("si,io->so", cond_slice, modulation_weight)
    part = part.reshape(n_fsdp, MB, -1)
    part = lax.all_to_all(part, "fsdp", split_axis=0, concat_axis=0, tiled=True)
    pair_half = jnp.sum(part, axis=0)
    mod_base = lax.all_to_all(pair_half, "seq", split_axis=0, concat_axis=1, tiled=True)
    cond_act = lax.dynamic_slice_in_dim(cond_act_pair, mine, 1, 0)
    middle_ada = dot("ti,ri->tr", cond_act, downs[0]).astype(bf16)
    modulation = mod_base + modulation_bias + dot("tr,ro->to", middle_ada, ups[0])
    shift_first, scale_first, gate_first, shift_second, scale_second, gate_second = jnp.split(
        modulation, 6, axis=-1
    )

    length = token_rows.shape[0]
    normed_first, inverse_first = normalize(token_rows)
    hidden = (normed_first * (1.0 + scale_first) + shift_first).astype(bf16)
    middle_qkv = dot("ti,ri->tr", hidden, downs[1]).astype(bf16)
    packed = dot(
        "ti,io->ot",
        jnp.concatenate([hidden, middle_qkv], 1),
        jnp.concatenate([full_qkv, ups[1]], 0),
    ).astype(bf16)
    qkv = packed.reshape(3, HEADS, HD, length)
    mixed_heads, log_total = heads_forward(qkv, step=1024)
    mixed = mixed_heads.reshape(MODEL_WIDTH, length)

    middle_proj = dot("it,ri->tr", mixed, downs[2]).astype(bf16)
    branch = (
        dot("it,io->to", mixed, full_proj)
        + attention_out_bias
        + dot("tr,ro->to", middle_proj, ups[2])
    )
    residual = token_rows + gate_first * branch
    normed_second, inverse_second = normalize(residual)
    second = (normed_second * (1.0 + scale_second) + shift_second).astype(bf16)
    middle_expand = dot("ti,ri->tr", second, downs[3]).astype(bf16)
    d_final = (gate_second * cot_rows).astype(bf16)
    dmiddle_shrink = dot("to,ro->tr", d_final, ups[4]).astype(bf16)

    fill = jnp.zeros((length, 128 - RANK), bf16)
    final_ext, dsecond_ext, up_expand, down_shrink = feed(
        jnp.concatenate([second, middle_expand, fill], 1),
        jnp.concatenate([d_final, dmiddle_shrink, fill], 1),
        middle_expand.T,
        dmiddle_shrink.T,
        full_widen,
        full_narrow,
        jnp.pad(ups[3], ((0, 128 - RANK), (0, 0))),
        jnp.pad(downs[4].T, ((0, 0), (0, 128 - RANK))),
        widen_bias[None],
        chunk=512,
        rows=1024,
    )
    middle_shrink = final_ext[:, MODEL_WIDTH : MODEL_WIDTH + RANK].astype(bf16)
    final_out = (
        final_ext[:, :MODEL_WIDTH] + narrow_bias + dot("tr,ro->to", middle_shrink, ups[4])
    )
    block_rows = (residual + gate_second * final_out).astype(bf16)
    block_out = lax.all_to_all(block_rows[None], "seq", split_axis=1, concat_axis=0, tiled=True)
    d_gate_second = jnp.sum(cot_rows * final_out, axis=0, keepdims=True)
    up_shrink = dot("tr,to->ro", middle_shrink, d_final)
    dmiddle_expand = dsecond_ext[:, MODEL_WIDTH : MODEL_WIDTH + RANK].astype(bf16)
    down_expand = dot("tr,ti->ri", dmiddle_expand, second)
    d_second = dsecond_ext[:, :MODEL_WIDTH] + dot("tr,ri->ti", dmiddle_expand, downs[3])
    d_shift_second = jnp.sum(d_second, axis=0, keepdims=True)
    d_scale_second = jnp.sum(d_second * normed_second, axis=0, keepdims=True)
    d_residual = cot_rows + normalize_back(
        d_second * (1.0 + scale_second), normed_second, inverse_second
    )
    d_branch = (gate_first * d_residual).astype(bf16)
    d_gate_first = jnp.sum(d_residual * branch, axis=0, keepdims=True)
    up_proj = dot("tr,to->ro", middle_proj, d_branch)
    dmiddle_proj = dot("to,ro->tr", d_branch, ups[2]).astype(bf16)
    down_proj = dot("tr,it->ri", dmiddle_proj, mixed)
    d_mixed = (
        dot("to,io->it", d_branch, full_proj) + dot("tr,ri->it", dmiddle_proj, downs[2])
    ).astype(bf16)

    d_qkv = heads_back(qkv, d_mixed.reshape(HEADS, HD, length), log_total, step=512)
    d_packed = d_qkv.reshape(3 * MODEL_WIDTH, length)
    up_qkv = dot("tr,ot->ro", middle_qkv, d_packed)
    dmiddle_qkv = dot("ot,ro->tr", d_packed, ups[1]).astype(bf16)
    down_qkv = dot("tr,ti->ri", dmiddle_qkv, hidden)
    d_hidden = dot("ot,io->ti", d_packed, full_qkv) + dot("tr,ri->ti", dmiddle_qkv, downs[1])
    d_shift_first = jnp.sum(d_hidden, axis=0, keepdims=True)
    d_scale_first = jnp.sum(d_hidden * normed_first, axis=0, keepdims=True)
    token_back = d_residual + normalize_back(
        d_hidden * (1.0 + scale_first), normed_first, inverse_first
    )
    token_grad = lax.all_to_all(
        token_back.astype(bf16)[None], "seq", split_axis=1, concat_axis=0, tiled=True
    ).astype(jnp.float32)

    d_modulation = jnp.concatenate(
        [
            d_shift_first,
            d_scale_first,
            d_gate_first,
            d_shift_second,
            d_scale_second,
            d_gate_second,
        ],
        -1,
    ).astype(bf16)
    up_ada = dot("tr,to->ro", middle_ada, d_modulation)
    dmiddle_ada = dot("to,ro->tr", d_modulation, ups[0]).astype(bf16)
    down_ada = dot("tr,ti->ri", dmiddle_ada, cond_act)
    own_cond = dot("tr,ri->ti", dmiddle_ada, downs[0])
    mod_half = lax.all_to_all(d_modulation, "seq", split_axis=1, concat_axis=0, tiled=True)
    every_mod = lax.all_gather(mod_half, "fsdp", axis=0, tiled=True)
    cond_part = dot("so,io->si", every_mod, modulation_weight).reshape(n_fsdp, MB, -1)
    cond_part = lax.all_to_all(cond_part, "fsdp", split_axis=0, concat_axis=0, tiled=True)
    d_cond = jnp.moveaxis(cond_part, 0, 1).reshape(MB, MODEL_WIDTH)
    d_cond = d_cond + jnp.where(jnp.arange(MB)[:, None] == mine, own_cond, 0.0)
    d_cond = d_cond + swap(d_cond)
    cond_grad = jax.vjp(jax.nn.silu, condition)[1](d_cond)[0]

    seq_down = jnp.concatenate([down_ada, down_qkv, down_proj, down_expand, down_shrink], -1)
    seq_up = jnp.concatenate([up_ada, up_qkv, up_proj, up_expand, up_shrink], -1)
    sent = jnp.concatenate(
        [seq_down.reshape(RANK, n_fsdp, down_chunk), seq_up.reshape(RANK, n_fsdp, up_chunk)], -1
    )
    sent = jnp.moveaxis(sent, 1, 0).astype(bf16)
    came = lax.all_to_all(sent, "fsdp", split_axis=0, concat_axis=0, tiled=True)
    summed = dot("fa,frc->arc", picks, came)
    held = lowrank_down.shape[0]
    kept = lax.dynamic_slice_in_dim(summed, mine * held, held, 0)
    given = lax.dynamic_slice_in_dim(summed, (1 - mine) * held, held, 0)
    gradient = kept + swap(given.astype(bf16)).astype(jnp.float32)
    sequence_down = gradient[:, :, :down_chunk]
    sequence_up = gradient[:, :, down_chunk:]

    squared = jnp.broadcast_to(jnp.sum(gradient * gradient), (n_fsdp * MB, 128))
    squared = lax.all_to_all(squared, ("fsdp", "seq"), split_axis=0, concat_axis=0, tiled=True)
    grad_norm = jnp.sqrt(jnp.sum(squared[:, 0]))
    clip_factor = jnp.minimum(1.0, clip_limit / (grad_norm + norm_eps))

    def optimizer_update(params, gradient, moment, square):
        gradient = gradient * clip_factor
        moment_new = beta_first * moment + (1.0 - beta_first) * gradient
        square_new = beta_second * square + (1.0 - beta_second) * gradient * gradient
        direction = (
            moment_new
            / (1.0 - beta_first**STEP)
            / (jnp.sqrt(square_new / (1.0 - beta_second**STEP)) + adam_eps)
        )
        return (params - learn_rate * (direction + decay_rate * params), moment_new, square_new)

    stepped_down, next_first_down, next_second_down = optimizer_update(
        lowrank_down, sequence_down, first_moment_down, second_moment_down
    )
    stepped_up, next_first_up, next_second_up = optimizer_update(
        lowrank_up, sequence_up, first_moment_up, second_moment_up
    )
    return (
        block_out,
        token_grad,
        cond_grad,
        grad_norm,
        stepped_down,
        stepped_up,
        next_first_down,
        next_first_up,
        next_second_down,
        next_second_up,
    )


def solution(mesh):
    in_specs = (
        P("fsdp", "seq", None),
        P("fsdp", None),
        P("fsdp"),
        P("fsdp", "seq", None),
        P("fsdp", "seq"),
        P(),
        P("fsdp", "seq"),
        P("fsdp", "seq"),
        P(),
        P("fsdp", "seq"),
        P(),
        P("fsdp", "seq"),
        P(),
        P("seq", None, "fsdp"),
        P("seq", None, "fsdp"),
        P("seq", None, "fsdp"),
        P("seq", None, "fsdp"),
        P("seq", None, "fsdp"),
        P("seq", None, "fsdp"),
    )
    out_specs = (
        P("fsdp", "seq", None),
        P("fsdp", "seq", None),
        P("fsdp", None),
        P(),
        P("seq", None, "fsdp"),
        P("seq", None, "fsdp"),
        P("seq", None, "fsdp"),
        P("seq", None, "fsdp"),
        P("seq", None, "fsdp"),
        P("seq", None, "fsdp"),
    )
    body = fast_shards if fits(mesh) else shards
    return jax.shard_map(body, mesh=mesh, in_specs=in_specs, out_specs=out_specs, check_vma=False)
```

```python
import functools

import jax
import jax.numpy as jnp
from jax import lax
from jax.experimental import pallas as pl
from jax.experimental.pallas import tpu as pltpu
from jax.sharding import PartitionSpec as P

MODEL_WIDTH = 1152
HD = 72
FF = 4608
ADAPTER_RANK = 16
ADAPTER_COUNT = 8
MB = 2
SEQ_MB = 1
STEP = 10


beta_first = 0.9
beta_second = 0.999
learn_rate = 0.05
decay_rate = 0.1
adam_eps = 1e-08
clip_limit = 1.0
norm_eps = 1e-06
pair_heads = 2
highest = lax.Precision.HIGHEST


def linear(inputs, weight):
    return jnp.einsum("sti,io->sto", inputs, weight, preferred_element_type=jnp.float32)


def linear_back(gradient, weight):
    return jnp.einsum("sto,io->sti", gradient, weight, preferred_element_type=jnp.float32)


def normalize(stream):
    center = stream - jnp.mean(stream, -1, keepdims=True)
    inverse = lax.rsqrt(jnp.mean(center * center, -1, keepdims=True) + norm_eps)
    return (center * inverse, inverse)


def normalize_back(gradient, normed, inverse):
    return inverse * (
        gradient
        - jnp.mean(gradient, -1, keepdims=True)
        - normed * jnp.mean(gradient * normed, -1, keepdims=True)
    )


def adapt_forward(inputs, down_part, up_part):
    middle = jnp.einsum(
        "sti,sri->str", inputs, down_part, preferred_element_type=jnp.float32
    ).astype(jnp.bfloat16)
    return (middle, jnp.einsum("str,sro->sto", middle, up_part, preferred_element_type=jnp.float32))


def adapt_backward(inputs, middle, gradient, down_part, up_part):
    up_grad = jnp.einsum("str,sto->sro", middle, gradient, preferred_element_type=jnp.float32)
    middle_grad = jnp.einsum(
        "sto,sro->str", gradient, up_part, preferred_element_type=jnp.float32
    ).astype(jnp.bfloat16)
    down_grad = jnp.einsum("str,sti->sri", middle_grad, inputs, preferred_element_type=jnp.float32)
    input_grad = jnp.einsum(
        "str,sri->sti", middle_grad, down_part, preferred_element_type=jnp.float32
    )
    return (input_grad, down_grad, up_grad)


def grouped(matrix):
    seq_count, row_count, col_count = matrix.shape
    return jnp.moveaxis(
        matrix.reshape(seq_count, row_count, col_count // (pair_heads * HD), pair_heads, HD), 2, 0
    )


def ungrouped(stacked):
    moved = jnp.moveaxis(stacked, 0, 2)
    return moved.reshape(moved.shape[0], moved.shape[1], -1)


def attend_group(group_inputs):
    queries, all_keys, all_values = group_inputs
    factor = queries.shape[-1] ** (-0.5)
    scores = (
        jnp.einsum("sqhd,skhd->shqk", queries, all_keys, preferred_element_type=jnp.float32)
        * factor
    )
    row_max = jnp.max(scores, -1, keepdims=True)
    exponent = jnp.exp(scores - row_max)
    row_total = jnp.sum(exponent, -1, keepdims=True)
    weights = (exponent / row_total).astype(jnp.bfloat16)
    mixed_heads = jnp.einsum(
        "shqk,skhd->sqhd", weights, all_values, preferred_element_type=jnp.float32
    )
    return (mixed_heads, row_max + jnp.log(row_total))


def attend_back(group_inputs):
    queries, all_keys, all_values, d_mixed, log_total = group_inputs
    factor = queries.shape[-1] ** (-0.5)
    scores = (
        jnp.einsum("sqhd,skhd->shqk", queries, all_keys, preferred_element_type=jnp.float32)
        * factor
    )
    probable = jnp.exp(scores - log_total)
    d_values = jnp.einsum(
        "shqk,sqhd->skhd",
        probable.astype(jnp.bfloat16),
        d_mixed,
        preferred_element_type=jnp.float32,
    )
    d_weights = jnp.einsum(
        "sqhd,skhd->shqk", d_mixed, all_values, preferred_element_type=jnp.float32
    )
    inner_sum = jnp.sum(d_weights * probable, -1, keepdims=True)
    d_scores = (probable * (d_weights - inner_sum) * factor).astype(jnp.bfloat16)
    d_queries = jnp.einsum(
        "shqk,skhd->sqhd", d_scores, all_keys, preferred_element_type=jnp.float32
    )
    d_keys = jnp.einsum("shqk,sqhd->skhd", d_scores, queries, preferred_element_type=jnp.float32)
    return (d_queries, d_keys, d_values)


def gelu_tanh(inner_act):
    return jax.nn.gelu(inner_act, approximate=True)


def shards(
    tokens,
    condition,
    adapter,
    cotangent,
    modulation_weight,
    modulation_bias,
    query_key_value_weight,
    attention_out_weight,
    attention_out_bias,
    widen_weight,
    widen_bias,
    narrow_weight,
    narrow_bias,
    lowrank_down,
    lowrank_up,
    first_moment_down,
    first_moment_up,
    second_moment_down,
    second_moment_up,
):
    seq_count_axis = lax.axis_size("seq")
    seq_share = 1.0 / seq_count_axis
    down_portion = lowrank_down.astype(jnp.bfloat16)
    up_portion = lowrank_up.astype(jnp.bfloat16)
    down_edges = (
        0,
        MODEL_WIDTH,
        2 * MODEL_WIDTH,
        3 * MODEL_WIDTH,
        4 * MODEL_WIDTH,
        4 * MODEL_WIDTH + FF,
    )
    up_edges = (
        0,
        6 * MODEL_WIDTH,
        9 * MODEL_WIDTH,
        10 * MODEL_WIDTH,
        10 * MODEL_WIDTH + FF,
        11 * MODEL_WIDTH + FF,
    )

    def fetch():
        across = (
            lax.all_gather(modulation_weight, "seq", axis=1, tiled=True),
            lax.all_gather(query_key_value_weight, "seq", axis=1, tiled=True),
            lax.all_gather(attention_out_weight, "seq", axis=1, tiled=True),
            lax.all_gather(widen_weight, "seq", axis=1, tiled=True),
            lax.all_gather(narrow_weight, "seq", axis=1, tiled=True),
            lax.all_gather(down_portion, "seq", axis=0, tiled=True),
            lax.all_gather(up_portion, "seq", axis=0, tiled=True),
        )
        return (
            lax.all_gather(across[0], "fsdp", axis=0, tiled=True),
            lax.all_gather(across[1], "fsdp", axis=0, tiled=True),
            lax.all_gather(across[2], "fsdp", axis=0, tiled=True),
            lax.all_gather(across[3], "fsdp", axis=0, tiled=True),
            lax.all_gather(across[4], "fsdp", axis=0, tiled=True),
            lax.all_gather(across[5], "fsdp", axis=2, tiled=True),
            lax.all_gather(across[6], "fsdp", axis=2, tiled=True),
        )

    def select(gathered_now, picked_adapter):
        down_sel = gathered_now[5][picked_adapter]
        up_sel = gathered_now[6][picked_adapter]
        down_blocks = [
            down_sel[:, :, down_edges[target] : down_edges[target + 1]] for target in range(5)
        ]
        up_blocks = [up_sel[:, :, up_edges[target] : up_edges[target + 1]] for target in range(5)]
        return (
            gathered_now[0],
            gathered_now[1],
            gathered_now[2],
            gathered_now[3],
            gathered_now[4],
            down_blocks,
            up_blocks,
        )

    down_gradient = jnp.zeros((ADAPTER_COUNT, ADAPTER_RANK, down_edges[5]), jnp.float32)
    up_gradient = jnp.zeros((ADAPTER_COUNT, ADAPTER_RANK, up_edges[5]), jnp.float32)
    output_list, token_list, cond_list = ([], [], [])
    for micro_batch in range(MB):
        first_seq = micro_batch * SEQ_MB
        token_rows = tokens[first_seq : first_seq + SEQ_MB].astype(jnp.float32)
        cond_rows = condition[first_seq : first_seq + SEQ_MB]
        picked_adapter = adapter[first_seq : first_seq + SEQ_MB]
        cot_rows = cotangent[first_seq : first_seq + SEQ_MB].astype(jnp.float32)
        batch_seqs = token_rows.shape[0]
        local_rows = token_rows.shape[1]
        gathered = fetch()
        full_ada, full_qkv, full_proj, full_expand, full_shrink, down_blocks, up_blocks = select(
            gathered, picked_adapter
        )
        cond_act = jax.nn.silu(cond_rows).astype(jnp.bfloat16)[:, None, :]
        middle_ada, extra_ada = adapt_forward(cond_act, down_blocks[0], up_blocks[0])
        modulation = linear(cond_act, full_ada) + modulation_bias + extra_ada
        shift_first, scale_first, gate_first, shift_second, scale_second, gate_second = jnp.split(
            modulation, 6, axis=-1
        )
        normed_first, inverse_first = normalize(token_rows)
        hidden = (normed_first * (1.0 + scale_first) + shift_first).astype(jnp.bfloat16)
        middle_qkv, extra_qkv = adapt_forward(hidden, down_blocks[1], up_blocks[1])
        packed = (linear(hidden, full_qkv) + extra_qkv).astype(jnp.bfloat16)
        head_blocks = packed.reshape(
            batch_seqs, local_rows, 3, seq_count_axis, MODEL_WIDTH // seq_count_axis
        )
        by_heads = lax.all_to_all(head_blocks, "seq", split_axis=3, concat_axis=1, tiled=True)
        query_groups = grouped(by_heads[:, :, 0, 0])
        key_groups = grouped(by_heads[:, :, 1, 0])
        value_groups = grouped(by_heads[:, :, 2, 0])
        mixed_groups, log_total = lax.map(attend_group, (query_groups, key_groups, value_groups))
        mixed = lax.all_to_all(
            ungrouped(mixed_groups).astype(jnp.bfloat16),
            "seq",
            split_axis=1,
            concat_axis=2,
            tiled=True,
        )
        middle_proj, extra_proj = adapt_forward(mixed, down_blocks[2], up_blocks[2])
        branch = linear(mixed, full_proj) + attention_out_bias + extra_proj
        residual = token_rows + gate_first * branch
        normed_second, inverse_second = normalize(residual)
        second = (normed_second * (1.0 + scale_second) + shift_second).astype(jnp.bfloat16)
        middle_expand, extra_expand = adapt_forward(second, down_blocks[3], up_blocks[3])
        inner_act = linear(second, full_expand) + widen_bias + extra_expand
        active = gelu_tanh(inner_act).astype(jnp.bfloat16)
        middle_shrink, extra_shrink = adapt_forward(active, down_blocks[4], up_blocks[4])
        final_out = linear(active, full_shrink) + narrow_bias + extra_shrink
        output_list.append((residual + gate_second * final_out).astype(jnp.bfloat16))
        gathered = fetch()
        full_ada, full_qkv, full_proj, full_expand, full_shrink, down_blocks, up_blocks = select(
            gathered, picked_adapter
        )
        d_final = (gate_second * cot_rows).astype(jnp.bfloat16)
        d_gate_second = jnp.sum(cot_rows * final_out, axis=1, keepdims=True)
        d_active, down_shrink, up_shrink = adapt_backward(
            active, middle_shrink, d_final, down_blocks[4], up_blocks[4]
        )
        d_active = d_active + linear_back(d_final, full_shrink)
        d_inner = jax.vjp(gelu_tanh, inner_act)[1](d_active)[0].astype(jnp.bfloat16)
        d_second, down_expand, up_expand = adapt_backward(
            second, middle_expand, d_inner, down_blocks[3], up_blocks[3]
        )
        d_second = d_second + linear_back(d_inner, full_expand)
        d_shift_second = jnp.sum(d_second, axis=1, keepdims=True)
        d_scale_second = jnp.sum(d_second * normed_second, axis=1, keepdims=True)
        d_residual = cot_rows + normalize_back(
            d_second * (1.0 + scale_second), normed_second, inverse_second
        )
        d_branch = (gate_first * d_residual).astype(jnp.bfloat16)
        d_gate_first = jnp.sum(d_residual * branch, axis=1, keepdims=True)
        d_mixed, down_proj, up_proj = adapt_backward(
            mixed, middle_proj, d_branch, down_blocks[2], up_blocks[2]
        )
        d_mixed = (d_mixed + linear_back(d_branch, full_proj)).astype(jnp.bfloat16)
        d_by_heads = lax.all_to_all(d_mixed, "seq", split_axis=2, concat_axis=1, tiled=True)
        dquery_groups, dkey_groups, dvalue_groups = lax.map(
            attend_back, (query_groups, key_groups, value_groups, grouped(d_by_heads), log_total)
        )
        stacked = jnp.stack(
            [
                ungrouped(dquery_groups).astype(jnp.bfloat16),
                ungrouped(dkey_groups).astype(jnp.bfloat16),
                ungrouped(dvalue_groups).astype(jnp.bfloat16),
            ],
            2,
        )[:, :, :, None, :]
        returned = lax.all_to_all(stacked, "seq", split_axis=1, concat_axis=3, tiled=True)
        d_packed = returned.reshape(batch_seqs, local_rows, 3 * MODEL_WIDTH)
        d_hidden, down_qkv, up_qkv = adapt_backward(
            hidden, middle_qkv, d_packed, down_blocks[1], up_blocks[1]
        )
        d_hidden = d_hidden + linear_back(d_packed, full_qkv)
        d_shift_first = jnp.sum(d_hidden, axis=1, keepdims=True)
        d_scale_first = jnp.sum(d_hidden * normed_first, axis=1, keepdims=True)
        token_list.append(
            d_residual + normalize_back(d_hidden * (1.0 + scale_first), normed_first, inverse_first)
        )
        partial_mod = jnp.concatenate(
            [
                d_shift_first,
                d_scale_first,
                d_gate_first,
                d_shift_second,
                d_scale_second,
                d_gate_second,
            ],
            -1,
        )
        d_modulation = lax.psum(partial_mod, "seq").astype(jnp.bfloat16)
        d_cond_act, down_ada, up_ada = adapt_backward(
            cond_act, middle_ada, d_modulation, down_blocks[0], up_blocks[0]
        )
        d_cond_act = d_cond_act + linear_back(d_modulation, full_ada)
        cond_list.append(jax.vjp(jax.nn.silu, cond_rows)[1](d_cond_act[:, 0, :])[0])
        seq_down = jnp.concatenate(
            [down_ada * seq_share, down_qkv, down_proj, down_expand, down_shrink], -1
        )
        seq_up = jnp.concatenate([up_ada * seq_share, up_qkv, up_proj, up_expand, up_shrink], -1)
        selector = jax.nn.one_hot(picked_adapter, ADAPTER_COUNT, dtype=jnp.float32)
        down_gradient = down_gradient + jnp.einsum(
            "sa,src->arc", selector, seq_down, precision=highest
        )
        up_gradient = up_gradient + jnp.einsum("sa,src->arc", selector, seq_up, precision=highest)
    part_down, part_up = (
        lax.psum_scatter(down_gradient, "fsdp", scatter_dimension=2, tiled=True),
        lax.psum_scatter(up_gradient, "fsdp", scatter_dimension=2, tiled=True),
    )
    sequence_down, sequence_up = (
        lax.psum_scatter(
            part_down.astype(jnp.bfloat16), "seq", scatter_dimension=0, tiled=True
        ).astype(jnp.float32),
        lax.psum_scatter(
            part_up.astype(jnp.bfloat16), "seq", scatter_dimension=0, tiled=True
        ).astype(jnp.float32),
    )
    squared = lax.psum(
        jnp.sum(sequence_down * sequence_down) + jnp.sum(sequence_up * sequence_up), ("fsdp", "seq")
    )
    grad_norm = jnp.sqrt(squared)
    clip_factor = jnp.minimum(1.0, clip_limit / (grad_norm + norm_eps))

    def optimizer_update(params, gradient, moment, square):
        gradient = gradient * clip_factor
        moment_new = beta_first * moment + (1.0 - beta_first) * gradient
        square_new = beta_second * square + (1.0 - beta_second) * gradient * gradient
        direction = (
            moment_new
            / (1.0 - beta_first**STEP)
            / (jnp.sqrt(square_new / (1.0 - beta_second**STEP)) + adam_eps)
        )
        return (params - learn_rate * (direction + decay_rate * params), moment_new, square_new)

    stepped_down, next_first_down, next_second_down = optimizer_update(
        lowrank_down, sequence_down, first_moment_down, second_moment_down
    )
    stepped_up, next_first_up, next_second_up = optimizer_update(
        lowrank_up, sequence_up, first_moment_up, second_moment_up
    )
    block_out = jnp.concatenate(output_list, 0)
    token_grad = jnp.concatenate(token_list, 0)
    cond_grad = jnp.concatenate(cond_list, 0)
    return (
        block_out,
        token_grad,
        cond_grad,
        grad_norm,
        stepped_down,
        stepped_up,
        next_first_down,
        next_first_up,
        next_second_down,
        next_second_up,
    )


HEADS = 16
LOG2E = 1.4426950408889634
SCORE_SCALE = HD ** (-0.5)


def tn(left, right):
    return lax.dot_general(left, right, (((0,), (0,)), ((), ())), preferred_element_type=jnp.float32)


def nn(left, right):
    return lax.dot_general(left, right, (((1,), (0,)), ((), ())), preferred_element_type=jnp.float32)


def nt(left, right):
    return lax.dot_general(left, right, (((1,), (1,)), ((), ())), preferred_element_type=jnp.float32)


def heads_kernel(qkv_ref, mixed_ref, log_ref, *, step):
    length = qkv_ref.shape[-1]
    keys = qkv_ref[1, 0].astype(jnp.float32).T.astype(jnp.bfloat16)
    values_t = qkv_ref[2, 0]
    for start in range(0, length, step):
        queries_t = qkv_ref[0, 0, :, start : start + step]
        scores = nn(keys, queries_t) * (SCORE_SCALE * LOG2E)
        top = jnp.max(scores, axis=0, keepdims=True)
        exponent = jnp.exp2(scores - top)
        total = jnp.sum(exponent, axis=0, keepdims=True)
        weights = (exponent * (1.0 / total)).astype(jnp.bfloat16)
        mixed_ref[0, :, start : start + step] = nn(values_t, weights).astype(jnp.bfloat16)
        log_ref[0, :, start : start + step] = top + jnp.log2(total)


def heads_forward(qkv, step=256):
    _, heads, width, length = qkv.shape
    return pl.pallas_call(
        functools.partial(heads_kernel, step=step),
        grid=(heads,),
        in_specs=[pl.BlockSpec((3, 1, width, length), lambda h: (0, h, 0, 0))],
        out_specs=[
            pl.BlockSpec((1, width, length), lambda h: (h, 0, 0)),
            pl.BlockSpec((1, 1, length), lambda h: (h, 0, 0)),
        ],
        out_shape=[
            jax.ShapeDtypeStruct((heads, width, length), jnp.bfloat16),
            jax.ShapeDtypeStruct((heads, 1, length), jnp.float32),
        ],
        cost_estimate=pl.CostEstimate(
            flops=4 * heads * length * length * 256,
            bytes_accessed=10 * heads * width * length,
            transcendentals=heads * length * length,
        ),
        compiler_params=pltpu.CompilerParams(vmem_limit_bytes=48 * 1024 * 1024),
        name="heads_forward",
    )(qkv)


def heads_back_kernel(qkv_ref, grad_ref, log_ref, out_ref, key_acc, value_acc, *, step):
    length = qkv_ref.shape[-1]
    keys_t = qkv_ref[1, 0]
    keys = keys_t.astype(jnp.float32).T.astype(jnp.bfloat16)
    values = qkv_ref[2, 0].astype(jnp.float32).T.astype(jnp.bfloat16)
    for start in range(0, length, step):
        queries_t = qkv_ref[0, 0, :, start : start + step]
        grad_t = grad_ref[0, :, start : start + step]
        queries = queries_t.astype(jnp.float32).T.astype(jnp.bfloat16)
        grad = grad_t.astype(jnp.float32).T.astype(jnp.bfloat16)
        scores = nn(keys, queries_t) * (SCORE_SCALE * LOG2E)
        probable = jnp.exp2(scores - log_ref[0, :, start : start + step])
        d_weights = nn(values, grad_t)
        inner_sum = jnp.sum(d_weights * probable, axis=0, keepdims=True)
        d_scores = (probable * (d_weights - inner_sum)).astype(jnp.bfloat16)
        d_values = nn(probable.astype(jnp.bfloat16), grad)
        d_keys = nn(d_scores, queries)
        if start == 0:
            value_acc[...] = d_values
            key_acc[...] = d_keys
        else:
            value_acc[...] += d_values
            key_acc[...] += d_keys
        out_ref[0, 0, :, start : start + step] = (nn(keys_t, d_scores) * SCORE_SCALE).astype(
            jnp.bfloat16
        )
    out_ref[1, 0] = (key_acc[...] * SCORE_SCALE).T.astype(jnp.bfloat16)
    out_ref[2, 0] = value_acc[...].T.astype(jnp.bfloat16)


def heads_back(qkv, grad, log_total, step=256):
    _, heads, width, length = qkv.shape
    return pl.pallas_call(
        functools.partial(heads_back_kernel, step=step),
        grid=(heads,),
        in_specs=[
            pl.BlockSpec((3, 1, width, length), lambda h: (0, h, 0, 0)),
            pl.BlockSpec((1, width, length), lambda h: (h, 0, 0)),
            pl.BlockSpec((1, 1, length), lambda h: (h, 0, 0)),
        ],
        out_specs=pl.BlockSpec((3, 1, width, length), lambda h: (0, h, 0, 0)),
        out_shape=jax.ShapeDtypeStruct((3, heads, width, length), jnp.bfloat16),
        scratch_shapes=[
            pltpu.VMEM((length, width), jnp.float32),
            pltpu.VMEM((length, width), jnp.float32),
        ],
        cost_estimate=pl.CostEstimate(
            flops=10 * heads * length * length * 256,
            bytes_accessed=16 * heads * width * length,
            transcendentals=heads * length * length,
        ),
        compiler_params=pltpu.CompilerParams(vmem_limit_bytes=48 * 1024 * 1024),
        name="heads_back",
    )(qkv, grad, log_total)


RANK = ADAPTER_RANK
LANES = 128
PADDED = MODEL_WIDTH + LANES
HALF = MODEL_WIDTH // 2
MIB = 1024 * 1024


def transposed(block):
    return block.astype(jnp.float32).T


def once(shape):
    return pl.BlockSpec(shape, lambda *_: (0,) * len(shape), pipeline_mode=pl.Buffered(1))


def rows_of(shape, axis):
    return pl.BlockSpec(shape, lambda i: tuple(i if a == axis else 0 for a in range(len(shape))))


def standard(stream):
    center = stream - jnp.mean(stream, -1, keepdims=True)
    inverse = lax.rsqrt(jnp.mean(center * center, -1, keepdims=True) + norm_eps)
    return (center * inverse, inverse)


def assemble_kernel(
    place_ref, near_ref, far_ref, next_near_ref, next_far_ref, out_ref, sems, *, late_x
):
    z, x, core, y = (place_ref[i] for i in range(4))
    depth = out_ref.shape[1]
    copies = []
    for side, pair in enumerate(((near_ref, far_ref), (next_near_ref, next_far_ref))):
        source = core if side == 0 else 1 - core
        for stage, ref in enumerate(pair):
            for hop in range(2):
                by_x = stage if late_x else jnp.where(source == 0, hop, stage)
                by_y = hop + stage - by_x
                for shift in range(depth):
                    target = out_ref.at[
                        lax.rem(y + by_y, 2),
                        lax.rem(z + depth - shift, depth),
                        lax.rem(x + by_x, 2),
                        source,
                    ]
                    block = ref.at[shift, hop] if late_x else ref.at[hop, shift]
                    copy = pltpu.make_async_copy(block, target, sems.at[len(copies)])
                    copy.start()
                    copies.append(copy)
    for copy in copies:
        copy.wait()


def assemble(place, near, far, next_near, next_far, late_x):
    rows, columns = near.shape[2:]
    depth = near.shape[0] * near.shape[1] // 2
    return pl.pallas_call(
        functools.partial(assemble_kernel, late_x=late_x),
        in_specs=[pl.BlockSpec(memory_space=pltpu.SMEM)]
        + [pl.BlockSpec(memory_space=pltpu.VMEM)] * 4,
        out_specs=pl.BlockSpec(memory_space=pl.ANY),
        out_shape=jax.ShapeDtypeStruct((2, depth, 2, 2, rows, columns), near.dtype),
        scratch_shapes=[pltpu.SemaphoreType.DMA((8 * depth,))],
        cost_estimate=pl.CostEstimate(
            flops=0, bytes_accessed=16 * near.size, transcendentals=0
        ),
        compiler_params=pltpu.CompilerParams(vmem_limit_bytes=32 * MIB),
        name="assemble",
    )(place, near, far, next_near, next_far)


def entry_kernel(
    token_ref, mod_ref, weight_ref, up_ref, down_ref, hidden_ref, middle_ref, qkv_ref, weight_aug
):
    half = 3 * HALF

    @pl.when(pl.program_id(0) == 0)
    def _():
        weight_aug[:MODEL_WIDTH, :half] = weight_ref[0, :, HALF:]
        weight_aug[:MODEL_WIDTH, half:] = weight_ref[1, :, HALF:]
        weight_aug[MODEL_WIDTH:, :] = up_ref[...]

    normed, _ = standard(token_ref[...].astype(jnp.float32))
    hidden = (normed * (1.0 + mod_ref[1:2]) + mod_ref[0:1]).astype(jnp.bfloat16)
    middle = nt(hidden, down_ref[...]).astype(jnp.bfloat16)
    hidden_ref[...] = hidden
    middle_ref[...] = middle
    joined = jnp.concatenate([hidden, middle], 1)
    for part in range(3):
        columns = slice(part * MODEL_WIDTH, (part + 1) * MODEL_WIDTH)
        packed = nn(joined, weight_aug[:, columns])
        qkv_ref[part] = packed.T.reshape(qkv_ref.shape[1:]).astype(jnp.bfloat16)


def entry(tokens, mods, weight, up, down, tile=256):
    length = tokens.shape[0]
    bf16 = jnp.bfloat16
    return pl.pallas_call(
        entry_kernel,
        grid=(length // tile,),
        in_specs=[
            rows_of((tile, MODEL_WIDTH), 0),
            once(mods.shape),
            once(weight.shape),
            once(up.shape),
            once(down.shape),
        ],
        out_specs=[
            rows_of((tile, MODEL_WIDTH), 0),
            rows_of((tile, LANES), 0),
            rows_of((3, HEADS, HD, tile), 3),
        ],
        out_shape=[
            jax.ShapeDtypeStruct((length, MODEL_WIDTH), bf16),
            jax.ShapeDtypeStruct((length, LANES), bf16),
            jax.ShapeDtypeStruct((3, HEADS, HD, length), bf16),
        ],
        scratch_shapes=[pltpu.VMEM((PADDED, 3 * MODEL_WIDTH), bf16)],
        cost_estimate=pl.CostEstimate(
            flops=6 * length * MODEL_WIDTH * PADDED,
            bytes_accessed=2 * weight.size + 12 * length * MODEL_WIDTH,
            transcendentals=0,
        ),
        compiler_params=pltpu.CompilerParams(vmem_limit_bytes=56 * MIB),
        name="entry",
    )(tokens, mods, weight, up, down)


def load_proj(proj_aug, weight_ref, up_ref):
    @pl.when(pl.program_id(0) == 0)
    def _():
        proj_aug[:MODEL_WIDTH, :HALF] = weight_ref[0, :, :HALF]
        proj_aug[:MODEL_WIDTH, HALF:] = weight_ref[1, :, :HALF]
        proj_aug[MODEL_WIDTH:, :] = up_ref[...]


def before_kernel(
    mixed_ref,
    token_ref,
    cot_ref,
    mod_ref,
    weight_ref,
    up_proj_ref,
    down_proj_ref,
    down_expand_ref,
    up_shrink_ref,
    bias_ref,
    second_ref,
    dfinal_ref,
    branch_ref,
    middle_ref,
    proj_aug,
):
    bf16 = jnp.bfloat16
    load_proj(proj_aug, weight_ref, up_proj_ref)
    mixed = transposed(mixed_ref[...]).astype(bf16)
    middle_proj = nt(mixed, down_proj_ref[...])
    branch = nn(jnp.concatenate([mixed, middle_proj.astype(bf16)], 1), proj_aug[...])
    branch = branch + bias_ref[...]
    branch_ref[...] = branch
    residual = token_ref[...].astype(jnp.float32) + mod_ref[2:3] * branch
    normed, _ = standard(residual)
    second = (normed * (1.0 + mod_ref[4:5]) + mod_ref[3:4]).astype(bf16)
    middle_expand = nt(second, down_expand_ref[...])
    second_ref[:, :MODEL_WIDTH] = second
    second_ref[:, MODEL_WIDTH:] = middle_expand.astype(bf16)
    d_final = (mod_ref[5:6] * cot_ref[...].astype(jnp.float32)).astype(bf16)
    dmiddle_shrink = nt(d_final, up_shrink_ref[...])
    dfinal_ref[:, :MODEL_WIDTH] = d_final
    dfinal_ref[:, MODEL_WIDTH:] = dmiddle_shrink.astype(bf16)
    middle_ref[0] = middle_proj.T[:RANK].astype(bf16)
    middle_ref[1] = middle_expand.T[:RANK].astype(bf16)
    middle_ref[2] = dmiddle_shrink.T[:RANK].astype(bf16)


def before_feed(
    mixed, tokens, cotangent, mods, weight, up_proj, down_proj, down_expand, up_shrink, bias, tile=256
):
    length = tokens.shape[0]
    bf16 = jnp.bfloat16
    return pl.pallas_call(
        before_kernel,
        grid=(length // tile,),
        in_specs=[
            rows_of((MODEL_WIDTH, tile), 1),
            rows_of((tile, MODEL_WIDTH), 0),
            rows_of((tile, MODEL_WIDTH), 0),
            once(mods.shape),
            once((2, MODEL_WIDTH, 5 * LANES)),
            once(up_proj.shape),
            once(down_proj.shape),
            once(down_expand.shape),
            once(up_shrink.shape),
            once(bias.shape),
        ],
        out_specs=[
            rows_of((tile, PADDED), 0),
            rows_of((tile, PADDED), 0),
            rows_of((tile, MODEL_WIDTH), 0),
            rows_of((3, RANK, tile), 2),
        ],
        out_shape=[
            jax.ShapeDtypeStruct((length, PADDED), bf16),
            jax.ShapeDtypeStruct((length, PADDED), bf16),
            jax.ShapeDtypeStruct((length, MODEL_WIDTH), jnp.float32),
            jax.ShapeDtypeStruct((3, RANK, length), bf16),
        ],
        scratch_shapes=[pltpu.VMEM((PADDED, MODEL_WIDTH), bf16)],
        cost_estimate=pl.CostEstimate(
            flops=4 * length * MODEL_WIDTH * PADDED,
            bytes_accessed=16 * length * MODEL_WIDTH,
            transcendentals=0,
        ),
        compiler_params=pltpu.CompilerParams(vmem_limit_bytes=48 * MIB),
        name="before_feed",
    )(mixed, tokens, cotangent, mods, weight, up_proj, down_proj, down_expand, up_shrink, bias)


GELU_RATE = 0.7978845608
GELU_CUBE = 0.044715


def gelu_pair(inner, d_active):
    square = inner * inner
    tanh = jnp.tanh(inner * (GELU_RATE + (GELU_RATE * GELU_CUBE) * square))
    half = 0.5 + 0.5 * tanh
    slope = half + inner * (half * (1.0 - tanh)) * (
        GELU_RATE + (3.0 * GELU_CUBE * GELU_RATE) * square
    )
    return (inner * half).astype(jnp.bfloat16), (d_active * slope).astype(jnp.bfloat16)


def feed_kernel(
    second_ref, dfinal_ref, middle_ref, weight_ref, up_ref, down_ref, bias_ref,
    final_in_ref, dsecond_in_ref, final_ref, dsecond_ref, up_grad_ref, down_grad_ref,
    widen_aug, narrow_aug, *, rows, first, sub,
):
    width = MODEL_WIDTH
    chunks = weight_ref.shape[-1] // width
    for chunk in range(chunks):
        for side in range(2):
            part = slice(chunk * width + side * HALF, chunk * width + (side + 1) * HALF)
            widen_aug[:width, part] = weight_ref[side, :, chunk * width : chunk * width + HALF]
            narrow_aug[chunk * width : (chunk + 1) * width, side * HALF : (side + 1) * HALF] = weight_ref[side, :, chunk * width + HALF : (chunk + 1) * width]
    widen_aug[width:, :] = up_ref[...]
    narrow_aug[:, width:] = down_ref[...]
    length = second_ref.shape[0]
    for index in range(chunks * width // sub):
        cols = slice(index * sub, (index + 1) * sub)
        for start in range(0, length, rows):
            at = slice(start, start + rows)
            inner = nn(second_ref[at, :], widen_aug[:, cols]) + bias_ref[:, cols]
            active, d_inner = gelu_pair(inner, nt(dfinal_ref[at, :], narrow_aug[cols, :]))
            final = nn(active, narrow_aug[cols, :])
            dsecond = nt(d_inner, widen_aug[:, cols])
            if index == 0 and first:
                final_ref[at, :] = final
                dsecond_ref[at, :] = dsecond
            elif index == 0:
                final_ref[at, :] = final_in_ref[at, :] + final
                dsecond_ref[at, :] = dsecond_in_ref[at, :] + dsecond
            else:
                final_ref[at, :] += final
                dsecond_ref[at, :] += dsecond
            up_grad = nn(middle_ref[1, :, at], d_inner)
            down_grad = nn(middle_ref[2, :, at], active)
            if start == 0:
                up_grad_ref[:, cols] = up_grad
                down_grad_ref[:, cols] = down_grad
            else:
                up_grad_ref[:, cols] += up_grad
                down_grad_ref[:, cols] += down_grad


def feed(second, dfinal, middles, weight, up, down, bias, sums, rows=1024, sub=768):
    length, padded = second.shape
    hidden = weight.shape[-1]
    first = sums is None
    if first:
        sums = (jnp.zeros((8, LANES), jnp.float32),) * 2
    return pl.pallas_call(
        functools.partial(feed_kernel, rows=rows, first=first, sub=sub),
        grid=(1,),
        in_specs=[
            once((length, padded)), once((length, padded)), once(middles.shape),
            once(weight.shape), once(up.shape), once(down.shape), once(bias.shape),
            once(sums[0].shape), once(sums[1].shape),
        ],
        out_specs=[once((length, padded)), once((length, padded)), once((RANK, hidden)), once((RANK, hidden))],
        out_shape=[
            jax.ShapeDtypeStruct((length, padded), jnp.float32),
            jax.ShapeDtypeStruct((length, padded), jnp.float32),
            jax.ShapeDtypeStruct((RANK, hidden), jnp.float32),
            jax.ShapeDtypeStruct((RANK, hidden), jnp.float32),
        ],
        scratch_shapes=[pltpu.VMEM((padded, hidden), jnp.bfloat16), pltpu.VMEM((hidden, padded), jnp.bfloat16)],
        input_output_aliases={} if first else {7: 0, 8: 1},
        cost_estimate=pl.CostEstimate(
            flops=8 * length * padded * hidden,
            bytes_accessed=2 * weight.size + 12 * length * padded,
            transcendentals=length * hidden,
        ),
        compiler_params=pltpu.CompilerParams(vmem_limit_bytes=63 * MIB),
        name="feed",
    )(second, dfinal, middles, weight, up, down, bias, *sums)


def back_through(gradient, normed, inverse):
    return inverse * (
        gradient
        - jnp.mean(gradient, -1, keepdims=True)
        - normed * jnp.mean(gradient * normed, -1, keepdims=True)
    )


def total(values):
    return jnp.sum(values, axis=0, keepdims=True)


def after_kernel(
    final_ref,
    dsecond_ref,
    token_ref,
    cot_ref,
    branch_ref,
    second_ref,
    dfinal_ref,
    mixed_ref,
    middle_ref,
    mod_ref,
    weight_ref,
    up_proj_ref,
    down_proj_ref,
    down_expand_ref,
    up_shrink_ref,
    bias_ref,
    block_ref,
    dresidual_ref,
    dmixed_ref,
    sums_ref,
    up_shrink_grad,
    down_expand_grad,
    up_proj_grad,
    down_proj_grad,
    proj_aug,
):
    bf16 = jnp.bfloat16
    load_proj(proj_aug, weight_ref, up_proj_ref)
    cot = cot_ref[...].astype(jnp.float32)
    branch = branch_ref[...]
    residual = token_ref[...].astype(jnp.float32) + mod_ref[2:3] * branch
    normed, inverse = standard(residual)
    middle_shrink = final_ref[:, MODEL_WIDTH:]
    final = final_ref[:, :MODEL_WIDTH] + bias_ref[...]
    final = final + nn(middle_shrink.astype(bf16), up_shrink_ref[...])
    block_ref[...] = (residual + mod_ref[5:6] * final).astype(bf16)
    dmiddle_expand = dsecond_ref[:, MODEL_WIDTH:]
    d_second = dsecond_ref[:, :MODEL_WIDTH] + nn(dmiddle_expand.astype(bf16), down_expand_ref[...])
    d_residual = cot + back_through(d_second * (1.0 + mod_ref[4:5]), normed, inverse)
    dresidual_ref[...] = d_residual
    d_branch = (mod_ref[2:3] * d_residual).astype(bf16)
    joined = nt(d_branch, proj_aug[...])
    dmiddle_proj = joined[:, MODEL_WIDTH:].astype(bf16)
    d_mixed = joined[:, :MODEL_WIDTH] + nn(dmiddle_proj, down_proj_ref[...])
    dmixed_ref[...] = d_mixed.T.astype(bf16)
    sums = jnp.concatenate(
        [
            total(d_residual * branch),
            total(d_second),
            total(d_second * normed),
            total(cot * final),
            jnp.zeros((4, MODEL_WIDTH), jnp.float32),
        ],
        0,
    )
    grads = (
        nn(middle_shrink.T[:RANK].astype(bf16), dfinal_ref[...]),
        nn(dmiddle_expand.T[:RANK].astype(bf16), second_ref[...]),
        nn(middle_ref[0], d_branch),
        nn(mixed_ref[...], dmiddle_proj),
    )
    refs = (up_shrink_grad, down_expand_grad, up_proj_grad, down_proj_grad)

    @pl.when(pl.program_id(0) == 0)
    def _():
        sums_ref[...] = sums
        for ref, grad in zip(refs, grads):
            ref[...] = grad

    @pl.when(pl.program_id(0) > 0)
    def _():
        sums_ref[...] += sums
        for ref, grad in zip(refs, grads):
            ref[...] += grad


def after_feed(
    final,
    dsecond,
    tokens,
    cotangent,
    branch,
    second,
    dfinal,
    mixed,
    middles,
    mods,
    weight,
    up_proj,
    down_proj,
    down_expand,
    up_shrink,
    bias,
    tile=256,
):
    length = tokens.shape[0]
    bf16, f32 = jnp.bfloat16, jnp.float32
    low_rank = jax.ShapeDtypeStruct((RANK, MODEL_WIDTH), f32)
    return pl.pallas_call(
        after_kernel,
        grid=(length // tile,),
        in_specs=[
            rows_of((tile, PADDED), 0),
            rows_of((tile, PADDED), 0),
            rows_of((tile, MODEL_WIDTH), 0),
            rows_of((tile, MODEL_WIDTH), 0),
            rows_of((tile, MODEL_WIDTH), 0),
            rows_of((tile, MODEL_WIDTH), 0),
            rows_of((tile, MODEL_WIDTH), 0),
            rows_of((MODEL_WIDTH, tile), 1),
            rows_of((3, RANK, tile), 2),
            once(mods.shape),
            once((2, MODEL_WIDTH, 5 * LANES)),
            once(up_proj.shape),
            once(down_proj.shape),
            once(down_expand.shape),
            once(up_shrink.shape),
            once(bias.shape),
        ],
        out_specs=[
            rows_of((tile, MODEL_WIDTH), 0),
            rows_of((tile, MODEL_WIDTH), 0),
            rows_of((MODEL_WIDTH, tile), 1),
            once((8, MODEL_WIDTH)),
            once((RANK, MODEL_WIDTH)),
            once((RANK, MODEL_WIDTH)),
            once((RANK, MODEL_WIDTH)),
            once((MODEL_WIDTH, LANES)),
        ],
        out_shape=[
            jax.ShapeDtypeStruct((length, MODEL_WIDTH), bf16),
            jax.ShapeDtypeStruct((length, MODEL_WIDTH), f32),
            jax.ShapeDtypeStruct((MODEL_WIDTH, length), bf16),
            jax.ShapeDtypeStruct((8, MODEL_WIDTH), f32),
            low_rank,
            low_rank,
            low_rank,
            jax.ShapeDtypeStruct((MODEL_WIDTH, LANES), f32),
        ],
        scratch_shapes=[pltpu.VMEM((PADDED, MODEL_WIDTH), bf16)],
        cost_estimate=pl.CostEstimate(
            flops=5 * length * MODEL_WIDTH * PADDED,
            bytes_accessed=32 * length * MODEL_WIDTH,
            transcendentals=0,
        ),
        compiler_params=pltpu.CompilerParams(vmem_limit_bytes=60 * MIB),
        name="after_feed",
    )(
        final,
        dsecond,
        tokens,
        cotangent,
        branch,
        second,
        dfinal,
        mixed,
        middles,
        mods,
        weight,
        up_proj,
        down_proj,
        down_expand,
        up_shrink,
        bias,
    )


def leave_kernel(
    dqkv_ref,
    token_ref,
    dresidual_ref,
    hidden_ref,
    middle_ref,
    mod_ref,
    weight_ref,
    up_ref,
    down_ref,
    token_grad_ref,
    sums_ref,
    up_grad,
    down_grad,
    weight_aug,
):
    bf16 = jnp.bfloat16
    half = 3 * HALF

    @pl.when(pl.program_id(0) == 0)
    def _():
        weight_aug[:MODEL_WIDTH, :half] = weight_ref[0, :, HALF:]
        weight_aug[:MODEL_WIDTH, half:] = weight_ref[1, :, HALF:]
        weight_aug[MODEL_WIDTH:, :] = up_ref[...]

    tile = token_ref.shape[0]
    middle_t = transposed(middle_ref[...])[:RANK].astype(bf16)
    joined = jnp.zeros((tile, PADDED), jnp.float32)
    up_grads = []
    for part in range(3):
        columns = slice(part * MODEL_WIDTH, (part + 1) * MODEL_WIDTH)
        packed_t = dqkv_ref[part].astype(jnp.float32).reshape(MODEL_WIDTH, tile)
        packed = packed_t.T.astype(bf16)
        joined = joined + nt(packed, weight_aug[:, columns])
        up_grads.append(nn(middle_t, packed))
    dmiddle = joined[:, MODEL_WIDTH:]
    d_hidden = joined[:, :MODEL_WIDTH] + nn(dmiddle.astype(bf16), down_ref[...])
    normed, inverse = standard(token_ref[...].astype(jnp.float32))
    back = back_through(d_hidden * (1.0 + mod_ref[1:2]), normed, inverse)
    token_grad_ref[...] = (dresidual_ref[...] + back).astype(bf16)
    sums = jnp.concatenate(
        [total(d_hidden), total(d_hidden * normed), jnp.zeros((6, MODEL_WIDTH), jnp.float32)], 0
    )
    down = nn(dmiddle.T[:RANK].astype(bf16), hidden_ref[...])

    @pl.when(pl.program_id(0) == 0)
    def _():
        sums_ref[...] = sums
        down_grad[...] = down
        for part in range(3):
            up_grad[:, part * MODEL_WIDTH : (part + 1) * MODEL_WIDTH] = up_grads[part]

    @pl.when(pl.program_id(0) > 0)
    def _():
        sums_ref[...] += sums
        down_grad[...] += down
        for part in range(3):
            up_grad[:, part * MODEL_WIDTH : (part + 1) * MODEL_WIDTH] += up_grads[part]


def leave(dqkv, tokens, dresidual, hidden, middle, mods, weight, up, down, tile=256):
    length = tokens.shape[0]
    bf16, f32 = jnp.bfloat16, jnp.float32
    return pl.pallas_call(
        leave_kernel,
        grid=(length // tile,),
        in_specs=[
            rows_of((3, HEADS, HD, tile), 3),
            rows_of((tile, MODEL_WIDTH), 0),
            rows_of((tile, MODEL_WIDTH), 0),
            rows_of((tile, MODEL_WIDTH), 0),
            rows_of((tile, LANES), 0),
            once(mods.shape),
            once(weight.shape),
            once(up.shape),
            once(down.shape),
        ],
        out_specs=[
            rows_of((tile, MODEL_WIDTH), 0),
            once((8, MODEL_WIDTH)),
            once((RANK, 3 * MODEL_WIDTH)),
            once((RANK, MODEL_WIDTH)),
        ],
        out_shape=[
            jax.ShapeDtypeStruct((length, MODEL_WIDTH), bf16),
            jax.ShapeDtypeStruct((8, MODEL_WIDTH), f32),
            jax.ShapeDtypeStruct((RANK, 3 * MODEL_WIDTH), f32),
            jax.ShapeDtypeStruct((RANK, MODEL_WIDTH), f32),
        ],
        scratch_shapes=[pltpu.VMEM((PADDED, 3 * MODEL_WIDTH), bf16)],
        cost_estimate=pl.CostEstimate(
            flops=7 * length * MODEL_WIDTH * PADDED,
            bytes_accessed=2 * weight.size + 18 * length * MODEL_WIDTH,
            transcendentals=0,
        ),
        compiler_params=pltpu.CompilerParams(vmem_limit_bytes=60 * MIB),
        name="leave",
    )(dqkv, tokens, dresidual, hidden, middle, mods, weight, up, down)


def layout(n_fsdp):
    return [(f // 4, f // 2 % 2, f % 2) for f in range(n_fsdp)]


def moved(n_fsdp, step):
    pairs = []
    for f, (z, x, c) in enumerate(layout(n_fsdp)):
        for y in range(2):
            to_z, to_x, to_c, to_y = step(z, x, c, y)
            pairs.append((2 * f + y, 2 * (4 * to_z + 2 * to_x + to_c) + to_y))
    return pairs


BOTH = ("fsdp", "seq")


def step_z(block, n_fsdp):
    depth = n_fsdp // 4
    by_shift = [block]
    for shift in range(1, depth):
        pairs = moved(n_fsdp, lambda z, x, c, y: ((z + shift) % depth, x, c, y))
        by_shift.append(lax.ppermute(block, BOTH, pairs))
    return jnp.stack(by_shift)


def step_first(block, n_fsdp):
    return lax.ppermute(
        block,
        BOTH,
        moved(n_fsdp, lambda z, x, c, y: (z, x, c, 1 - y) if c else (z, 1 - x, c, y)),
    )


def step_second(block, n_fsdp):
    return lax.ppermute(
        block,
        BOTH,
        moved(n_fsdp, lambda z, x, c, y: (z, 1 - x, c, y) if c else (z, x, c, 1 - y)),
    )


def step_x(block, n_fsdp):
    return lax.ppermute(block, BOTH, moved(n_fsdp, lambda z, x, c, y: (z, 1 - x, c, y)))


def step_core(block, n_fsdp):
    return lax.ppermute(block, BOTH, moved(n_fsdp, lambda z, x, c, y: (z, x, 1 - c, y)))


def behind(block, *earlier):
    return lax.optimization_barrier((block, *earlier))[0]


def complete(near, far, n_fsdp, place, late_x=False):
    rows, columns = near.shape[2:]
    gathered = assemble(
        place, near, far, step_core(near, n_fsdp), step_core(far, n_fsdp), late_x
    )
    return gathered.reshape(2, n_fsdp * rows, columns)


def gather_all(blocks, n_fsdp, place, told, mod_base, parts):
    heads_block, low_block, high_block = blocks
    heads_line = behind(step_z(heads_block, n_fsdp), told)
    heads_near = jnp.stack([heads_line, step_first(heads_line, n_fsdp)])
    heads_far = step_second(behind(heads_near, mod_base), n_fsdp)
    low_line = step_z(behind(low_block, heads_line), n_fsdp)
    low_line = behind(low_line, heads_far)
    low_near = jnp.stack([low_line, step_first(low_line, n_fsdp)])
    low_far = step_second(low_near, n_fsdp)
    high_pair = jnp.stack([high_block, swap(behind(high_block, heads_line))])
    high_near = step_z(behind(high_pair, low_line), n_fsdp)
    high_far = step_x(behind(high_near, low_far), n_fsdp)
    return (
        complete(behind(heads_near, *parts), behind(heads_far, *parts), n_fsdp, place),
        complete(low_near, low_far, n_fsdp, place),
        complete(high_near, high_far, n_fsdp, place, True),
        heads_far,
        high_far,
    )


DOWN_EDGES = (0, 1152, 2304, 3456, 4608, 9216)
UP_EDGES = (0, 6912, 10368, 11520, 16128, 17280)
PIECES = FF // HD


def piece_order(n_fsdp):
    per = PIECES // n_fsdp
    return [f * per + q for q in range(per) for f in range(n_fsdp)]


def unpack_kernel(came_ref, *refs, order, down_chunk, up_chunk):
    bf16 = jnp.bfloat16
    outs, (down_all, up_all, mixed) = refs[:-3], refs[-3:]
    down_outs, up_outs, shrink_t = outs[:4], outs[4:9], outs[9]
    for f in range(came_ref.shape[0]):
        block = came_ref[f].astype(jnp.float32)
        down_all[:, f * down_chunk : (f + 1) * down_chunk] = block[:, :down_chunk]
        up_all[:, f * up_chunk : (f + 1) * up_chunk] = block[:, down_chunk:]
    for target, out in enumerate(down_outs):
        out[...] = jnp.zeros_like(out)
        out[:RANK] = down_all[:, DOWN_EDGES[target] : DOWN_EDGES[target + 1]].astype(bf16)
    mixed[...] = jnp.zeros_like(mixed)
    for target, out in enumerate(up_outs):
        if target == 3:
            for to, piece in enumerate(order):
                at = UP_EDGES[3] + piece * HD
                mixed[:RANK, to * HD : (to + 1) * HD] = up_all[:, at : at + HD]
            out[...] = mixed[...].astype(bf16)
        else:
            out[...] = jnp.zeros_like(out)
            out[:RANK] = up_all[:, UP_EDGES[target] : UP_EDGES[target + 1]].astype(bf16)
    for to, piece in enumerate(order):
        at = DOWN_EDGES[4] + piece * HD
        mixed[:RANK, to * HD : (to + 1) * HD] = down_all[:, at : at + HD]
    for start in range(0, FF, MODEL_WIDTH):
        shrink_t[start : start + MODEL_WIDTH, :] = mixed[:, start : start + MODEL_WIDTH].T.astype(
            bf16
        )


def unpack(came, order, down_chunk, up_chunk):
    bf16 = jnp.bfloat16
    widths = [DOWN_EDGES[t + 1] - DOWN_EDGES[t] for t in range(4)]
    widths += [UP_EDGES[t + 1] - UP_EDGES[t] for t in range(5)]
    return pl.pallas_call(
        functools.partial(
            unpack_kernel, order=order, down_chunk=down_chunk, up_chunk=up_chunk
        ),
        out_shape=[jax.ShapeDtypeStruct((LANES, w), bf16) for w in widths]
        + [jax.ShapeDtypeStruct((FF, LANES), bf16)],
        scratch_shapes=[
            pltpu.VMEM((RANK, DOWN_EDGES[5]), jnp.float32),
            pltpu.VMEM((RANK, UP_EDGES[5]), jnp.float32),
            pltpu.VMEM((LANES, FF), jnp.float32),
        ],
        compiler_params=pltpu.CompilerParams(vmem_limit_bytes=48 * MIB),
        name="unpack",
    )(came)


def pack_kernel(
    leave_ref,
    after_ref,
    middle_ref,
    cond_ref,
    down_ada_ref,
    up_ada_ref,
    down_qkv,
    up_qkv,
    down_proj,
    up_proj,
    down_expand,
    up_expand_low,
    up_expand_high,
    down_shrink_low,
    down_shrink_high,
    up_shrink,
    sent_ref,
    dmod_ref,
    own_ref,
    down_all,
    up_all,
    *,
    order,
    down_chunk,
    up_chunk,
):
    bf16, f32 = jnp.bfloat16, jnp.float32
    width = MODEL_WIDTH
    dmiddle = jnp.zeros((RANK, 1), f32)
    for block in range(6):
        source = leave_ref if block < 2 else after_ref
        line = source[block % 2 if block < 2 else block - 2, :].reshape(1, width)
        line = line.astype(bf16).astype(f32)
        columns = slice(block * width, (block + 1) * width)
        side, at = block // 3, block % 3 * width
        dmod_ref[side : side + 1, at : at + width] = line
        up_all[:, columns] = middle_ref[...] * line
        dmiddle += jnp.sum(up_ada_ref[:RANK, columns].astype(f32) * line, axis=1, keepdims=True)
    dmiddle = dmiddle.astype(bf16).astype(f32)
    down_all[:, :width] = dmiddle * cond_ref[...]
    own_ref[...] = total(dmiddle * down_ada_ref[:RANK].astype(f32))
    down_all[:, width : 2 * width] = down_qkv[...]
    down_all[:, 2 * width : 3 * width] = down_proj[...].T[:RANK]
    down_all[:, 3 * width : 4 * width] = down_expand[...]
    up_all[:, UP_EDGES[1] : UP_EDGES[2]] = up_qkv[...]
    up_all[:, UP_EDGES[2] : UP_EDGES[3]] = up_proj[...]
    up_all[:, UP_EDGES[4] : UP_EDGES[5]] = up_shrink[...]
    half = PIECES // 2
    for at, piece in enumerate(order):
        ups = up_expand_low if at < half else up_expand_high
        downs = down_shrink_low if at < half else down_shrink_high
        columns = slice((at % half) * HD, (at % half + 1) * HD)
        to = UP_EDGES[3] + piece * HD
        up_all[:, to : to + HD] = ups[:, columns]
        to = DOWN_EDGES[4] + piece * HD
        down_all[:, to : to + HD] = downs[:, columns]
    for f in range(sent_ref.shape[0]):
        sent_ref[f, :, :down_chunk] = down_all[:, f * down_chunk : (f + 1) * down_chunk].astype(bf16)
        sent_ref[f, :, down_chunk:] = up_all[:, f * up_chunk : (f + 1) * up_chunk].astype(bf16)


def pack(operands, n_fsdp, order, down_chunk, up_chunk):
    bf16, f32 = jnp.bfloat16, jnp.float32
    return pl.pallas_call(
        functools.partial(pack_kernel, order=order, down_chunk=down_chunk, up_chunk=up_chunk),
        out_shape=[
            jax.ShapeDtypeStruct((n_fsdp, RANK, down_chunk + up_chunk), bf16),
            jax.ShapeDtypeStruct((2, 3 * MODEL_WIDTH), f32),
            jax.ShapeDtypeStruct((1, MODEL_WIDTH), f32),
        ],
        scratch_shapes=[
            pltpu.VMEM((RANK, DOWN_EDGES[5]), f32),
            pltpu.VMEM((RANK, UP_EDGES[5]), f32),
        ],
        compiler_params=pltpu.CompilerParams(vmem_limit_bytes=48 * MIB),
        name="pack",
    )(*operands)


def owners_kernel(ids_ref, place_ref, came_ref, kept_ref, given_ref, sums):
    sums[...] = jnp.zeros_like(sums)
    for f in range(came_ref.shape[0]):
        sums[ids_ref[f]] += came_ref[f].astype(jnp.float32)
    held = kept_ref.shape[0]
    mine = place_ref[3]
    for index in range(held):
        kept_ref[index] = sums[mine * held + index]
        given_ref[index] = sums[(1 - mine) * held + index].astype(jnp.bfloat16)


def owners(ids, place, came):
    held = ADAPTER_COUNT // 2
    shape = (held,) + came.shape[1:]
    return pl.pallas_call(
        owners_kernel,
        in_specs=[
            pl.BlockSpec(memory_space=pltpu.SMEM),
            pl.BlockSpec(memory_space=pltpu.SMEM),
            pl.BlockSpec(memory_space=pltpu.VMEM),
        ],
        out_shape=[
            jax.ShapeDtypeStruct(shape, jnp.float32),
            jax.ShapeDtypeStruct(shape, jnp.bfloat16),
        ],
        scratch_shapes=[pltpu.VMEM((ADAPTER_COUNT,) + came.shape[1:], jnp.float32)],
        compiler_params=pltpu.CompilerParams(vmem_limit_bytes=32 * MIB),
        name="owners",
    )(ids, place, came)


def update_kernel(gradient_ref, squared_ref, *refs):
    down_chunk = refs[0].shape[-1]
    grad_norm = jnp.sqrt(jnp.sum(squared_ref[:, :1], axis=0, keepdims=True))
    clip_factor = jnp.minimum(1.0, clip_limit / (grad_norm + norm_eps))
    ins, outs, norm_ref = refs[:6], refs[6:12], refs[12]
    norm_ref[...] = jnp.broadcast_to(grad_norm, norm_ref.shape)
    for kind in range(2):
        part = slice(0, down_chunk) if kind == 0 else slice(down_chunk, None)
        for index in range(gradient_ref.shape[0]):
            gradient = gradient_ref[index, :, part] * clip_factor
            params = ins[kind][index]
            moment_new = beta_first * ins[2 + kind][index] + (1.0 - beta_first) * gradient
            square_new = (
                beta_second * ins[4 + kind][index] + (1.0 - beta_second) * gradient * gradient
            )
            direction = (
                moment_new
                / (1.0 - beta_first**STEP)
                / (jnp.sqrt(square_new / (1.0 - beta_second**STEP)) + adam_eps)
            )
            outs[kind][index] = params - learn_rate * (direction + decay_rate * params)
            outs[2 + kind][index] = moment_new
            outs[4 + kind][index] = square_new


def update(gradient, squared, states):
    f32 = jnp.float32
    outs = pl.pallas_call(
        update_kernel,
        out_shape=[jax.ShapeDtypeStruct(s.shape, f32) for s in states]
        + [jax.ShapeDtypeStruct((8, LANES), f32)],
        compiler_params=pltpu.CompilerParams(vmem_limit_bytes=32 * MIB),
        name="update",
    )(gradient, squared, *states)
    return outs[:6], outs[6][0, 0]


def fits(mesh):
    return mesh.shape["seq"] == MB and mesh.shape["fsdp"] == 16


def dot(equation, left, right):
    return jnp.einsum(equation, left, right, preferred_element_type=jnp.float32)


def swap(block):
    return lax.ppermute(block, "seq", [(0, 1), (1, 0)])


def by_seq(own, other, mine):
    first = mine == 0
    return jnp.stack([jnp.where(first, own, other), jnp.where(first, other, own)])


def swap_rows(halves, mine):
    sent = lax.dynamic_index_in_dim(halves, 1 - mine, 0, False)
    return by_seq(lax.dynamic_index_in_dim(halves, mine, 0, False), swap(sent), mine)


def to_all(block):
    return lax.all_to_all(block, ("fsdp", "seq"), split_axis=0, concat_axis=0, tiled=True)


def to_fsdp(block):
    return lax.all_to_all(block, "fsdp", split_axis=0, concat_axis=0, tiled=True)


def fast_shards(
    tokens,
    condition,
    adapter,
    cotangent,
    modulation_weight,
    modulation_bias,
    query_key_value_weight,
    attention_out_weight,
    attention_out_bias,
    widen_weight,
    widen_bias,
    narrow_weight,
    narrow_bias,
    lowrank_down,
    lowrank_up,
    first_moment_down,
    first_moment_up,
    second_moment_down,
    second_moment_up,
):
    bf16 = jnp.bfloat16
    n_fsdp = lax.axis_size("fsdp")
    mine = lax.axis_index("seq")
    row = lax.axis_index("fsdp")
    place = jnp.stack([row // 4, row // 2 % 2, row % 2, mine]).astype(jnp.int32)
    down_chunk, up_chunk = lowrank_down.shape[-1], lowrank_up.shape[-1]
    depth = modulation_weight.shape[0]
    order = piece_order(n_fsdp)
    per = PIECES // n_fsdp

    cond_act_pair = jax.nn.silu(condition).astype(bf16)
    told = jnp.moveaxis(cond_act_pair.reshape(MB, n_fsdp, depth), 1, 0)
    numbers = jnp.broadcast_to(adapter.astype(bf16)[None, :, None], (n_fsdp, MB, 8))
    told = to_fsdp(jnp.concatenate([told, numbers], 2))
    own_ids = lax.dynamic_index_in_dim(told[:, :, depth], mine, 1, False).astype(jnp.int32)

    wide = jnp.moveaxis(widen_weight.reshape(depth, -1, per, HD), 2, 0).reshape(per, depth, HALF)
    narrow = narrow_weight.reshape(per, depth, HALF)
    joined = [jnp.concatenate([wide[q], narrow[q]], 1) for q in range(per)]
    portions = jnp.concatenate([lowrank_down.astype(bf16), lowrank_up.astype(bf16)], -1)
    others = swap(portions)
    table = by_seq(portions, others, mine).reshape(ADAPTER_COUNT, RANK, -1)
    picks = jax.nn.one_hot(own_ids, ADAPTER_COUNT, dtype=bf16)
    chosen = dot("fa,arc->frc", picks, table).astype(bf16)
    parts = unpack(to_fsdp(chosen), order, down_chunk, up_chunk)
    down_ada, down_qkv, down_proj, down_expand = parts[:4]
    up_ada, up_qkv, up_proj, up_expand, up_shrink = parts[4:9]
    down_shrink_t = parts[9]

    spoken = told[:, :, :depth].reshape(n_fsdp * MB, depth)
    mod_part = to_all(dot("si,io->so", spoken, modulation_weight))
    mod_base = jnp.sum(mod_part.reshape(n_fsdp, MB, -1), axis=0).reshape(1, -1)

    heads_weight, low_weight, high_weight, arrived, ended = gather_all(
        (
            jnp.concatenate([attention_out_weight, query_key_value_weight], 1),
            jnp.concatenate(joined[: per // 2], 1),
            jnp.concatenate(joined[per // 2 :], 1),
        ),
        n_fsdp,
        place,
        told,
        mod_base,
        parts,
    )
    cond_act = lax.dynamic_slice_in_dim(cond_act_pair, mine, 1, 0)
    middle_ada = dot("ti,ri->tr", cond_act, down_ada).astype(bf16)
    modulation = mod_base + modulation_bias + dot("tr,ro->to", middle_ada, up_ada)
    mods = jnp.pad(modulation.reshape(6, MODEL_WIDTH), ((0, 2), (0, 0)))

    length = MB * tokens.shape[1]
    token_rows = swap_rows(tokens, mine).reshape(length, MODEL_WIDTH)
    cot_rows = swap_rows(behind(cotangent, arrived), mine).reshape(length, MODEL_WIDTH)

    hidden, middle_qkv, qkv = entry(token_rows, mods, heads_weight, up_qkv, down_qkv)
    mixed_heads, log_total = heads_forward(qkv, step=length)
    mixed = mixed_heads.reshape(MODEL_WIDTH, length)
    second, dfinal, branch, middles = before_feed(
        mixed,
        token_rows,
        cot_rows,
        mods,
        heads_weight,
        up_proj,
        down_proj,
        down_expand,
        up_shrink,
        attention_out_bias[None],
    )
    bias = jnp.moveaxis(widen_bias.reshape(n_fsdp, per, HD), 0, 1).reshape(1, FF)
    cut = FF // 2
    final, dsecond, up_expand_low, down_shrink_low = feed(
        second,
        dfinal,
        middles,
        low_weight,
        up_expand[:, :cut],
        down_shrink_t[:cut],
        bias[:, :cut],
        None,
    )
    final, dsecond, up_expand_high, down_shrink_high = feed(
        second,
        dfinal,
        middles,
        high_weight,
        up_expand[:, cut:],
        down_shrink_t[cut:],
        bias[:, cut:],
        (final, dsecond),
    )
    (
        block_rows,
        d_residual,
        d_mixed,
        after_sums,
        up_shrink_grad,
        down_expand_grad,
        up_proj_grad,
        down_proj_grad,
    ) = after_feed(
        final,
        dsecond,
        token_rows,
        cot_rows,
        branch,
        second,
        dfinal,
        mixed,
        middles,
        mods,
        heads_weight,
        up_proj,
        down_proj,
        down_expand,
        up_shrink,
        narrow_bias[None],
    )
    block_out = swap_rows(block_rows.reshape(tokens.shape), mine)
    d_qkv = heads_back(qkv, d_mixed.reshape(HEADS, HD, length), log_total, step=length // 2)
    token_rows_grad, leave_sums, up_qkv_grad, down_qkv_grad = leave(
        d_qkv, token_rows, d_residual, hidden, middle_qkv, mods, heads_weight, up_qkv, down_qkv
    )

    sent, d_modulation, own_cond = pack(
        (
            leave_sums,
            after_sums,
            middle_ada[:, :RANK].astype(jnp.float32).T,
            cond_act.astype(jnp.float32),
            down_ada,
            up_ada,
            down_qkv_grad,
            up_qkv_grad,
            down_proj_grad,
            up_proj_grad,
            down_expand_grad,
            up_expand_low,
            up_expand_high,
            down_shrink_low,
            down_shrink_high,
            up_shrink_grad,
        ),
        n_fsdp,
        order,
        down_chunk,
        up_chunk,
    )
    kept, given = owners(own_ids, place, to_fsdp(sent))
    gradient = kept + swap(given).astype(jnp.float32)
    squared = to_all(jnp.broadcast_to(jnp.sum(gradient * gradient), (n_fsdp * MB, LANES)))

    half_weight = lax.all_gather(
        behind(modulation_weight, ended), "fsdp", axis=0, tiled=True
    )
    both_mod = swap_rows(d_modulation.astype(bf16), mine)
    d_cond = dot("so,io->si", both_mod, half_weight)
    d_cond = d_cond + jnp.where(jnp.arange(MB)[:, None] == mine, own_cond, 0.0)
    d_cond = d_cond + swap(d_cond)
    cond_grad = jax.vjp(jax.nn.silu, condition)[1](d_cond)[0]
    token_grad = swap_rows(token_rows_grad.reshape(tokens.shape), mine).astype(jnp.float32)

    states = (
        lowrank_down,
        lowrank_up,
        first_moment_down,
        first_moment_up,
        second_moment_down,
        second_moment_up,
    )
    fresh, grad_norm = update(gradient, squared, states)
    return (block_out, token_grad, cond_grad, grad_norm, *fresh)


def solution(mesh):
    in_specs = (
        P("fsdp", "seq", None),
        P("fsdp", None),
        P("fsdp"),
        P("fsdp", "seq", None),
        P("fsdp", "seq"),
        P(),
        P("fsdp", "seq"),
        P("fsdp", "seq"),
        P(),
        P("fsdp", "seq"),
        P(),
        P("fsdp", "seq"),
        P(),
        P("seq", None, "fsdp"),
        P("seq", None, "fsdp"),
        P("seq", None, "fsdp"),
        P("seq", None, "fsdp"),
        P("seq", None, "fsdp"),
        P("seq", None, "fsdp"),
    )
    out_specs = (
        P("fsdp", "seq", None),
        P("fsdp", "seq", None),
        P("fsdp", None),
        P(),
        P("seq", None, "fsdp"),
        P("seq", None, "fsdp"),
        P("seq", None, "fsdp"),
        P("seq", None, "fsdp"),
        P("seq", None, "fsdp"),
        P("seq", None, "fsdp"),
    )
    body = fast_shards if fits(mesh) else shards
    return jax.shard_map(body, mesh=mesh, in_specs=in_specs, out_specs=out_specs, check_vma=False)
```

```python
import functools

import jax
import jax.numpy as jnp
from jax import lax
from jax.experimental import pallas as pl
from jax.experimental.pallas import tpu as pltpu
from jax.sharding import PartitionSpec as P

MODEL_WIDTH = 1152
HD = 72
FF = 4608
ADAPTER_RANK = 16
ADAPTER_COUNT = 8
MB = 2
SEQ_MB = 1
STEP = 10


beta_first = 0.9
beta_second = 0.999
learn_rate = 0.05
decay_rate = 0.1
adam_eps = 1e-08
clip_limit = 1.0
norm_eps = 1e-06
pair_heads = 2
highest = lax.Precision.HIGHEST


def linear(inputs, weight):
    return jnp.einsum("sti,io->sto", inputs, weight, preferred_element_type=jnp.float32)


def linear_back(gradient, weight):
    return jnp.einsum("sto,io->sti", gradient, weight, preferred_element_type=jnp.float32)


def normalize(stream):
    center = stream - jnp.mean(stream, -1, keepdims=True)
    inverse = lax.rsqrt(jnp.mean(center * center, -1, keepdims=True) + norm_eps)
    return (center * inverse, inverse)


def normalize_back(gradient, normed, inverse):
    return inverse * (
        gradient
        - jnp.mean(gradient, -1, keepdims=True)
        - normed * jnp.mean(gradient * normed, -1, keepdims=True)
    )


def adapt_forward(inputs, down_part, up_part):
    middle = jnp.einsum(
        "sti,sri->str", inputs, down_part, preferred_element_type=jnp.float32
    ).astype(jnp.bfloat16)
    return (middle, jnp.einsum("str,sro->sto", middle, up_part, preferred_element_type=jnp.float32))


def adapt_backward(inputs, middle, gradient, down_part, up_part):
    up_grad = jnp.einsum("str,sto->sro", middle, gradient, preferred_element_type=jnp.float32)
    middle_grad = jnp.einsum(
        "sto,sro->str", gradient, up_part, preferred_element_type=jnp.float32
    ).astype(jnp.bfloat16)
    down_grad = jnp.einsum("str,sti->sri", middle_grad, inputs, preferred_element_type=jnp.float32)
    input_grad = jnp.einsum(
        "str,sri->sti", middle_grad, down_part, preferred_element_type=jnp.float32
    )
    return (input_grad, down_grad, up_grad)


def grouped(matrix):
    seq_count, row_count, col_count = matrix.shape
    return jnp.moveaxis(
        matrix.reshape(seq_count, row_count, col_count // (pair_heads * HD), pair_heads, HD), 2, 0
    )


def ungrouped(stacked):
    moved = jnp.moveaxis(stacked, 0, 2)
    return moved.reshape(moved.shape[0], moved.shape[1], -1)


def attend_group(group_inputs):
    queries, all_keys, all_values = group_inputs
    factor = queries.shape[-1] ** (-0.5)
    scores = (
        jnp.einsum("sqhd,skhd->shqk", queries, all_keys, preferred_element_type=jnp.float32)
        * factor
    )
    row_max = jnp.max(scores, -1, keepdims=True)
    exponent = jnp.exp(scores - row_max)
    row_total = jnp.sum(exponent, -1, keepdims=True)
    weights = (exponent / row_total).astype(jnp.bfloat16)
    mixed_heads = jnp.einsum(
        "shqk,skhd->sqhd", weights, all_values, preferred_element_type=jnp.float32
    )
    return (mixed_heads, row_max + jnp.log(row_total))


def attend_back(group_inputs):
    queries, all_keys, all_values, d_mixed, log_total = group_inputs
    factor = queries.shape[-1] ** (-0.5)
    scores = (
        jnp.einsum("sqhd,skhd->shqk", queries, all_keys, preferred_element_type=jnp.float32)
        * factor
    )
    probable = jnp.exp(scores - log_total)
    d_values = jnp.einsum(
        "shqk,sqhd->skhd",
        probable.astype(jnp.bfloat16),
        d_mixed,
        preferred_element_type=jnp.float32,
    )
    d_weights = jnp.einsum(
        "sqhd,skhd->shqk", d_mixed, all_values, preferred_element_type=jnp.float32
    )
    inner_sum = jnp.sum(d_weights * probable, -1, keepdims=True)
    d_scores = (probable * (d_weights - inner_sum) * factor).astype(jnp.bfloat16)
    d_queries = jnp.einsum(
        "shqk,skhd->sqhd", d_scores, all_keys, preferred_element_type=jnp.float32
    )
    d_keys = jnp.einsum("shqk,sqhd->skhd", d_scores, queries, preferred_element_type=jnp.float32)
    return (d_queries, d_keys, d_values)


def gelu_tanh(inner_act):
    return jax.nn.gelu(inner_act, approximate=True)


def shards(
    tokens,
    condition,
    adapter,
    cotangent,
    modulation_weight,
    modulation_bias,
    query_key_value_weight,
    attention_out_weight,
    attention_out_bias,
    widen_weight,
    widen_bias,
    narrow_weight,
    narrow_bias,
    lowrank_down,
    lowrank_up,
    first_moment_down,
    first_moment_up,
    second_moment_down,
    second_moment_up,
):
    seq_count_axis = lax.axis_size("seq")
    seq_share = 1.0 / seq_count_axis
    down_portion = lowrank_down.astype(jnp.bfloat16)
    up_portion = lowrank_up.astype(jnp.bfloat16)
    down_edges = (
        0,
        MODEL_WIDTH,
        2 * MODEL_WIDTH,
        3 * MODEL_WIDTH,
        4 * MODEL_WIDTH,
        4 * MODEL_WIDTH + FF,
    )
    up_edges = (
        0,
        6 * MODEL_WIDTH,
        9 * MODEL_WIDTH,
        10 * MODEL_WIDTH,
        10 * MODEL_WIDTH + FF,
        11 * MODEL_WIDTH + FF,
    )

    def fetch():
        across = (
            lax.all_gather(modulation_weight, "seq", axis=1, tiled=True),
            lax.all_gather(query_key_value_weight, "seq", axis=1, tiled=True),
            lax.all_gather(attention_out_weight, "seq", axis=1, tiled=True),
            lax.all_gather(widen_weight, "seq", axis=1, tiled=True),
            lax.all_gather(narrow_weight, "seq", axis=1, tiled=True),
            lax.all_gather(down_portion, "seq", axis=0, tiled=True),
            lax.all_gather(up_portion, "seq", axis=0, tiled=True),
        )
        return (
            lax.all_gather(across[0], "fsdp", axis=0, tiled=True),
            lax.all_gather(across[1], "fsdp", axis=0, tiled=True),
            lax.all_gather(across[2], "fsdp", axis=0, tiled=True),
            lax.all_gather(across[3], "fsdp", axis=0, tiled=True),
            lax.all_gather(across[4], "fsdp", axis=0, tiled=True),
            lax.all_gather(across[5], "fsdp", axis=2, tiled=True),
            lax.all_gather(across[6], "fsdp", axis=2, tiled=True),
        )

    def select(gathered_now, picked_adapter):
        down_sel = gathered_now[5][picked_adapter]
        up_sel = gathered_now[6][picked_adapter]
        down_blocks = [
            down_sel[:, :, down_edges[target] : down_edges[target + 1]] for target in range(5)
        ]
        up_blocks = [up_sel[:, :, up_edges[target] : up_edges[target + 1]] for target in range(5)]
        return (
            gathered_now[0],
            gathered_now[1],
            gathered_now[2],
            gathered_now[3],
            gathered_now[4],
            down_blocks,
            up_blocks,
        )

    down_gradient = jnp.zeros((ADAPTER_COUNT, ADAPTER_RANK, down_edges[5]), jnp.float32)
    up_gradient = jnp.zeros((ADAPTER_COUNT, ADAPTER_RANK, up_edges[5]), jnp.float32)
    output_list, token_list, cond_list = ([], [], [])
    for micro_batch in range(MB):
        first_seq = micro_batch * SEQ_MB
        token_rows = tokens[first_seq : first_seq + SEQ_MB].astype(jnp.float32)
        cond_rows = condition[first_seq : first_seq + SEQ_MB]
        picked_adapter = adapter[first_seq : first_seq + SEQ_MB]
        cot_rows = cotangent[first_seq : first_seq + SEQ_MB].astype(jnp.float32)
        batch_seqs = token_rows.shape[0]
        local_rows = token_rows.shape[1]
        gathered = fetch()
        full_ada, full_qkv, full_proj, full_expand, full_shrink, down_blocks, up_blocks = select(
            gathered, picked_adapter
        )
        cond_act = jax.nn.silu(cond_rows).astype(jnp.bfloat16)[:, None, :]
        middle_ada, extra_ada = adapt_forward(cond_act, down_blocks[0], up_blocks[0])
        modulation = linear(cond_act, full_ada) + modulation_bias + extra_ada
        shift_first, scale_first, gate_first, shift_second, scale_second, gate_second = jnp.split(
            modulation, 6, axis=-1
        )
        normed_first, inverse_first = normalize(token_rows)
        hidden = (normed_first * (1.0 + scale_first) + shift_first).astype(jnp.bfloat16)
        middle_qkv, extra_qkv = adapt_forward(hidden, down_blocks[1], up_blocks[1])
        packed = (linear(hidden, full_qkv) + extra_qkv).astype(jnp.bfloat16)
        head_blocks = packed.reshape(
            batch_seqs, local_rows, 3, seq_count_axis, MODEL_WIDTH // seq_count_axis
        )
        by_heads = lax.all_to_all(head_blocks, "seq", split_axis=3, concat_axis=1, tiled=True)
        query_groups = grouped(by_heads[:, :, 0, 0])
        key_groups = grouped(by_heads[:, :, 1, 0])
        value_groups = grouped(by_heads[:, :, 2, 0])
        mixed_groups, log_total = lax.map(attend_group, (query_groups, key_groups, value_groups))
        mixed = lax.all_to_all(
            ungrouped(mixed_groups).astype(jnp.bfloat16),
            "seq",
            split_axis=1,
            concat_axis=2,
            tiled=True,
        )
        middle_proj, extra_proj = adapt_forward(mixed, down_blocks[2], up_blocks[2])
        branch = linear(mixed, full_proj) + attention_out_bias + extra_proj
        residual = token_rows + gate_first * branch
        normed_second, inverse_second = normalize(residual)
        second = (normed_second * (1.0 + scale_second) + shift_second).astype(jnp.bfloat16)
        middle_expand, extra_expand = adapt_forward(second, down_blocks[3], up_blocks[3])
        inner_act = linear(second, full_expand) + widen_bias + extra_expand
        active = gelu_tanh(inner_act).astype(jnp.bfloat16)
        middle_shrink, extra_shrink = adapt_forward(active, down_blocks[4], up_blocks[4])
        final_out = linear(active, full_shrink) + narrow_bias + extra_shrink
        output_list.append((residual + gate_second * final_out).astype(jnp.bfloat16))
        gathered = fetch()
        full_ada, full_qkv, full_proj, full_expand, full_shrink, down_blocks, up_blocks = select(
            gathered, picked_adapter
        )
        d_final = (gate_second * cot_rows).astype(jnp.bfloat16)
        d_gate_second = jnp.sum(cot_rows * final_out, axis=1, keepdims=True)
        d_active, down_shrink, up_shrink = adapt_backward(
            active, middle_shrink, d_final, down_blocks[4], up_blocks[4]
        )
        d_active = d_active + linear_back(d_final, full_shrink)
        d_inner = jax.vjp(gelu_tanh, inner_act)[1](d_active)[0].astype(jnp.bfloat16)
        d_second, down_expand, up_expand = adapt_backward(
            second, middle_expand, d_inner, down_blocks[3], up_blocks[3]
        )
        d_second = d_second + linear_back(d_inner, full_expand)
        d_shift_second = jnp.sum(d_second, axis=1, keepdims=True)
        d_scale_second = jnp.sum(d_second * normed_second, axis=1, keepdims=True)
        d_residual = cot_rows + normalize_back(
            d_second * (1.0 + scale_second), normed_second, inverse_second
        )
        d_branch = (gate_first * d_residual).astype(jnp.bfloat16)
        d_gate_first = jnp.sum(d_residual * branch, axis=1, keepdims=True)
        d_mixed, down_proj, up_proj = adapt_backward(
            mixed, middle_proj, d_branch, down_blocks[2], up_blocks[2]
        )
        d_mixed = (d_mixed + linear_back(d_branch, full_proj)).astype(jnp.bfloat16)
        d_by_heads = lax.all_to_all(d_mixed, "seq", split_axis=2, concat_axis=1, tiled=True)
        dquery_groups, dkey_groups, dvalue_groups = lax.map(
            attend_back, (query_groups, key_groups, value_groups, grouped(d_by_heads), log_total)
        )
        stacked = jnp.stack(
            [
                ungrouped(dquery_groups).astype(jnp.bfloat16),
                ungrouped(dkey_groups).astype(jnp.bfloat16),
                ungrouped(dvalue_groups).astype(jnp.bfloat16),
            ],
            2,
        )[:, :, :, None, :]
        returned = lax.all_to_all(stacked, "seq", split_axis=1, concat_axis=3, tiled=True)
        d_packed = returned.reshape(batch_seqs, local_rows, 3 * MODEL_WIDTH)
        d_hidden, down_qkv, up_qkv = adapt_backward(
            hidden, middle_qkv, d_packed, down_blocks[1], up_blocks[1]
        )
        d_hidden = d_hidden + linear_back(d_packed, full_qkv)
        d_shift_first = jnp.sum(d_hidden, axis=1, keepdims=True)
        d_scale_first = jnp.sum(d_hidden * normed_first, axis=1, keepdims=True)
        token_list.append(
            d_residual + normalize_back(d_hidden * (1.0 + scale_first), normed_first, inverse_first)
        )
        partial_mod = jnp.concatenate(
            [
                d_shift_first,
                d_scale_first,
                d_gate_first,
                d_shift_second,
                d_scale_second,
                d_gate_second,
            ],
            -1,
        )
        d_modulation = lax.psum(partial_mod, "seq").astype(jnp.bfloat16)
        d_cond_act, down_ada, up_ada = adapt_backward(
            cond_act, middle_ada, d_modulation, down_blocks[0], up_blocks[0]
        )
        d_cond_act = d_cond_act + linear_back(d_modulation, full_ada)
        cond_list.append(jax.vjp(jax.nn.silu, cond_rows)[1](d_cond_act[:, 0, :])[0])
        seq_down = jnp.concatenate(
            [down_ada * seq_share, down_qkv, down_proj, down_expand, down_shrink], -1
        )
        seq_up = jnp.concatenate([up_ada * seq_share, up_qkv, up_proj, up_expand, up_shrink], -1)
        selector = jax.nn.one_hot(picked_adapter, ADAPTER_COUNT, dtype=jnp.float32)
        down_gradient = down_gradient + jnp.einsum(
            "sa,src->arc", selector, seq_down, precision=highest
        )
        up_gradient = up_gradient + jnp.einsum("sa,src->arc", selector, seq_up, precision=highest)
    part_down, part_up = (
        lax.psum_scatter(down_gradient, "fsdp", scatter_dimension=2, tiled=True),
        lax.psum_scatter(up_gradient, "fsdp", scatter_dimension=2, tiled=True),
    )
    sequence_down, sequence_up = (
        lax.psum_scatter(
            part_down.astype(jnp.bfloat16), "seq", scatter_dimension=0, tiled=True
        ).astype(jnp.float32),
        lax.psum_scatter(
            part_up.astype(jnp.bfloat16), "seq", scatter_dimension=0, tiled=True
        ).astype(jnp.float32),
    )
    squared = lax.psum(
        jnp.sum(sequence_down * sequence_down) + jnp.sum(sequence_up * sequence_up), ("fsdp", "seq")
    )
    grad_norm = jnp.sqrt(squared)
    clip_factor = jnp.minimum(1.0, clip_limit / (grad_norm + norm_eps))

    def optimizer_update(params, gradient, moment, square):
        gradient = gradient * clip_factor
        moment_new = beta_first * moment + (1.0 - beta_first) * gradient
        square_new = beta_second * square + (1.0 - beta_second) * gradient * gradient
        direction = (
            moment_new
            / (1.0 - beta_first**STEP)
            / (jnp.sqrt(square_new / (1.0 - beta_second**STEP)) + adam_eps)
        )
        return (params - learn_rate * (direction + decay_rate * params), moment_new, square_new)

    stepped_down, next_first_down, next_second_down = optimizer_update(
        lowrank_down, sequence_down, first_moment_down, second_moment_down
    )
    stepped_up, next_first_up, next_second_up = optimizer_update(
        lowrank_up, sequence_up, first_moment_up, second_moment_up
    )
    block_out = jnp.concatenate(output_list, 0)
    token_grad = jnp.concatenate(token_list, 0)
    cond_grad = jnp.concatenate(cond_list, 0)
    return (
        block_out,
        token_grad,
        cond_grad,
        grad_norm,
        stepped_down,
        stepped_up,
        next_first_down,
        next_first_up,
        next_second_down,
        next_second_up,
    )


HEADS = 16
LOG2E = 1.4426950408889634
SCORE_SCALE = HD ** (-0.5)


def tn(left, right):
    return lax.dot_general(left, right, (((0,), (0,)), ((), ())), preferred_element_type=jnp.float32)


def nn(left, right):
    return lax.dot_general(left, right, (((1,), (0,)), ((), ())), preferred_element_type=jnp.float32)


def nt(left, right):
    return lax.dot_general(left, right, (((1,), (1,)), ((), ())), preferred_element_type=jnp.float32)


def heads_kernel(qkv_ref, mixed_ref, log_ref, *, step):
    length = qkv_ref.shape[-1]
    keys = qkv_ref[1, 0].astype(jnp.float32).T.astype(jnp.bfloat16)
    values_t = qkv_ref[2, 0]
    for start in range(0, length, step):
        queries_t = qkv_ref[0, 0, :, start : start + step]
        scores = nn(keys, queries_t) * (SCORE_SCALE * LOG2E)
        top = jnp.max(scores, axis=0, keepdims=True)
        exponent = jnp.exp2(scores - top)
        total = jnp.sum(exponent, axis=0, keepdims=True)
        weights = (exponent * (1.0 / total)).astype(jnp.bfloat16)
        mixed_ref[0, :, start : start + step] = nn(values_t, weights).astype(jnp.bfloat16)
        log_ref[0, :, start : start + step] = top + jnp.log2(total)


def heads_forward(qkv, step=256):
    _, heads, width, length = qkv.shape
    return pl.pallas_call(
        functools.partial(heads_kernel, step=step),
        grid=(heads,),
        in_specs=[pl.BlockSpec((3, 1, width, length), lambda h: (0, h, 0, 0))],
        out_specs=[
            pl.BlockSpec((1, width, length), lambda h: (h, 0, 0)),
            pl.BlockSpec((1, 1, length), lambda h: (h, 0, 0)),
        ],
        out_shape=[
            jax.ShapeDtypeStruct((heads, width, length), jnp.bfloat16),
            jax.ShapeDtypeStruct((heads, 1, length), jnp.float32),
        ],
        cost_estimate=pl.CostEstimate(
            flops=4 * heads * length * length * 256,
            bytes_accessed=10 * heads * width * length,
            transcendentals=heads * length * length,
        ),
        compiler_params=pltpu.CompilerParams(vmem_limit_bytes=48 * 1024 * 1024),
        name="heads_forward",
    )(qkv)


def heads_back_kernel(qkv_ref, grad_ref, log_ref, out_ref, key_acc, value_acc, *, step):
    length = qkv_ref.shape[-1]
    keys_t = qkv_ref[1, 0]
    keys = keys_t.astype(jnp.float32).T.astype(jnp.bfloat16)
    values = qkv_ref[2, 0].astype(jnp.float32).T.astype(jnp.bfloat16)
    for start in range(0, length, step):
        queries_t = qkv_ref[0, 0, :, start : start + step]
        grad_t = grad_ref[0, :, start : start + step]
        queries = queries_t.astype(jnp.float32).T.astype(jnp.bfloat16)
        grad = grad_t.astype(jnp.float32).T.astype(jnp.bfloat16)
        scores = nn(keys, queries_t) * (SCORE_SCALE * LOG2E)
        probable = jnp.exp2(scores - log_ref[0, :, start : start + step])
        d_weights = nn(values, grad_t)
        inner_sum = jnp.sum(d_weights * probable, axis=0, keepdims=True)
        d_scores = (probable * (d_weights - inner_sum)).astype(jnp.bfloat16)
        d_values = nn(probable.astype(jnp.bfloat16), grad)
        d_keys = nn(d_scores, queries)
        if start == 0:
            value_acc[...] = d_values
            key_acc[...] = d_keys
        else:
            value_acc[...] += d_values
            key_acc[...] += d_keys
        out_ref[0, 0, :, start : start + step] = (nn(keys_t, d_scores) * SCORE_SCALE).astype(
            jnp.bfloat16
        )
    out_ref[1, 0] = (key_acc[...] * SCORE_SCALE).T.astype(jnp.bfloat16)
    out_ref[2, 0] = value_acc[...].T.astype(jnp.bfloat16)


def heads_back(qkv, grad, log_total, step=256):
    _, heads, width, length = qkv.shape
    return pl.pallas_call(
        functools.partial(heads_back_kernel, step=step),
        grid=(heads,),
        in_specs=[
            pl.BlockSpec((3, 1, width, length), lambda h: (0, h, 0, 0)),
            pl.BlockSpec((1, width, length), lambda h: (h, 0, 0)),
            pl.BlockSpec((1, 1, length), lambda h: (h, 0, 0)),
        ],
        out_specs=pl.BlockSpec((3, 1, width, length), lambda h: (0, h, 0, 0)),
        out_shape=jax.ShapeDtypeStruct((3, heads, width, length), jnp.bfloat16),
        scratch_shapes=[
            pltpu.VMEM((length, width), jnp.float32),
            pltpu.VMEM((length, width), jnp.float32),
        ],
        cost_estimate=pl.CostEstimate(
            flops=10 * heads * length * length * 256,
            bytes_accessed=16 * heads * width * length,
            transcendentals=heads * length * length,
        ),
        compiler_params=pltpu.CompilerParams(vmem_limit_bytes=48 * 1024 * 1024),
        name="heads_back",
    )(qkv, grad, log_total)


RANK = ADAPTER_RANK
LANES = 128
PADDED = MODEL_WIDTH + LANES
HALF = MODEL_WIDTH // 2
MIB = 1024 * 1024


def transposed(block):
    return block.astype(jnp.float32).T


def once(shape):
    return pl.BlockSpec(shape, lambda *_: (0,) * len(shape), pipeline_mode=pl.Buffered(1))


def rows_of(shape, axis):
    return pl.BlockSpec(shape, lambda i: tuple(i if a == axis else 0 for a in range(len(shape))))


def standard(stream):
    center = stream - jnp.mean(stream, -1, keepdims=True)
    inverse = lax.rsqrt(jnp.mean(center * center, -1, keepdims=True) + norm_eps)
    return (center * inverse, inverse)


def assemble_kernel(place_ref, near_ref, far_ref, next_near_ref, next_far_ref, out_ref, sems):
    z, x, core, y = (place_ref[i] for i in range(4))
    depth = out_ref.shape[1]
    copies = []
    for side, pair in enumerate(((near_ref, far_ref), (next_near_ref, next_far_ref))):
        source = core if side == 0 else 1 - core
        for stage, ref in enumerate(pair):
            for hop in range(2):
                by_x = jnp.where(source == 0, hop, stage)
                by_y = hop + stage - by_x
                for shift in range(depth):
                    target = out_ref.at[
                        lax.rem(y + by_y, 2),
                        lax.rem(z + depth - shift, depth),
                        lax.rem(x + by_x, 2),
                        source,
                    ]
                    copy = pltpu.make_async_copy(
                        ref.at[hop, shift], target, sems.at[len(copies)]
                    )
                    copy.start()
                    copies.append(copy)
    for copy in copies:
        copy.wait()


def assemble(place, near, far, next_near, next_far):
    _, depth, rows, columns = near.shape
    return pl.pallas_call(
        assemble_kernel,
        in_specs=[pl.BlockSpec(memory_space=pltpu.SMEM)]
        + [pl.BlockSpec(memory_space=pltpu.VMEM)] * 4,
        out_specs=pl.BlockSpec(memory_space=pl.ANY),
        out_shape=jax.ShapeDtypeStruct((2, depth, 2, 2, rows, columns), near.dtype),
        scratch_shapes=[pltpu.SemaphoreType.DMA((8 * depth,))],
        cost_estimate=pl.CostEstimate(
            flops=0, bytes_accessed=16 * near.size, transcendentals=0
        ),
        compiler_params=pltpu.CompilerParams(vmem_limit_bytes=32 * MIB),
        name="assemble",
    )(place, near, far, next_near, next_far)


def entry_kernel(
    token_ref, mod_ref, weight_ref, up_ref, down_ref, hidden_ref, middle_ref, qkv_ref, weight_aug
):
    @pl.when(pl.program_id(0) == 0)
    def _():
        weight_aug[:MODEL_WIDTH, :] = weight_ref[...]
        weight_aug[MODEL_WIDTH:, :] = up_ref[...]

    normed, _ = standard(token_ref[...].astype(jnp.float32))
    hidden = (normed * (1.0 + mod_ref[1:2]) + mod_ref[0:1]).astype(jnp.bfloat16)
    middle = nt(hidden, down_ref[...]).astype(jnp.bfloat16)
    hidden_ref[...] = hidden
    middle_ref[...] = middle
    joined = jnp.concatenate([hidden, middle], 1)
    for part in range(3):
        columns = slice(part * MODEL_WIDTH, (part + 1) * MODEL_WIDTH)
        packed = nn(joined, weight_aug[:, columns])
        qkv_ref[part] = packed.T.reshape(qkv_ref.shape[1:]).astype(jnp.bfloat16)


def entry(tokens, mods, weight, up, down, tile=256):
    length = tokens.shape[0]
    bf16 = jnp.bfloat16
    return pl.pallas_call(
        entry_kernel,
        grid=(length // tile,),
        in_specs=[
            rows_of((tile, MODEL_WIDTH), 0),
            once(mods.shape),
            once((MODEL_WIDTH, 3 * MODEL_WIDTH)),
            once(up.shape),
            once(down.shape),
        ],
        out_specs=[
            rows_of((tile, MODEL_WIDTH), 0),
            rows_of((tile, LANES), 0),
            rows_of((3, HEADS, HD, tile), 3),
        ],
        out_shape=[
            jax.ShapeDtypeStruct((length, MODEL_WIDTH), bf16),
            jax.ShapeDtypeStruct((length, LANES), bf16),
            jax.ShapeDtypeStruct((3, HEADS, HD, length), bf16),
        ],
        scratch_shapes=[pltpu.VMEM((PADDED, 3 * MODEL_WIDTH), bf16)],
        cost_estimate=pl.CostEstimate(
            flops=6 * length * MODEL_WIDTH * PADDED,
            bytes_accessed=6 * MODEL_WIDTH * MODEL_WIDTH + 12 * length * MODEL_WIDTH,
            transcendentals=0,
        ),
        compiler_params=pltpu.CompilerParams(vmem_limit_bytes=56 * MIB),
        name="entry",
    )(tokens, mods, weight, up, down)


def load_proj(proj_aug, weight_ref, up_ref):
    @pl.when(pl.program_id(0) == 0)
    def _():
        proj_aug[:MODEL_WIDTH, :] = weight_ref[...]
        proj_aug[MODEL_WIDTH:, :] = up_ref[...]


def before_kernel(
    mixed_ref,
    token_ref,
    cot_ref,
    mod_ref,
    weight_ref,
    up_proj_ref,
    down_proj_ref,
    down_expand_ref,
    up_shrink_ref,
    bias_ref,
    second_ref,
    dfinal_ref,
    branch_ref,
    middle_ref,
    proj_aug,
):
    bf16 = jnp.bfloat16
    load_proj(proj_aug, weight_ref, up_proj_ref)
    mixed = transposed(mixed_ref[...]).astype(bf16)
    middle_proj = nt(mixed, down_proj_ref[...])
    branch = nn(jnp.concatenate([mixed, middle_proj.astype(bf16)], 1), proj_aug[...])
    branch = branch + bias_ref[...]
    branch_ref[...] = branch
    residual = token_ref[...].astype(jnp.float32) + mod_ref[2:3] * branch
    normed, _ = standard(residual)
    second = (normed * (1.0 + mod_ref[4:5]) + mod_ref[3:4]).astype(bf16)
    middle_expand = nt(second, down_expand_ref[...])
    second_ref[:, :MODEL_WIDTH] = second
    second_ref[:, MODEL_WIDTH:] = middle_expand.astype(bf16)
    d_final = (mod_ref[5:6] * cot_ref[...].astype(jnp.float32)).astype(bf16)
    dmiddle_shrink = nt(d_final, up_shrink_ref[...])
    dfinal_ref[:, :MODEL_WIDTH] = d_final
    dfinal_ref[:, MODEL_WIDTH:] = dmiddle_shrink.astype(bf16)
    middle_ref[0] = middle_proj.T[:RANK].astype(bf16)
    middle_ref[1] = middle_expand.T[:RANK].astype(bf16)
    middle_ref[2] = dmiddle_shrink.T[:RANK].astype(bf16)


def before_feed(
    mixed, tokens, cotangent, mods, weight, up_proj, down_proj, down_expand, up_shrink, bias, tile=256
):
    length = tokens.shape[0]
    bf16 = jnp.bfloat16
    return pl.pallas_call(
        before_kernel,
        grid=(length // tile,),
        in_specs=[
            rows_of((MODEL_WIDTH, tile), 1),
            rows_of((tile, MODEL_WIDTH), 0),
            rows_of((tile, MODEL_WIDTH), 0),
            once(mods.shape),
            pl.BlockSpec(
                (MODEL_WIDTH, MODEL_WIDTH), lambda *_: (0, 3), pipeline_mode=pl.Buffered(1)
            ),
            once(up_proj.shape),
            once(down_proj.shape),
            once(down_expand.shape),
            once(up_shrink.shape),
            once(bias.shape),
        ],
        out_specs=[
            rows_of((tile, PADDED), 0),
            rows_of((tile, PADDED), 0),
            rows_of((tile, MODEL_WIDTH), 0),
            rows_of((3, RANK, tile), 2),
        ],
        out_shape=[
            jax.ShapeDtypeStruct((length, PADDED), bf16),
            jax.ShapeDtypeStruct((length, PADDED), bf16),
            jax.ShapeDtypeStruct((length, MODEL_WIDTH), jnp.float32),
            jax.ShapeDtypeStruct((3, RANK, length), bf16),
        ],
        scratch_shapes=[pltpu.VMEM((PADDED, MODEL_WIDTH), bf16)],
        cost_estimate=pl.CostEstimate(
            flops=4 * length * MODEL_WIDTH * PADDED,
            bytes_accessed=16 * length * MODEL_WIDTH,
            transcendentals=0,
        ),
        compiler_params=pltpu.CompilerParams(vmem_limit_bytes=48 * MIB),
        name="before_feed",
    )(mixed, tokens, cotangent, mods, weight, up_proj, down_proj, down_expand, up_shrink, bias)


GELU_RATE = 0.7978845608
GELU_CUBE = 0.044715


def gelu_pair(inner, d_active):
    square = inner * inner
    tanh = jnp.tanh(inner * (GELU_RATE + (GELU_RATE * GELU_CUBE) * square))
    half = 0.5 + 0.5 * tanh
    slope = half + inner * (half * (1.0 - tanh)) * (
        GELU_RATE + (3.0 * GELU_CUBE * GELU_RATE) * square
    )
    return (inner * half).astype(jnp.bfloat16), (d_active * slope).astype(jnp.bfloat16)


def feed_kernel(
    second_ref, dfinal_ref, middle_ref, left_ref, right_ref, up_ref, down_ref, bias_ref,
    final_in_ref, dsecond_in_ref, final_ref, dsecond_ref, up_grad_ref, down_grad_ref,
    widen_aug, narrow_aug, *, rows, first, sub,
):
    width = MODEL_WIDTH
    chunks = left_ref.shape[-1] // width
    for chunk in range(chunks):
        rows_now = slice(chunk * width, (chunk + 1) * width)
        for side, ref in enumerate((left_ref, right_ref)):
            at = chunk * width + side * HALF
            widen_aug[:width, at : at + HALF] = ref[:, chunk * width : chunk * width + HALF]
            narrow_aug[rows_now, side * HALF : (side + 1) * HALF] = ref[
                :, chunk * width + HALF : (chunk + 1) * width
            ]
    widen_aug[width:, :] = up_ref[...]
    narrow_aug[:, width:] = down_ref[...]
    length = second_ref.shape[0]
    for index in range(chunks * width // sub):
        cols = slice(index * sub, (index + 1) * sub)
        for start in range(0, length, rows):
            at = slice(start, start + rows)
            inner = nn(second_ref[at, :], widen_aug[:, cols]) + bias_ref[:, cols]
            active, d_inner = gelu_pair(inner, nt(dfinal_ref[at, :], narrow_aug[cols, :]))
            final = nn(active, narrow_aug[cols, :])
            dsecond = nt(d_inner, widen_aug[:, cols])
            if index == 0 and first:
                final_ref[at, :] = final
                dsecond_ref[at, :] = dsecond
            elif index == 0:
                final_ref[at, :] = final_in_ref[at, :] + final
                dsecond_ref[at, :] = dsecond_in_ref[at, :] + dsecond
            else:
                final_ref[at, :] += final
                dsecond_ref[at, :] += dsecond
            up_grad = nn(middle_ref[1, :, at], d_inner)
            down_grad = nn(middle_ref[2, :, at], active)
            if start == 0:
                up_grad_ref[:, cols] = up_grad
                down_grad_ref[:, cols] = down_grad
            else:
                up_grad_ref[:, cols] += up_grad
                down_grad_ref[:, cols] += down_grad


def side_of(weight, side, width):
    if weight.ndim == 2:
        return pl.BlockSpec(
            (MODEL_WIDTH, width), lambda *_: (0, 2 + side), pipeline_mode=pl.Buffered(1)
        )
    return pl.BlockSpec(
        (None, MODEL_WIDTH, width), lambda *_: (side, 0, 0), pipeline_mode=pl.Buffered(1)
    )


def feed(second, dfinal, middles, weight, up, down, bias, sums, rows=1024, sub=768):
    length, padded = second.shape
    hidden = 2 * MODEL_WIDTH
    first = sums is None
    if first:
        sums = (jnp.zeros((8, LANES), jnp.float32),) * 2
    return pl.pallas_call(
        functools.partial(feed_kernel, rows=rows, first=first, sub=sub),
        grid=(1,),
        in_specs=[
            once((length, padded)), once((length, padded)), once(middles.shape),
            *(side_of(weight, side, hidden) for side in range(2)),
            once(up.shape), once(down.shape), once(bias.shape),
            once(sums[0].shape), once(sums[1].shape),
        ],
        out_specs=[once((length, padded)), once((length, padded)), once((RANK, hidden)), once((RANK, hidden))],
        out_shape=[
            jax.ShapeDtypeStruct((length, padded), jnp.float32),
            jax.ShapeDtypeStruct((length, padded), jnp.float32),
            jax.ShapeDtypeStruct((RANK, hidden), jnp.float32),
            jax.ShapeDtypeStruct((RANK, hidden), jnp.float32),
        ],
        scratch_shapes=[pltpu.VMEM((padded, hidden), jnp.bfloat16), pltpu.VMEM((hidden, padded), jnp.bfloat16)],
        input_output_aliases={} if first else {8: 0, 9: 1},
        cost_estimate=pl.CostEstimate(
            flops=8 * length * padded * hidden,
            bytes_accessed=4 * MODEL_WIDTH * hidden + 12 * length * padded,
            transcendentals=length * hidden,
        ),
        compiler_params=pltpu.CompilerParams(vmem_limit_bytes=63 * MIB),
        name="feed",
    )(second, dfinal, middles, weight, weight, up, down, bias, *sums)


def back_through(gradient, normed, inverse):
    return inverse * (
        gradient
        - jnp.mean(gradient, -1, keepdims=True)
        - normed * jnp.mean(gradient * normed, -1, keepdims=True)
    )


def total(values):
    return jnp.sum(values, axis=0, keepdims=True)


def after_kernel(
    final_ref,
    dsecond_ref,
    token_ref,
    cot_ref,
    branch_ref,
    second_ref,
    dfinal_ref,
    mixed_ref,
    middle_ref,
    mod_ref,
    weight_ref,
    up_proj_ref,
    down_proj_ref,
    down_expand_ref,
    up_shrink_ref,
    bias_ref,
    block_ref,
    dresidual_ref,
    dmixed_ref,
    sums_ref,
    up_shrink_grad,
    down_expand_grad,
    up_proj_grad,
    down_proj_grad,
    proj_aug,
):
    bf16 = jnp.bfloat16
    load_proj(proj_aug, weight_ref, up_proj_ref)
    cot = cot_ref[...].astype(jnp.float32)
    branch = branch_ref[...]
    residual = token_ref[...].astype(jnp.float32) + mod_ref[2:3] * branch
    normed, inverse = standard(residual)
    middle_shrink = final_ref[:, MODEL_WIDTH:]
    final = final_ref[:, :MODEL_WIDTH] + bias_ref[...]
    final = final + nn(middle_shrink.astype(bf16), up_shrink_ref[...])
    block_ref[...] = (residual + mod_ref[5:6] * final).astype(bf16)
    dmiddle_expand = dsecond_ref[:, MODEL_WIDTH:]
    d_second = dsecond_ref[:, :MODEL_WIDTH] + nn(dmiddle_expand.astype(bf16), down_expand_ref[...])
    d_residual = cot + back_through(d_second * (1.0 + mod_ref[4:5]), normed, inverse)
    dresidual_ref[...] = d_residual
    d_branch = (mod_ref[2:3] * d_residual).astype(bf16)
    joined = nt(d_branch, proj_aug[...])
    dmiddle_proj = joined[:, MODEL_WIDTH:].astype(bf16)
    d_mixed = joined[:, :MODEL_WIDTH] + nn(dmiddle_proj, down_proj_ref[...])
    dmixed_ref[...] = d_mixed.T.astype(bf16)
    sums = jnp.concatenate(
        [
            total(d_residual * branch),
            total(d_second),
            total(d_second * normed),
            total(cot * final),
            jnp.zeros((4, MODEL_WIDTH), jnp.float32),
        ],
        0,
    )
    grads = (
        nn(middle_shrink.T[:RANK].astype(bf16), dfinal_ref[...]),
        nn(dmiddle_expand.T[:RANK].astype(bf16), second_ref[...]),
        nn(middle_ref[0], d_branch),
        nn(mixed_ref[...], dmiddle_proj),
    )
    refs = (up_shrink_grad, down_expand_grad, up_proj_grad, down_proj_grad)

    @pl.when(pl.program_id(0) == 0)
    def _():
        sums_ref[...] = sums
        for ref, grad in zip(refs, grads):
            ref[...] = grad

    @pl.when(pl.program_id(0) > 0)
    def _():
        sums_ref[...] += sums
        for ref, grad in zip(refs, grads):
            ref[...] += grad


def after_feed(
    final,
    dsecond,
    tokens,
    cotangent,
    branch,
    second,
    dfinal,
    mixed,
    middles,
    mods,
    weight,
    up_proj,
    down_proj,
    down_expand,
    up_shrink,
    bias,
    tile=256,
):
    length = tokens.shape[0]
    bf16, f32 = jnp.bfloat16, jnp.float32
    low_rank = jax.ShapeDtypeStruct((RANK, MODEL_WIDTH), f32)
    return pl.pallas_call(
        after_kernel,
        grid=(length // tile,),
        in_specs=[
            rows_of((tile, PADDED), 0),
            rows_of((tile, PADDED), 0),
            rows_of((tile, MODEL_WIDTH), 0),
            rows_of((tile, MODEL_WIDTH), 0),
            rows_of((tile, MODEL_WIDTH), 0),
            rows_of((tile, MODEL_WIDTH), 0),
            rows_of((tile, MODEL_WIDTH), 0),
            rows_of((MODEL_WIDTH, tile), 1),
            rows_of((3, RANK, tile), 2),
            once(mods.shape),
            pl.BlockSpec(
                (MODEL_WIDTH, MODEL_WIDTH), lambda *_: (0, 3), pipeline_mode=pl.Buffered(1)
            ),
            once(up_proj.shape),
            once(down_proj.shape),
            once(down_expand.shape),
            once(up_shrink.shape),
            once(bias.shape),
        ],
        out_specs=[
            rows_of((tile, MODEL_WIDTH), 0),
            rows_of((tile, MODEL_WIDTH), 0),
            rows_of((MODEL_WIDTH, tile), 1),
            once((8, MODEL_WIDTH)),
            once((RANK, MODEL_WIDTH)),
            once((RANK, MODEL_WIDTH)),
            once((RANK, MODEL_WIDTH)),
            once((MODEL_WIDTH, LANES)),
        ],
        out_shape=[
            jax.ShapeDtypeStruct((length, MODEL_WIDTH), bf16),
            jax.ShapeDtypeStruct((length, MODEL_WIDTH), f32),
            jax.ShapeDtypeStruct((MODEL_WIDTH, length), bf16),
            jax.ShapeDtypeStruct((8, MODEL_WIDTH), f32),
            low_rank,
            low_rank,
            low_rank,
            jax.ShapeDtypeStruct((MODEL_WIDTH, LANES), f32),
        ],
        scratch_shapes=[pltpu.VMEM((PADDED, MODEL_WIDTH), bf16)],
        cost_estimate=pl.CostEstimate(
            flops=5 * length * MODEL_WIDTH * PADDED,
            bytes_accessed=32 * length * MODEL_WIDTH,
            transcendentals=0,
        ),
        compiler_params=pltpu.CompilerParams(vmem_limit_bytes=60 * MIB),
        name="after_feed",
    )(
        final,
        dsecond,
        tokens,
        cotangent,
        branch,
        second,
        dfinal,
        mixed,
        middles,
        mods,
        weight,
        up_proj,
        down_proj,
        down_expand,
        up_shrink,
        bias,
    )


def leave_kernel(
    dqkv_ref,
    token_ref,
    dresidual_ref,
    hidden_ref,
    middle_ref,
    mod_ref,
    weight_ref,
    up_ref,
    down_ref,
    token_grad_ref,
    sums_ref,
    up_grad,
    down_grad,
    weight_aug,
):
    bf16 = jnp.bfloat16
    @pl.when(pl.program_id(0) == 0)
    def _():
        weight_aug[:MODEL_WIDTH, :] = weight_ref[...]
        weight_aug[MODEL_WIDTH:, :] = up_ref[...]

    tile = token_ref.shape[0]
    middle_t = transposed(middle_ref[...])[:RANK].astype(bf16)
    joined = jnp.zeros((tile, PADDED), jnp.float32)
    up_grads = []
    for part in range(3):
        columns = slice(part * MODEL_WIDTH, (part + 1) * MODEL_WIDTH)
        packed_t = dqkv_ref[part].astype(jnp.float32).reshape(MODEL_WIDTH, tile)
        packed = packed_t.T.astype(bf16)
        joined = joined + nt(packed, weight_aug[:, columns])
        up_grads.append(nn(middle_t, packed))
    dmiddle = joined[:, MODEL_WIDTH:]
    d_hidden = joined[:, :MODEL_WIDTH] + nn(dmiddle.astype(bf16), down_ref[...])
    normed, inverse = standard(token_ref[...].astype(jnp.float32))
    back = back_through(d_hidden * (1.0 + mod_ref[1:2]), normed, inverse)
    token_grad_ref[...] = (dresidual_ref[...] + back).astype(bf16)
    sums = jnp.concatenate(
        [total(d_hidden), total(d_hidden * normed), jnp.zeros((6, MODEL_WIDTH), jnp.float32)], 0
    )
    down = nn(dmiddle.T[:RANK].astype(bf16), hidden_ref[...])

    @pl.when(pl.program_id(0) == 0)
    def _():
        sums_ref[...] = sums
        down_grad[...] = down
        for part in range(3):
            up_grad[:, part * MODEL_WIDTH : (part + 1) * MODEL_WIDTH] = up_grads[part]

    @pl.when(pl.program_id(0) > 0)
    def _():
        sums_ref[...] += sums
        down_grad[...] += down
        for part in range(3):
            up_grad[:, part * MODEL_WIDTH : (part + 1) * MODEL_WIDTH] += up_grads[part]


def leave(dqkv, tokens, dresidual, hidden, middle, mods, weight, up, down, tile=256):
    length = tokens.shape[0]
    bf16, f32 = jnp.bfloat16, jnp.float32
    return pl.pallas_call(
        leave_kernel,
        grid=(length // tile,),
        in_specs=[
            rows_of((3, HEADS, HD, tile), 3),
            rows_of((tile, MODEL_WIDTH), 0),
            rows_of((tile, MODEL_WIDTH), 0),
            rows_of((tile, MODEL_WIDTH), 0),
            rows_of((tile, LANES), 0),
            once(mods.shape),
            once((MODEL_WIDTH, 3 * MODEL_WIDTH)),
            once(up.shape),
            once(down.shape),
        ],
        out_specs=[
            rows_of((tile, MODEL_WIDTH), 0),
            once((8, MODEL_WIDTH)),
            once((RANK, 3 * MODEL_WIDTH)),
            once((RANK, MODEL_WIDTH)),
        ],
        out_shape=[
            jax.ShapeDtypeStruct((length, MODEL_WIDTH), bf16),
            jax.ShapeDtypeStruct((8, MODEL_WIDTH), f32),
            jax.ShapeDtypeStruct((RANK, 3 * MODEL_WIDTH), f32),
            jax.ShapeDtypeStruct((RANK, MODEL_WIDTH), f32),
        ],
        scratch_shapes=[pltpu.VMEM((PADDED, 3 * MODEL_WIDTH), bf16)],
        cost_estimate=pl.CostEstimate(
            flops=7 * length * MODEL_WIDTH * PADDED,
            bytes_accessed=6 * MODEL_WIDTH * MODEL_WIDTH + 18 * length * MODEL_WIDTH,
            transcendentals=0,
        ),
        compiler_params=pltpu.CompilerParams(vmem_limit_bytes=60 * MIB),
        name="leave",
    )(dqkv, tokens, dresidual, hidden, middle, mods, weight, up, down)


def layout(n_fsdp):
    return [(f // 4, f // 2 % 2, f % 2) for f in range(n_fsdp)]


def moved(n_fsdp, step):
    pairs = []
    for f, (z, x, c) in enumerate(layout(n_fsdp)):
        for y in range(2):
            to_z, to_x, to_c, to_y = step(z, x, c, y)
            pairs.append((2 * f + y, 2 * (4 * to_z + 2 * to_x + to_c) + to_y))
    return pairs


BOTH = ("fsdp", "seq")


def step_z(block, n_fsdp):
    depth = n_fsdp // 4
    by_shift = [block]
    for shift in range(1, depth):
        pairs = moved(n_fsdp, lambda z, x, c, y: ((z + shift) % depth, x, c, y))
        by_shift.append(lax.ppermute(block, BOTH, pairs))
    return jnp.stack(by_shift)


def step_first(block, n_fsdp):
    return lax.ppermute(
        block,
        BOTH,
        moved(n_fsdp, lambda z, x, c, y: (z, x, c, 1 - y) if c else (z, 1 - x, c, y)),
    )


def step_second(block, n_fsdp):
    return lax.ppermute(
        block,
        BOTH,
        moved(n_fsdp, lambda z, x, c, y: (z, 1 - x, c, y) if c else (z, x, c, 1 - y)),
    )


def step_core(block, n_fsdp):
    return lax.ppermute(block, BOTH, moved(n_fsdp, lambda z, x, c, y: (z, x, 1 - c, y)))


def behind(block, *earlier):
    for array in earlier:
        element = lax.slice(array, [n - 1 for n in array.shape], array.shape).reshape(())
        element = element.astype(jnp.float32)
        block = block + jnp.minimum(jnp.abs(element), 0.0).astype(block.dtype)
    return block


def gather_late(block, n_fsdp, place):
    line = step_z(block, n_fsdp)
    near = jnp.stack([line, step_first(line, n_fsdp)])
    far = step_second(near, n_fsdp)
    gathered = assemble(place, near, far, step_core(near, n_fsdp), step_core(far, n_fsdp))
    return gathered.reshape(2, n_fsdp * block.shape[0], block.shape[1])


DOWN_EDGES = (0, 1152, 2304, 3456, 4608, 9216)
UP_EDGES = (0, 6912, 10368, 11520, 16128, 17280)
PIECES = FF // HD


def piece_order(n_fsdp):
    per = PIECES // n_fsdp
    return [f * per + q for q in range(per) for f in range(n_fsdp)]


def unpack_kernel(came_ref, *refs, order, down_chunk, up_chunk):
    bf16 = jnp.bfloat16
    outs, (down_all, up_all, mixed) = refs[:-3], refs[-3:]
    down_outs, up_outs, shrink_t = outs[:4], outs[4:9], outs[9]
    for f in range(came_ref.shape[0]):
        block = came_ref[f].astype(jnp.float32)
        down_all[:, f * down_chunk : (f + 1) * down_chunk] = block[:, :down_chunk]
        up_all[:, f * up_chunk : (f + 1) * up_chunk] = block[:, down_chunk:]
    for target, out in enumerate(down_outs):
        out[...] = jnp.zeros_like(out)
        out[:RANK] = down_all[:, DOWN_EDGES[target] : DOWN_EDGES[target + 1]].astype(bf16)
    mixed[...] = jnp.zeros_like(mixed)
    for target, out in enumerate(up_outs):
        if target == 3:
            for to, piece in enumerate(order):
                at = UP_EDGES[3] + piece * HD
                mixed[:RANK, to * HD : (to + 1) * HD] = up_all[:, at : at + HD]
            out[...] = mixed[...].astype(bf16)
        else:
            out[...] = jnp.zeros_like(out)
            out[:RANK] = up_all[:, UP_EDGES[target] : UP_EDGES[target + 1]].astype(bf16)
    for to, piece in enumerate(order):
        at = DOWN_EDGES[4] + piece * HD
        mixed[:RANK, to * HD : (to + 1) * HD] = down_all[:, at : at + HD]
    for start in range(0, FF, MODEL_WIDTH):
        shrink_t[start : start + MODEL_WIDTH, :] = mixed[:, start : start + MODEL_WIDTH].T.astype(
            bf16
        )


def unpack(came, order, down_chunk, up_chunk):
    bf16 = jnp.bfloat16
    widths = [DOWN_EDGES[t + 1] - DOWN_EDGES[t] for t in range(4)]
    widths += [UP_EDGES[t + 1] - UP_EDGES[t] for t in range(5)]
    return pl.pallas_call(
        functools.partial(
            unpack_kernel, order=order, down_chunk=down_chunk, up_chunk=up_chunk
        ),
        out_shape=[jax.ShapeDtypeStruct((LANES, w), bf16) for w in widths]
        + [jax.ShapeDtypeStruct((FF, LANES), bf16)],
        scratch_shapes=[
            pltpu.VMEM((RANK, DOWN_EDGES[5]), jnp.float32),
            pltpu.VMEM((RANK, UP_EDGES[5]), jnp.float32),
            pltpu.VMEM((LANES, FF), jnp.float32),
        ],
        compiler_params=pltpu.CompilerParams(vmem_limit_bytes=48 * MIB),
        name="unpack",
    )(came)


def pack_kernel(
    leave_ref,
    after_ref,
    middle_ref,
    cond_ref,
    down_ada_ref,
    up_ada_ref,
    down_qkv,
    up_qkv,
    down_proj,
    up_proj,
    down_expand,
    up_expand_low,
    up_expand_high,
    down_shrink_low,
    down_shrink_high,
    up_shrink,
    sent_ref,
    dmod_ref,
    own_ref,
    down_all,
    up_all,
    *,
    order,
    down_chunk,
    up_chunk,
):
    bf16, f32 = jnp.bfloat16, jnp.float32
    width = MODEL_WIDTH
    dmiddle = jnp.zeros((RANK, 1), f32)
    for block in range(6):
        source = leave_ref if block < 2 else after_ref
        line = source[block % 2 if block < 2 else block - 2, :].reshape(1, width)
        line = line.astype(bf16).astype(f32)
        columns = slice(block * width, (block + 1) * width)
        side, at = block // 3, block % 3 * width
        dmod_ref[side : side + 1, at : at + width] = line
        up_all[:, columns] = middle_ref[...] * line
        dmiddle += jnp.sum(up_ada_ref[:RANK, columns].astype(f32) * line, axis=1, keepdims=True)
    dmiddle = dmiddle.astype(bf16).astype(f32)
    down_all[:, :width] = dmiddle * cond_ref[...]
    own_ref[...] = total(dmiddle * down_ada_ref[:RANK].astype(f32))
    down_all[:, width : 2 * width] = down_qkv[...]
    down_all[:, 2 * width : 3 * width] = down_proj[...].T[:RANK]
    down_all[:, 3 * width : 4 * width] = down_expand[...]
    up_all[:, UP_EDGES[1] : UP_EDGES[2]] = up_qkv[...]
    up_all[:, UP_EDGES[2] : UP_EDGES[3]] = up_proj[...]
    up_all[:, UP_EDGES[4] : UP_EDGES[5]] = up_shrink[...]
    half = PIECES // 2
    for at, piece in enumerate(order):
        ups = up_expand_low if at < half else up_expand_high
        downs = down_shrink_low if at < half else down_shrink_high
        columns = slice((at % half) * HD, (at % half + 1) * HD)
        to = UP_EDGES[3] + piece * HD
        up_all[:, to : to + HD] = ups[:, columns]
        to = DOWN_EDGES[4] + piece * HD
        down_all[:, to : to + HD] = downs[:, columns]
    for f in range(sent_ref.shape[0]):
        sent_ref[f, :, :down_chunk] = down_all[:, f * down_chunk : (f + 1) * down_chunk].astype(bf16)
        sent_ref[f, :, down_chunk:] = up_all[:, f * up_chunk : (f + 1) * up_chunk].astype(bf16)


def pack(operands, n_fsdp, order, down_chunk, up_chunk):
    bf16, f32 = jnp.bfloat16, jnp.float32
    return pl.pallas_call(
        functools.partial(pack_kernel, order=order, down_chunk=down_chunk, up_chunk=up_chunk),
        out_shape=[
            jax.ShapeDtypeStruct((n_fsdp, RANK, down_chunk + up_chunk), bf16),
            jax.ShapeDtypeStruct((2, 3 * MODEL_WIDTH), f32),
            jax.ShapeDtypeStruct((1, MODEL_WIDTH), f32),
        ],
        scratch_shapes=[
            pltpu.VMEM((RANK, DOWN_EDGES[5]), f32),
            pltpu.VMEM((RANK, UP_EDGES[5]), f32),
        ],
        compiler_params=pltpu.CompilerParams(vmem_limit_bytes=48 * MIB),
        name="pack",
    )(*operands)


def owners_kernel(ids_ref, place_ref, came_ref, kept_ref, given_ref, sums):
    sums[...] = jnp.zeros_like(sums)
    for f in range(came_ref.shape[0]):
        sums[ids_ref[f]] += came_ref[f].astype(jnp.float32)
    held = kept_ref.shape[0]
    mine = place_ref[3]
    for index in range(held):
        kept_ref[index] = sums[mine * held + index]
        given_ref[index] = sums[(1 - mine) * held + index].astype(jnp.bfloat16)


def owners(ids, place, came):
    held = ADAPTER_COUNT // 2
    shape = (held,) + came.shape[1:]
    return pl.pallas_call(
        owners_kernel,
        in_specs=[
            pl.BlockSpec(memory_space=pltpu.SMEM),
            pl.BlockSpec(memory_space=pltpu.SMEM),
            pl.BlockSpec(memory_space=pltpu.VMEM),
        ],
        out_shape=[
            jax.ShapeDtypeStruct(shape, jnp.float32),
            jax.ShapeDtypeStruct(shape, jnp.bfloat16),
        ],
        scratch_shapes=[pltpu.VMEM((ADAPTER_COUNT,) + came.shape[1:], jnp.float32)],
        compiler_params=pltpu.CompilerParams(vmem_limit_bytes=32 * MIB),
        name="owners",
    )(ids, place, came)


def update_kernel(gradient_ref, squared_ref, *refs):
    down_chunk = refs[0].shape[-1]
    grad_norm = jnp.sqrt(jnp.sum(squared_ref[:, :1], axis=0, keepdims=True))
    clip_factor = jnp.minimum(1.0, clip_limit / (grad_norm + norm_eps))
    ins, outs, norm_ref = refs[:6], refs[6:12], refs[12]
    norm_ref[...] = jnp.broadcast_to(grad_norm, norm_ref.shape)
    for kind in range(2):
        part = slice(0, down_chunk) if kind == 0 else slice(down_chunk, None)
        for index in range(gradient_ref.shape[0]):
            gradient = gradient_ref[index, :, part] * clip_factor
            params = ins[kind][index]
            moment_new = beta_first * ins[2 + kind][index] + (1.0 - beta_first) * gradient
            square_new = (
                beta_second * ins[4 + kind][index] + (1.0 - beta_second) * gradient * gradient
            )
            direction = (
                moment_new
                / (1.0 - beta_first**STEP)
                / (jnp.sqrt(square_new / (1.0 - beta_second**STEP)) + adam_eps)
            )
            outs[kind][index] = params - learn_rate * (direction + decay_rate * params)
            outs[2 + kind][index] = moment_new
            outs[4 + kind][index] = square_new


def update(gradient, squared, states):
    f32 = jnp.float32
    outs = pl.pallas_call(
        update_kernel,
        out_shape=[jax.ShapeDtypeStruct(s.shape, f32) for s in states]
        + [jax.ShapeDtypeStruct((8, LANES), f32)],
        compiler_params=pltpu.CompilerParams(vmem_limit_bytes=32 * MIB),
        name="update",
    )(gradient, squared, *states)
    return outs[:6], outs[6][0, 0]


def fits(mesh):
    return mesh.shape["seq"] == MB and mesh.shape["fsdp"] == 16


def dot(equation, left, right):
    return jnp.einsum(equation, left, right, preferred_element_type=jnp.float32)


def swap(block):
    return lax.ppermute(block, "seq", [(0, 1), (1, 0)])


def by_seq(own, other, mine):
    first = mine == 0
    return jnp.stack([jnp.where(first, own, other), jnp.where(first, other, own)])


def swap_rows(halves, mine):
    kept, came = send_row(halves, mine)
    return by_seq(kept, came, mine)


def send_row(halves, mine):
    sent = lax.dynamic_index_in_dim(halves, 1 - mine, 0, False)
    return lax.dynamic_index_in_dim(halves, mine, 0, False), swap(sent)


def to_all(block):
    return lax.all_to_all(block, ("fsdp", "seq"), split_axis=0, concat_axis=0, tiled=True)


def to_fsdp(block):
    return lax.all_to_all(block, "fsdp", split_axis=0, concat_axis=0, tiled=True)


def fast_shards(
    tokens,
    condition,
    adapter,
    cotangent,
    modulation_weight,
    modulation_bias,
    query_key_value_weight,
    attention_out_weight,
    attention_out_bias,
    widen_weight,
    widen_bias,
    narrow_weight,
    narrow_bias,
    lowrank_down,
    lowrank_up,
    first_moment_down,
    first_moment_up,
    second_moment_down,
    second_moment_up,
):
    bf16 = jnp.bfloat16
    n_fsdp = lax.axis_size("fsdp")
    mine = lax.axis_index("seq")
    row = lax.axis_index("fsdp")
    place = jnp.stack([row // 4, row // 2 % 2, row % 2, mine]).astype(jnp.int32)
    down_chunk, up_chunk = lowrank_down.shape[-1], lowrank_up.shape[-1]
    depth = modulation_weight.shape[0]
    order = piece_order(n_fsdp)
    per = PIECES // n_fsdp

    cond_act_pair = jax.nn.silu(condition).astype(bf16)
    told = jnp.moveaxis(cond_act_pair.reshape(MB, n_fsdp, depth), 1, 0)
    numbers = jnp.broadcast_to(adapter.astype(bf16)[None, :, None], (n_fsdp, MB, 8))
    told = to_fsdp(jnp.concatenate([told, numbers], 2))
    own_ids = lax.dynamic_index_in_dim(told[:, :, depth], mine, 1, False).astype(jnp.int32)

    wide = jnp.moveaxis(widen_weight.reshape(depth, -1, per, HD), 2, 0).reshape(per, depth, HALF)
    narrow = narrow_weight.reshape(per, depth, HALF)
    joined = [jnp.concatenate([wide[q], narrow[q]], 1) for q in range(per)]
    early = jnp.concatenate(
        [query_key_value_weight, attention_out_weight, *joined[: per // 2]], 1
    )
    early = by_seq(early, swap(early), mine)
    edges = (0, 3 * HALF, 4 * HALF, early.shape[2])
    early_weight = lax.all_gather(
        jnp.concatenate(
            [early[side, :, edges[i] : edges[i + 1]] for i in range(3) for side in range(2)], 1
        ),
        "fsdp",
        axis=0,
        tiled=True,
    )
    high_weight = gather_late(jnp.concatenate(joined[per // 2 :], 1), n_fsdp, place)

    portions = jnp.concatenate([lowrank_down.astype(bf16), lowrank_up.astype(bf16)], -1)
    others = swap(portions)
    table = by_seq(portions, others, mine).reshape(ADAPTER_COUNT, RANK, -1)
    picks = jax.nn.one_hot(own_ids, ADAPTER_COUNT, dtype=bf16)
    chosen = dot("fa,arc->frc", picks, table).astype(bf16)
    parts = unpack(to_fsdp(chosen), order, down_chunk, up_chunk)
    down_ada, down_qkv, down_proj, down_expand = parts[:4]
    up_ada, up_qkv, up_proj, up_expand, up_shrink = parts[4:9]
    down_shrink_t = parts[9]

    spoken = told[:, :, :depth].reshape(n_fsdp * MB, depth)
    mod_part = to_all(dot("si,io->so", spoken, modulation_weight))
    mod_base = jnp.sum(mod_part.reshape(n_fsdp, MB, -1), axis=0).reshape(1, -1)

    cond_act = lax.dynamic_slice_in_dim(cond_act_pair, mine, 1, 0)
    middle_ada = dot("ti,ri->tr", cond_act, down_ada).astype(bf16)
    modulation = mod_base + modulation_bias + dot("tr,ro->to", middle_ada, up_ada)
    mods = jnp.pad(modulation.reshape(6, MODEL_WIDTH), ((0, 2), (0, 0)))

    length = MB * tokens.shape[1]
    token_rows = swap_rows(tokens, mine).reshape(length, MODEL_WIDTH)
    cot_rows = swap_rows(cotangent, mine).reshape(length, MODEL_WIDTH)

    hidden, middle_qkv, qkv = entry(token_rows, mods, early_weight, up_qkv, down_qkv)
    mixed_heads, log_total = heads_forward(qkv, step=length)
    mixed = mixed_heads.reshape(MODEL_WIDTH, length)
    second, dfinal, branch, middles = before_feed(
        mixed,
        token_rows,
        cot_rows,
        mods,
        early_weight,
        up_proj,
        down_proj,
        down_expand,
        up_shrink,
        attention_out_bias[None],
    )
    bias = jnp.moveaxis(widen_bias.reshape(n_fsdp, per, HD), 0, 1).reshape(1, FF)
    cut = FF // 2
    final, dsecond, up_expand_low, down_shrink_low = feed(
        second,
        dfinal,
        middles,
        early_weight,
        up_expand[:, :cut],
        down_shrink_t[:cut],
        bias[:, :cut],
        None,
    )
    final, dsecond, up_expand_high, down_shrink_high = feed(
        second,
        dfinal,
        middles,
        high_weight,
        up_expand[:, cut:],
        down_shrink_t[cut:],
        bias[:, cut:],
        (final, dsecond),
    )
    (
        block_rows,
        d_residual,
        d_mixed,
        after_sums,
        up_shrink_grad,
        down_expand_grad,
        up_proj_grad,
        down_proj_grad,
    ) = after_feed(
        final,
        dsecond,
        token_rows,
        cot_rows,
        branch,
        second,
        dfinal,
        mixed,
        middles,
        mods,
        early_weight,
        up_proj,
        down_proj,
        down_expand,
        up_shrink,
        narrow_bias[None],
    )
    block_out = swap_rows(block_rows.reshape(tokens.shape), mine)
    d_qkv = heads_back(qkv, d_mixed.reshape(HEADS, HD, length), log_total, step=length // 2)
    token_rows_grad, leave_sums, up_qkv_grad, down_qkv_grad = leave(
        d_qkv, token_rows, d_residual, hidden, middle_qkv, mods, early_weight, up_qkv, down_qkv
    )

    sent, d_modulation, own_cond = pack(
        (
            leave_sums,
            after_sums,
            middle_ada[:, :RANK].astype(jnp.float32).T,
            cond_act.astype(jnp.float32),
            down_ada,
            up_ada,
            down_qkv_grad,
            up_qkv_grad,
            down_proj_grad,
            up_proj_grad,
            down_expand_grad,
            up_expand_low,
            up_expand_high,
            down_shrink_low,
            down_shrink_high,
            up_shrink_grad,
        ),
        n_fsdp,
        order,
        down_chunk,
        up_chunk,
    )
    kept, given = owners(own_ids, place, to_fsdp(sent))
    gradient = kept + swap(given).astype(jnp.float32)
    squared = to_all(jnp.broadcast_to(jnp.sum(gradient * gradient), (n_fsdp * MB, LANES)))

    half_weight = lax.all_gather(
        behind(modulation_weight, second), "fsdp", axis=0, tiled=True
    )
    both_mod = behind(swap_rows(d_modulation.astype(bf16), mine), kept)
    d_cond = dot("so,io->si", both_mod, half_weight)
    d_cond = d_cond + jnp.where(jnp.arange(MB)[:, None] == mine, own_cond, 0.0)
    d_cond = d_cond + swap(d_cond)
    cond_grad = jax.vjp(jax.nn.silu, condition)[1](d_cond)[0]
    token_kept, token_came = send_row(token_rows_grad.reshape(tokens.shape), mine)
    token_grad = by_seq(behind(token_kept, gradient), token_came, mine).astype(jnp.float32)

    states = (
        lowrank_down,
        lowrank_up,
        first_moment_down,
        first_moment_up,
        second_moment_down,
        second_moment_up,
    )
    fresh, grad_norm = update(gradient, squared, states)
    return (block_out, token_grad, cond_grad, grad_norm, *fresh)


def solution(mesh):
    in_specs = (
        P("fsdp", "seq", None),
        P("fsdp", None),
        P("fsdp"),
        P("fsdp", "seq", None),
        P("fsdp", "seq"),
        P(),
        P("fsdp", "seq"),
        P("fsdp", "seq"),
        P(),
        P("fsdp", "seq"),
        P(),
        P("fsdp", "seq"),
        P(),
        P("seq", None, "fsdp"),
        P("seq", None, "fsdp"),
        P("seq", None, "fsdp"),
        P("seq", None, "fsdp"),
        P("seq", None, "fsdp"),
        P("seq", None, "fsdp"),
    )
    out_specs = (
        P("fsdp", "seq", None),
        P("fsdp", "seq", None),
        P("fsdp", None),
        P(),
        P("seq", None, "fsdp"),
        P("seq", None, "fsdp"),
        P("seq", None, "fsdp"),
        P("seq", None, "fsdp"),
        P("seq", None, "fsdp"),
        P("seq", None, "fsdp"),
    )
    body = fast_shards if fits(mesh) else shards
    return jax.shard_map(body, mesh=mesh, in_specs=in_specs, out_specs=out_specs, check_vma=False)
```

```python
import functools

import jax
import jax.numpy as jnp
from jax import lax
from jax.experimental import pallas as pl
from jax.experimental.pallas import tpu as pltpu
from jax.sharding import PartitionSpec as P

MODEL_WIDTH = 1152
HD = 72
FF = 4608
ADAPTER_RANK = 16
ADAPTER_COUNT = 8
MB = 2
SEQ_MB = 1
STEP = 10


beta_first = 0.9
beta_second = 0.999
learn_rate = 0.05
decay_rate = 0.1
adam_eps = 1e-08
clip_limit = 1.0
norm_eps = 1e-06
pair_heads = 2
highest = lax.Precision.HIGHEST


def linear(inputs, weight):
    return jnp.einsum("sti,io->sto", inputs, weight, preferred_element_type=jnp.float32)


def linear_back(gradient, weight):
    return jnp.einsum("sto,io->sti", gradient, weight, preferred_element_type=jnp.float32)


def normalize(stream):
    center = stream - jnp.mean(stream, -1, keepdims=True)
    inverse = lax.rsqrt(jnp.mean(center * center, -1, keepdims=True) + norm_eps)
    return (center * inverse, inverse)


def normalize_back(gradient, normed, inverse):
    return inverse * (
        gradient
        - jnp.mean(gradient, -1, keepdims=True)
        - normed * jnp.mean(gradient * normed, -1, keepdims=True)
    )


def adapt_forward(inputs, down_part, up_part):
    middle = jnp.einsum(
        "sti,sri->str", inputs, down_part, preferred_element_type=jnp.float32
    ).astype(jnp.bfloat16)
    return (middle, jnp.einsum("str,sro->sto", middle, up_part, preferred_element_type=jnp.float32))


def adapt_backward(inputs, middle, gradient, down_part, up_part):
    up_grad = jnp.einsum("str,sto->sro", middle, gradient, preferred_element_type=jnp.float32)
    middle_grad = jnp.einsum(
        "sto,sro->str", gradient, up_part, preferred_element_type=jnp.float32
    ).astype(jnp.bfloat16)
    down_grad = jnp.einsum("str,sti->sri", middle_grad, inputs, preferred_element_type=jnp.float32)
    input_grad = jnp.einsum(
        "str,sri->sti", middle_grad, down_part, preferred_element_type=jnp.float32
    )
    return (input_grad, down_grad, up_grad)


def grouped(matrix):
    seq_count, row_count, col_count = matrix.shape
    return jnp.moveaxis(
        matrix.reshape(seq_count, row_count, col_count // (pair_heads * HD), pair_heads, HD), 2, 0
    )


def ungrouped(stacked):
    moved = jnp.moveaxis(stacked, 0, 2)
    return moved.reshape(moved.shape[0], moved.shape[1], -1)


def attend_group(group_inputs):
    queries, all_keys, all_values = group_inputs
    factor = queries.shape[-1] ** (-0.5)
    scores = (
        jnp.einsum("sqhd,skhd->shqk", queries, all_keys, preferred_element_type=jnp.float32)
        * factor
    )
    row_max = jnp.max(scores, -1, keepdims=True)
    exponent = jnp.exp(scores - row_max)
    row_total = jnp.sum(exponent, -1, keepdims=True)
    weights = (exponent / row_total).astype(jnp.bfloat16)
    mixed_heads = jnp.einsum(
        "shqk,skhd->sqhd", weights, all_values, preferred_element_type=jnp.float32
    )
    return (mixed_heads, row_max + jnp.log(row_total))


def attend_back(group_inputs):
    queries, all_keys, all_values, d_mixed, log_total = group_inputs
    factor = queries.shape[-1] ** (-0.5)
    scores = (
        jnp.einsum("sqhd,skhd->shqk", queries, all_keys, preferred_element_type=jnp.float32)
        * factor
    )
    probable = jnp.exp(scores - log_total)
    d_values = jnp.einsum(
        "shqk,sqhd->skhd",
        probable.astype(jnp.bfloat16),
        d_mixed,
        preferred_element_type=jnp.float32,
    )
    d_weights = jnp.einsum(
        "sqhd,skhd->shqk", d_mixed, all_values, preferred_element_type=jnp.float32
    )
    inner_sum = jnp.sum(d_weights * probable, -1, keepdims=True)
    d_scores = (probable * (d_weights - inner_sum) * factor).astype(jnp.bfloat16)
    d_queries = jnp.einsum(
        "shqk,skhd->sqhd", d_scores, all_keys, preferred_element_type=jnp.float32
    )
    d_keys = jnp.einsum("shqk,sqhd->skhd", d_scores, queries, preferred_element_type=jnp.float32)
    return (d_queries, d_keys, d_values)


def gelu_tanh(inner_act):
    return jax.nn.gelu(inner_act, approximate=True)


def shards(
    tokens,
    condition,
    adapter,
    cotangent,
    modulation_weight,
    modulation_bias,
    query_key_value_weight,
    attention_out_weight,
    attention_out_bias,
    widen_weight,
    widen_bias,
    narrow_weight,
    narrow_bias,
    lowrank_down,
    lowrank_up,
    first_moment_down,
    first_moment_up,
    second_moment_down,
    second_moment_up,
):
    seq_count_axis = lax.axis_size("seq")
    seq_share = 1.0 / seq_count_axis
    down_portion = lowrank_down.astype(jnp.bfloat16)
    up_portion = lowrank_up.astype(jnp.bfloat16)
    down_edges = (
        0,
        MODEL_WIDTH,
        2 * MODEL_WIDTH,
        3 * MODEL_WIDTH,
        4 * MODEL_WIDTH,
        4 * MODEL_WIDTH + FF,
    )
    up_edges = (
        0,
        6 * MODEL_WIDTH,
        9 * MODEL_WIDTH,
        10 * MODEL_WIDTH,
        10 * MODEL_WIDTH + FF,
        11 * MODEL_WIDTH + FF,
    )

    def fetch():
        across = (
            lax.all_gather(modulation_weight, "seq", axis=1, tiled=True),
            lax.all_gather(query_key_value_weight, "seq", axis=1, tiled=True),
            lax.all_gather(attention_out_weight, "seq", axis=1, tiled=True),
            lax.all_gather(widen_weight, "seq", axis=1, tiled=True),
            lax.all_gather(narrow_weight, "seq", axis=1, tiled=True),
            lax.all_gather(down_portion, "seq", axis=0, tiled=True),
            lax.all_gather(up_portion, "seq", axis=0, tiled=True),
        )
        return (
            lax.all_gather(across[0], "fsdp", axis=0, tiled=True),
            lax.all_gather(across[1], "fsdp", axis=0, tiled=True),
            lax.all_gather(across[2], "fsdp", axis=0, tiled=True),
            lax.all_gather(across[3], "fsdp", axis=0, tiled=True),
            lax.all_gather(across[4], "fsdp", axis=0, tiled=True),
            lax.all_gather(across[5], "fsdp", axis=2, tiled=True),
            lax.all_gather(across[6], "fsdp", axis=2, tiled=True),
        )

    def select(gathered_now, picked_adapter):
        down_sel = gathered_now[5][picked_adapter]
        up_sel = gathered_now[6][picked_adapter]
        down_blocks = [
            down_sel[:, :, down_edges[target] : down_edges[target + 1]] for target in range(5)
        ]
        up_blocks = [up_sel[:, :, up_edges[target] : up_edges[target + 1]] for target in range(5)]
        return (
            gathered_now[0],
            gathered_now[1],
            gathered_now[2],
            gathered_now[3],
            gathered_now[4],
            down_blocks,
            up_blocks,
        )

    down_gradient = jnp.zeros((ADAPTER_COUNT, ADAPTER_RANK, down_edges[5]), jnp.float32)
    up_gradient = jnp.zeros((ADAPTER_COUNT, ADAPTER_RANK, up_edges[5]), jnp.float32)
    output_list, token_list, cond_list = ([], [], [])
    for micro_batch in range(MB):
        first_seq = micro_batch * SEQ_MB
        token_rows = tokens[first_seq : first_seq + SEQ_MB].astype(jnp.float32)
        cond_rows = condition[first_seq : first_seq + SEQ_MB]
        picked_adapter = adapter[first_seq : first_seq + SEQ_MB]
        cot_rows = cotangent[first_seq : first_seq + SEQ_MB].astype(jnp.float32)
        batch_seqs = token_rows.shape[0]
        local_rows = token_rows.shape[1]
        gathered = fetch()
        full_ada, full_qkv, full_proj, full_expand, full_shrink, down_blocks, up_blocks = select(
            gathered, picked_adapter
        )
        cond_act = jax.nn.silu(cond_rows).astype(jnp.bfloat16)[:, None, :]
        middle_ada, extra_ada = adapt_forward(cond_act, down_blocks[0], up_blocks[0])
        modulation = linear(cond_act, full_ada) + modulation_bias + extra_ada
        shift_first, scale_first, gate_first, shift_second, scale_second, gate_second = jnp.split(
            modulation, 6, axis=-1
        )
        normed_first, inverse_first = normalize(token_rows)
        hidden = (normed_first * (1.0 + scale_first) + shift_first).astype(jnp.bfloat16)
        middle_qkv, extra_qkv = adapt_forward(hidden, down_blocks[1], up_blocks[1])
        packed = (linear(hidden, full_qkv) + extra_qkv).astype(jnp.bfloat16)
        head_blocks = packed.reshape(
            batch_seqs, local_rows, 3, seq_count_axis, MODEL_WIDTH // seq_count_axis
        )
        by_heads = lax.all_to_all(head_blocks, "seq", split_axis=3, concat_axis=1, tiled=True)
        query_groups = grouped(by_heads[:, :, 0, 0])
        key_groups = grouped(by_heads[:, :, 1, 0])
        value_groups = grouped(by_heads[:, :, 2, 0])
        mixed_groups, log_total = lax.map(attend_group, (query_groups, key_groups, value_groups))
        mixed = lax.all_to_all(
            ungrouped(mixed_groups).astype(jnp.bfloat16),
            "seq",
            split_axis=1,
            concat_axis=2,
            tiled=True,
        )
        middle_proj, extra_proj = adapt_forward(mixed, down_blocks[2], up_blocks[2])
        branch = linear(mixed, full_proj) + attention_out_bias + extra_proj
        residual = token_rows + gate_first * branch
        normed_second, inverse_second = normalize(residual)
        second = (normed_second * (1.0 + scale_second) + shift_second).astype(jnp.bfloat16)
        middle_expand, extra_expand = adapt_forward(second, down_blocks[3], up_blocks[3])
        inner_act = linear(second, full_expand) + widen_bias + extra_expand
        active = gelu_tanh(inner_act).astype(jnp.bfloat16)
        middle_shrink, extra_shrink = adapt_forward(active, down_blocks[4], up_blocks[4])
        final_out = linear(active, full_shrink) + narrow_bias + extra_shrink
        output_list.append((residual + gate_second * final_out).astype(jnp.bfloat16))
        gathered = fetch()
        full_ada, full_qkv, full_proj, full_expand, full_shrink, down_blocks, up_blocks = select(
            gathered, picked_adapter
        )
        d_final = (gate_second * cot_rows).astype(jnp.bfloat16)
        d_gate_second = jnp.sum(cot_rows * final_out, axis=1, keepdims=True)
        d_active, down_shrink, up_shrink = adapt_backward(
            active, middle_shrink, d_final, down_blocks[4], up_blocks[4]
        )
        d_active = d_active + linear_back(d_final, full_shrink)
        d_inner = jax.vjp(gelu_tanh, inner_act)[1](d_active)[0].astype(jnp.bfloat16)
        d_second, down_expand, up_expand = adapt_backward(
            second, middle_expand, d_inner, down_blocks[3], up_blocks[3]
        )
        d_second = d_second + linear_back(d_inner, full_expand)
        d_shift_second = jnp.sum(d_second, axis=1, keepdims=True)
        d_scale_second = jnp.sum(d_second * normed_second, axis=1, keepdims=True)
        d_residual = cot_rows + normalize_back(
            d_second * (1.0 + scale_second), normed_second, inverse_second
        )
        d_branch = (gate_first * d_residual).astype(jnp.bfloat16)
        d_gate_first = jnp.sum(d_residual * branch, axis=1, keepdims=True)
        d_mixed, down_proj, up_proj = adapt_backward(
            mixed, middle_proj, d_branch, down_blocks[2], up_blocks[2]
        )
        d_mixed = (d_mixed + linear_back(d_branch, full_proj)).astype(jnp.bfloat16)
        d_by_heads = lax.all_to_all(d_mixed, "seq", split_axis=2, concat_axis=1, tiled=True)
        dquery_groups, dkey_groups, dvalue_groups = lax.map(
            attend_back, (query_groups, key_groups, value_groups, grouped(d_by_heads), log_total)
        )
        stacked = jnp.stack(
            [
                ungrouped(dquery_groups).astype(jnp.bfloat16),
                ungrouped(dkey_groups).astype(jnp.bfloat16),
                ungrouped(dvalue_groups).astype(jnp.bfloat16),
            ],
            2,
        )[:, :, :, None, :]
        returned = lax.all_to_all(stacked, "seq", split_axis=1, concat_axis=3, tiled=True)
        d_packed = returned.reshape(batch_seqs, local_rows, 3 * MODEL_WIDTH)
        d_hidden, down_qkv, up_qkv = adapt_backward(
            hidden, middle_qkv, d_packed, down_blocks[1], up_blocks[1]
        )
        d_hidden = d_hidden + linear_back(d_packed, full_qkv)
        d_shift_first = jnp.sum(d_hidden, axis=1, keepdims=True)
        d_scale_first = jnp.sum(d_hidden * normed_first, axis=1, keepdims=True)
        token_list.append(
            d_residual + normalize_back(d_hidden * (1.0 + scale_first), normed_first, inverse_first)
        )
        partial_mod = jnp.concatenate(
            [
                d_shift_first,
                d_scale_first,
                d_gate_first,
                d_shift_second,
                d_scale_second,
                d_gate_second,
            ],
            -1,
        )
        d_modulation = lax.psum(partial_mod, "seq").astype(jnp.bfloat16)
        d_cond_act, down_ada, up_ada = adapt_backward(
            cond_act, middle_ada, d_modulation, down_blocks[0], up_blocks[0]
        )
        d_cond_act = d_cond_act + linear_back(d_modulation, full_ada)
        cond_list.append(jax.vjp(jax.nn.silu, cond_rows)[1](d_cond_act[:, 0, :])[0])
        seq_down = jnp.concatenate(
            [down_ada * seq_share, down_qkv, down_proj, down_expand, down_shrink], -1
        )
        seq_up = jnp.concatenate([up_ada * seq_share, up_qkv, up_proj, up_expand, up_shrink], -1)
        selector = jax.nn.one_hot(picked_adapter, ADAPTER_COUNT, dtype=jnp.float32)
        down_gradient = down_gradient + jnp.einsum(
            "sa,src->arc", selector, seq_down, precision=highest
        )
        up_gradient = up_gradient + jnp.einsum("sa,src->arc", selector, seq_up, precision=highest)
    part_down, part_up = (
        lax.psum_scatter(down_gradient, "fsdp", scatter_dimension=2, tiled=True),
        lax.psum_scatter(up_gradient, "fsdp", scatter_dimension=2, tiled=True),
    )
    sequence_down, sequence_up = (
        lax.psum_scatter(
            part_down.astype(jnp.bfloat16), "seq", scatter_dimension=0, tiled=True
        ).astype(jnp.float32),
        lax.psum_scatter(
            part_up.astype(jnp.bfloat16), "seq", scatter_dimension=0, tiled=True
        ).astype(jnp.float32),
    )
    squared = lax.psum(
        jnp.sum(sequence_down * sequence_down) + jnp.sum(sequence_up * sequence_up), ("fsdp", "seq")
    )
    grad_norm = jnp.sqrt(squared)
    clip_factor = jnp.minimum(1.0, clip_limit / (grad_norm + norm_eps))

    def optimizer_update(params, gradient, moment, square):
        gradient = gradient * clip_factor
        moment_new = beta_first * moment + (1.0 - beta_first) * gradient
        square_new = beta_second * square + (1.0 - beta_second) * gradient * gradient
        direction = (
            moment_new
            / (1.0 - beta_first**STEP)
            / (jnp.sqrt(square_new / (1.0 - beta_second**STEP)) + adam_eps)
        )
        return (params - learn_rate * (direction + decay_rate * params), moment_new, square_new)

    stepped_down, next_first_down, next_second_down = optimizer_update(
        lowrank_down, sequence_down, first_moment_down, second_moment_down
    )
    stepped_up, next_first_up, next_second_up = optimizer_update(
        lowrank_up, sequence_up, first_moment_up, second_moment_up
    )
    block_out = jnp.concatenate(output_list, 0)
    token_grad = jnp.concatenate(token_list, 0)
    cond_grad = jnp.concatenate(cond_list, 0)
    return (
        block_out,
        token_grad,
        cond_grad,
        grad_norm,
        stepped_down,
        stepped_up,
        next_first_down,
        next_first_up,
        next_second_down,
        next_second_up,
    )


HEADS = 16
LOG2E = 1.4426950408889634
SCORE_SCALE = HD ** (-0.5)


def tn(left, right):
    return lax.dot_general(left, right, (((0,), (0,)), ((), ())), preferred_element_type=jnp.float32)


def nn(left, right):
    return lax.dot_general(left, right, (((1,), (0,)), ((), ())), preferred_element_type=jnp.float32)


def nt(left, right):
    return lax.dot_general(left, right, (((1,), (1,)), ((), ())), preferred_element_type=jnp.float32)


def heads_kernel(qkv_ref, mixed_ref, log_ref, *, step):
    length = qkv_ref.shape[-1]
    keys = qkv_ref[1, 0].astype(jnp.float32).T.astype(jnp.bfloat16)
    values_t = qkv_ref[2, 0]
    for start in range(0, length, step):
        queries_t = qkv_ref[0, 0, :, start : start + step]
        scores = nn(keys, queries_t) * (SCORE_SCALE * LOG2E)
        top = jnp.max(scores, axis=0, keepdims=True)
        exponent = jnp.exp2(scores - top)
        total = jnp.sum(exponent, axis=0, keepdims=True)
        weights = (exponent * (1.0 / total)).astype(jnp.bfloat16)
        mixed_ref[0, :, start : start + step] = nn(values_t, weights).astype(jnp.bfloat16)
        log_ref[0, :, start : start + step] = top + jnp.log2(total)


def heads_forward(qkv, step=256):
    _, heads, width, length = qkv.shape
    return pl.pallas_call(
        functools.partial(heads_kernel, step=step),
        grid=(heads,),
        in_specs=[pl.BlockSpec((3, 1, width, length), lambda h: (0, h, 0, 0))],
        out_specs=[
            pl.BlockSpec((1, width, length), lambda h: (h, 0, 0)),
            pl.BlockSpec((1, 1, length), lambda h: (h, 0, 0)),
        ],
        out_shape=[
            jax.ShapeDtypeStruct((heads, width, length), jnp.bfloat16),
            jax.ShapeDtypeStruct((heads, 1, length), jnp.float32),
        ],
        cost_estimate=pl.CostEstimate(
            flops=4 * heads * length * length * 256,
            bytes_accessed=10 * heads * width * length,
            transcendentals=heads * length * length,
        ),
        compiler_params=pltpu.CompilerParams(vmem_limit_bytes=48 * 1024 * 1024),
        name="heads_forward",
    )(qkv)


def heads_back_kernel(
    qkv_ref, grad_ref, mixed_ref, log_ref, out_ref, key_acc, value_acc, *, step
):
    length = qkv_ref.shape[-1]
    keys_t = qkv_ref[1, 0]
    keys = keys_t.astype(jnp.float32).T.astype(jnp.bfloat16)
    values = qkv_ref[2, 0].astype(jnp.float32).T.astype(jnp.bfloat16)
    for start in range(0, length, step):
        queries_t = qkv_ref[0, 0, :, start : start + step]
        grad_t = grad_ref[0, :, start : start + step]
        queries = queries_t.astype(jnp.float32).T.astype(jnp.bfloat16)
        grad = grad_t.astype(jnp.float32).T.astype(jnp.bfloat16)
        scores = nn(keys, queries_t) * (SCORE_SCALE * LOG2E)
        probable = jnp.exp2(scores - log_ref[0, :, start : start + step])
        d_weights = nn(values, grad_t)
        inner_sum = jnp.sum(
            grad_t.astype(jnp.float32) * mixed_ref[0, :, start : start + step].astype(jnp.float32),
            axis=0,
            keepdims=True,
        )
        d_scores = (probable * (d_weights - inner_sum)).astype(jnp.bfloat16)
        d_values = nn(probable.astype(jnp.bfloat16), grad)
        d_keys = nn(d_scores, queries)
        if start == 0:
            value_acc[...] = d_values
            key_acc[...] = d_keys
        else:
            value_acc[...] += d_values
            key_acc[...] += d_keys
        out_ref[0, 0, :, start : start + step] = (nn(keys_t, d_scores) * SCORE_SCALE).astype(
            jnp.bfloat16
        )
    out_ref[1, 0] = (key_acc[...] * SCORE_SCALE).T.astype(jnp.bfloat16)
    out_ref[2, 0] = value_acc[...].T.astype(jnp.bfloat16)


def heads_back(qkv, grad, mixed, log_total, step=256):
    _, heads, width, length = qkv.shape
    return pl.pallas_call(
        functools.partial(heads_back_kernel, step=step),
        grid=(heads,),
        in_specs=[
            pl.BlockSpec((3, 1, width, length), lambda h: (0, h, 0, 0)),
            pl.BlockSpec((1, width, length), lambda h: (h, 0, 0)),
            pl.BlockSpec((1, width, length), lambda h: (h, 0, 0)),
            pl.BlockSpec((1, 1, length), lambda h: (h, 0, 0)),
        ],
        out_specs=pl.BlockSpec((3, 1, width, length), lambda h: (0, h, 0, 0)),
        out_shape=jax.ShapeDtypeStruct((3, heads, width, length), jnp.bfloat16),
        scratch_shapes=[
            pltpu.VMEM((length, width), jnp.float32),
            pltpu.VMEM((length, width), jnp.float32),
        ],
        cost_estimate=pl.CostEstimate(
            flops=10 * heads * length * length * 256,
            bytes_accessed=16 * heads * width * length,
            transcendentals=heads * length * length,
        ),
        compiler_params=pltpu.CompilerParams(vmem_limit_bytes=60 * 1024 * 1024),
        name="heads_back",
    )(qkv, grad, mixed, log_total)


RANK = ADAPTER_RANK
LANES = 128
PADDED = MODEL_WIDTH + LANES
HALF = MODEL_WIDTH // 2
MIB = 1024 * 1024


def transposed(block):
    return block.astype(jnp.float32).T


def once(shape):
    return pl.BlockSpec(shape, lambda *_: (0,) * len(shape), pipeline_mode=pl.Buffered(1))


def rows_of(shape, axis):
    return pl.BlockSpec(shape, lambda i: tuple(i if a == axis else 0 for a in range(len(shape))))


def standard(stream):
    center = stream - jnp.mean(stream, -1, keepdims=True)
    inverse = lax.rsqrt(jnp.mean(center * center, -1, keepdims=True) + norm_eps)
    return (center * inverse, inverse)


def assemble_kernel(place_ref, near_ref, far_ref, next_near_ref, next_far_ref, out_ref, sems):
    z, x, core, y = (place_ref[i] for i in range(4))
    depth = out_ref.shape[1]
    copies = []
    for side, pair in enumerate(((near_ref, far_ref), (next_near_ref, next_far_ref))):
        source = core if side == 0 else 1 - core
        for stage, ref in enumerate(pair):
            for hop in range(2):
                by_x = jnp.where(source == 0, hop, stage)
                by_y = hop + stage - by_x
                for shift in range(depth):
                    target = out_ref.at[
                        lax.rem(y + by_y, 2),
                        lax.rem(z + depth - shift, depth),
                        lax.rem(x + by_x, 2),
                        source,
                    ]
                    copy = pltpu.make_async_copy(
                        ref.at[hop, shift], target, sems.at[len(copies)]
                    )
                    copy.start()
                    copies.append(copy)
    for copy in copies:
        copy.wait()


def assemble(place, near, far, next_near, next_far):
    _, depth, rows, columns = near.shape
    return pl.pallas_call(
        assemble_kernel,
        in_specs=[pl.BlockSpec(memory_space=pltpu.SMEM)]
        + [pl.BlockSpec(memory_space=pltpu.VMEM)] * 4,
        out_specs=pl.BlockSpec(memory_space=pl.ANY),
        out_shape=jax.ShapeDtypeStruct((2, depth, 2, 2, rows, columns), near.dtype),
        scratch_shapes=[pltpu.SemaphoreType.DMA((8 * depth,))],
        cost_estimate=pl.CostEstimate(
            flops=0, bytes_accessed=16 * near.size, transcendentals=0
        ),
        compiler_params=pltpu.CompilerParams(vmem_limit_bytes=32 * MIB),
        name="assemble",
    )(place, near, far, next_near, next_far)


def entry_kernel(
    token_ref, mod_ref, weight_ref, up_ref, down_ref, hidden_ref, middle_ref, qkv_ref, weight_aug
):
    @pl.when(pl.program_id(0) == 0)
    def _():
        weight_aug[:MODEL_WIDTH, :] = weight_ref[...]
        weight_aug[MODEL_WIDTH:, :] = up_ref[...]

    normed, _ = standard(token_ref[...].astype(jnp.float32))
    hidden = (normed * (1.0 + mod_ref[1:2]) + mod_ref[0:1]).astype(jnp.bfloat16)
    middle = nt(hidden, down_ref[...]).astype(jnp.bfloat16)
    hidden_ref[...] = hidden
    middle_ref[...] = middle
    joined = jnp.concatenate([hidden, middle], 1)
    for part in range(3):
        columns = slice(part * MODEL_WIDTH, (part + 1) * MODEL_WIDTH)
        packed = nn(joined, weight_aug[:, columns])
        qkv_ref[part] = packed.T.reshape(qkv_ref.shape[1:]).astype(jnp.bfloat16)


def entry(tokens, mods, weight, up, down, tile=256):
    length = tokens.shape[0]
    bf16 = jnp.bfloat16
    return pl.pallas_call(
        entry_kernel,
        grid=(length // tile,),
        in_specs=[
            rows_of((tile, MODEL_WIDTH), 0),
            once(mods.shape),
            once((MODEL_WIDTH, 3 * MODEL_WIDTH)),
            once(up.shape),
            once(down.shape),
        ],
        out_specs=[
            rows_of((tile, MODEL_WIDTH), 0),
            rows_of((tile, LANES), 0),
            rows_of((3, HEADS, HD, tile), 3),
        ],
        out_shape=[
            jax.ShapeDtypeStruct((length, MODEL_WIDTH), bf16),
            jax.ShapeDtypeStruct((length, LANES), bf16),
            jax.ShapeDtypeStruct((3, HEADS, HD, length), bf16),
        ],
        scratch_shapes=[pltpu.VMEM((PADDED, 3 * MODEL_WIDTH), bf16)],
        cost_estimate=pl.CostEstimate(
            flops=6 * length * MODEL_WIDTH * PADDED,
            bytes_accessed=2 * weight.size + 12 * length * MODEL_WIDTH,
            transcendentals=0,
        ),
        compiler_params=pltpu.CompilerParams(vmem_limit_bytes=56 * MIB),
        name="entry",
    )(tokens, mods, weight, up, down)


def load_proj(proj_aug, weight_ref, up_ref):
    @pl.when(pl.program_id(0) == 0)
    def _():
        proj_aug[:MODEL_WIDTH, :] = weight_ref[...]
        proj_aug[MODEL_WIDTH:, :] = up_ref[...]


def before_kernel(
    mixed_ref,
    token_ref,
    cot_ref,
    mod_ref,
    weight_ref,
    up_proj_ref,
    down_proj_ref,
    down_expand_ref,
    up_shrink_ref,
    bias_ref,
    second_ref,
    dfinal_ref,
    branch_ref,
    middle_ref,
    proj_aug,
):
    bf16 = jnp.bfloat16
    load_proj(proj_aug, weight_ref, up_proj_ref)
    mixed = transposed(mixed_ref[...]).astype(bf16)
    middle_proj = nt(mixed, down_proj_ref[...])
    branch = nn(jnp.concatenate([mixed, middle_proj.astype(bf16)], 1), proj_aug[...])
    branch = branch + bias_ref[...]
    branch_ref[...] = branch
    residual = token_ref[...].astype(jnp.float32) + mod_ref[2:3] * branch
    normed, _ = standard(residual)
    second = (normed * (1.0 + mod_ref[4:5]) + mod_ref[3:4]).astype(bf16)
    middle_expand = nt(second, down_expand_ref[...])
    second_ref[:, :MODEL_WIDTH] = second
    second_ref[:, MODEL_WIDTH:] = middle_expand.astype(bf16)
    d_final = (mod_ref[5:6] * cot_ref[...].astype(jnp.float32)).astype(bf16)
    dmiddle_shrink = nt(d_final, up_shrink_ref[...])
    dfinal_ref[:, :MODEL_WIDTH] = d_final
    dfinal_ref[:, MODEL_WIDTH:] = dmiddle_shrink.astype(bf16)
    middle_ref[0] = middle_proj.T[:RANK].astype(bf16)
    middle_ref[1] = middle_expand.T[:RANK].astype(bf16)
    middle_ref[2] = dmiddle_shrink.T[:RANK].astype(bf16)


def before_feed(
    mixed, tokens, cotangent, mods, weight, up_proj, down_proj, down_expand, up_shrink, bias, tile=256
):
    length = tokens.shape[0]
    bf16 = jnp.bfloat16
    return pl.pallas_call(
        before_kernel,
        grid=(length // tile,),
        in_specs=[
            rows_of((MODEL_WIDTH, tile), 1),
            rows_of((tile, MODEL_WIDTH), 0),
            rows_of((tile, MODEL_WIDTH), 0),
            once(mods.shape),
            pl.BlockSpec(
                (MODEL_WIDTH, MODEL_WIDTH), lambda *_: (0, 3), pipeline_mode=pl.Buffered(1)
            ),
            once(up_proj.shape),
            once(down_proj.shape),
            once(down_expand.shape),
            once(up_shrink.shape),
            once(bias.shape),
        ],
        out_specs=[
            rows_of((tile, PADDED), 0),
            rows_of((tile, PADDED), 0),
            rows_of((tile, MODEL_WIDTH), 0),
            rows_of((3, RANK, tile), 2),
        ],
        out_shape=[
            jax.ShapeDtypeStruct((length, PADDED), bf16),
            jax.ShapeDtypeStruct((length, PADDED), bf16),
            jax.ShapeDtypeStruct((length, MODEL_WIDTH), jnp.float32),
            jax.ShapeDtypeStruct((3, RANK, length), bf16),
        ],
        scratch_shapes=[pltpu.VMEM((PADDED, MODEL_WIDTH), bf16)],
        cost_estimate=pl.CostEstimate(
            flops=4 * length * MODEL_WIDTH * PADDED,
            bytes_accessed=16 * length * MODEL_WIDTH,
            transcendentals=0,
        ),
        compiler_params=pltpu.CompilerParams(vmem_limit_bytes=48 * MIB),
        name="before_feed",
    )(mixed, tokens, cotangent, mods, weight, up_proj, down_proj, down_expand, up_shrink, bias)


GELU_RATE = 0.7978845608
GELU_CUBE = 0.044715


def gelu_pair(inner, d_active):
    square = inner * inner
    tanh = jnp.tanh(inner * (GELU_RATE + (GELU_RATE * GELU_CUBE) * square))
    half = 0.5 + 0.5 * tanh
    slope = half + inner * (half * (1.0 - tanh)) * (
        GELU_RATE + (3.0 * GELU_CUBE * GELU_RATE) * square
    )
    return (inner * half).astype(jnp.bfloat16), (d_active * slope).astype(jnp.bfloat16)


def feed_kernel(
    second_ref, dfinal_ref, middle_ref, left_ref, right_ref, up_ref, down_ref, bias_ref,
    final_in_ref, dsecond_in_ref, final_ref, dsecond_ref, up_grad_ref, down_grad_ref,
    widen_aug, narrow_aug, *, rows, first, sub,
):
    width = MODEL_WIDTH
    chunks = left_ref.shape[-1] // width
    for chunk in range(chunks):
        rows_now = slice(chunk * width, (chunk + 1) * width)
        for side, ref in enumerate((left_ref, right_ref)):
            at = chunk * width + side * HALF
            widen_aug[:width, at : at + HALF] = ref[:, chunk * width : chunk * width + HALF]
            narrow_aug[rows_now, side * HALF : (side + 1) * HALF] = ref[
                :, chunk * width + HALF : (chunk + 1) * width
            ]
    widen_aug[width:, :] = up_ref[...]
    narrow_aug[:, width:] = down_ref[...]
    length = second_ref.shape[0]
    for index in range(chunks * width // sub):
        cols = slice(index * sub, (index + 1) * sub)
        for start in range(0, length, rows):
            at = slice(start, start + rows)
            inner = nn(second_ref[at, :], widen_aug[:, cols]) + bias_ref[:, cols]
            active, d_inner = gelu_pair(inner, nt(dfinal_ref[at, :], narrow_aug[cols, :]))
            final = nn(active, narrow_aug[cols, :])
            dsecond = nt(d_inner, widen_aug[:, cols])
            if index == 0 and first:
                final_ref[at, :] = final
                dsecond_ref[at, :] = dsecond
            elif index == 0:
                final_ref[at, :] = final_in_ref[at, :] + final
                dsecond_ref[at, :] = dsecond_in_ref[at, :] + dsecond
            else:
                final_ref[at, :] += final
                dsecond_ref[at, :] += dsecond
            up_grad = nn(middle_ref[1, :, at], d_inner)
            down_grad = nn(middle_ref[2, :, at], active)
            if start == 0:
                up_grad_ref[:, cols] = up_grad
                down_grad_ref[:, cols] = down_grad
            else:
                up_grad_ref[:, cols] += up_grad
                down_grad_ref[:, cols] += down_grad


def side_of(weight, side):
    width = weight.size // (2 * MODEL_WIDTH)
    if weight.ndim == 2:
        return pl.BlockSpec(
            (MODEL_WIDTH, width), lambda *_: (0, side), pipeline_mode=pl.Buffered(1)
        )
    return pl.BlockSpec(
        (None, MODEL_WIDTH, width), lambda *_: (side, 0, 0), pipeline_mode=pl.Buffered(1)
    )


def feed(second, dfinal, middles, weight, up, down, bias, sums, rows=1024, sub=768):
    length, padded = second.shape
    hidden = weight.size // (2 * MODEL_WIDTH)
    first = sums is None
    if first:
        sums = (jnp.zeros((8, LANES), jnp.float32),) * 2
    return pl.pallas_call(
        functools.partial(feed_kernel, rows=rows, first=first, sub=sub),
        grid=(1,),
        in_specs=[
            once((length, padded)), once((length, padded)), once(middles.shape),
            *(side_of(weight, side) for side in range(2)),
            once(up.shape), once(down.shape), once(bias.shape),
            once(sums[0].shape), once(sums[1].shape),
        ],
        out_specs=[once((length, padded)), once((length, padded)), once((RANK, hidden)), once((RANK, hidden))],
        out_shape=[
            jax.ShapeDtypeStruct((length, padded), jnp.float32),
            jax.ShapeDtypeStruct((length, padded), jnp.float32),
            jax.ShapeDtypeStruct((RANK, hidden), jnp.float32),
            jax.ShapeDtypeStruct((RANK, hidden), jnp.float32),
        ],
        scratch_shapes=[pltpu.VMEM((padded, hidden), jnp.bfloat16), pltpu.VMEM((hidden, padded), jnp.bfloat16)],
        input_output_aliases={} if first else {8: 0, 9: 1},
        cost_estimate=pl.CostEstimate(
            flops=8 * length * padded * hidden,
            bytes_accessed=weight.size + 12 * length * padded,
            transcendentals=length * hidden,
        ),
        compiler_params=pltpu.CompilerParams(vmem_limit_bytes=63 * MIB),
        name="feed",
    )(second, dfinal, middles, weight, weight, up, down, bias, *sums)


def back_through(gradient, normed, inverse):
    return inverse * (
        gradient
        - jnp.mean(gradient, -1, keepdims=True)
        - normed * jnp.mean(gradient * normed, -1, keepdims=True)
    )


def total(values):
    return jnp.sum(values, axis=0, keepdims=True)


def after_kernel(
    final_ref,
    dsecond_ref,
    token_ref,
    cot_ref,
    branch_ref,
    second_ref,
    dfinal_ref,
    mixed_ref,
    middle_ref,
    mod_ref,
    weight_ref,
    up_proj_ref,
    down_proj_ref,
    down_expand_ref,
    up_shrink_ref,
    bias_ref,
    block_ref,
    dresidual_ref,
    dmixed_ref,
    sums_ref,
    up_shrink_grad,
    down_expand_grad,
    up_proj_grad,
    down_proj_grad,
    proj_aug,
):
    bf16 = jnp.bfloat16
    load_proj(proj_aug, weight_ref, up_proj_ref)
    cot = cot_ref[...].astype(jnp.float32)
    branch = branch_ref[...]
    residual = token_ref[...].astype(jnp.float32) + mod_ref[2:3] * branch
    normed, inverse = standard(residual)
    middle_shrink = final_ref[:, MODEL_WIDTH:]
    final = final_ref[:, :MODEL_WIDTH] + bias_ref[...]
    final = final + nn(middle_shrink.astype(bf16), up_shrink_ref[...])
    block_ref[...] = (residual + mod_ref[5:6] * final).astype(bf16)
    dmiddle_expand = dsecond_ref[:, MODEL_WIDTH:]
    d_second = dsecond_ref[:, :MODEL_WIDTH] + nn(dmiddle_expand.astype(bf16), down_expand_ref[...])
    d_residual = cot + back_through(d_second * (1.0 + mod_ref[4:5]), normed, inverse)
    dresidual_ref[...] = d_residual
    d_branch = (mod_ref[2:3] * d_residual).astype(bf16)
    joined = nt(d_branch, proj_aug[...])
    dmiddle_proj = joined[:, MODEL_WIDTH:].astype(bf16)
    d_mixed = joined[:, :MODEL_WIDTH] + nn(dmiddle_proj, down_proj_ref[...])
    dmixed_ref[...] = d_mixed.T.astype(bf16)
    sums = jnp.concatenate(
        [
            total(d_residual * branch),
            total(d_second),
            total(d_second * normed),
            total(cot * final),
            jnp.zeros((4, MODEL_WIDTH), jnp.float32),
        ],
        0,
    )
    grads = (
        nn(middle_shrink.T[:RANK].astype(bf16), dfinal_ref[...]),
        nn(dmiddle_expand.T[:RANK].astype(bf16), second_ref[...]),
        nn(middle_ref[0], d_branch),
        nn(mixed_ref[...], dmiddle_proj),
    )
    refs = (up_shrink_grad, down_expand_grad, up_proj_grad, down_proj_grad)

    @pl.when(pl.program_id(0) == 0)
    def _():
        sums_ref[...] = sums
        for ref, grad in zip(refs, grads):
            ref[...] = grad

    @pl.when(pl.program_id(0) > 0)
    def _():
        sums_ref[...] += sums
        for ref, grad in zip(refs, grads):
            ref[...] += grad


def after_feed(
    final,
    dsecond,
    tokens,
    cotangent,
    branch,
    second,
    dfinal,
    mixed,
    middles,
    mods,
    weight,
    up_proj,
    down_proj,
    down_expand,
    up_shrink,
    bias,
    tile=256,
):
    length = tokens.shape[0]
    bf16, f32 = jnp.bfloat16, jnp.float32
    low_rank = jax.ShapeDtypeStruct((RANK, MODEL_WIDTH), f32)
    return pl.pallas_call(
        after_kernel,
        grid=(length // tile,),
        in_specs=[
            rows_of((tile, PADDED), 0),
            rows_of((tile, PADDED), 0),
            rows_of((tile, MODEL_WIDTH), 0),
            rows_of((tile, MODEL_WIDTH), 0),
            rows_of((tile, MODEL_WIDTH), 0),
            rows_of((tile, MODEL_WIDTH), 0),
            rows_of((tile, MODEL_WIDTH), 0),
            rows_of((MODEL_WIDTH, tile), 1),
            rows_of((3, RANK, tile), 2),
            once(mods.shape),
            pl.BlockSpec(
                (MODEL_WIDTH, MODEL_WIDTH), lambda *_: (0, 3), pipeline_mode=pl.Buffered(1)
            ),
            once(up_proj.shape),
            once(down_proj.shape),
            once(down_expand.shape),
            once(up_shrink.shape),
            once(bias.shape),
        ],
        out_specs=[
            rows_of((tile, MODEL_WIDTH), 0),
            rows_of((tile, MODEL_WIDTH), 0),
            rows_of((MODEL_WIDTH, tile), 1),
            once((8, MODEL_WIDTH)),
            once((RANK, MODEL_WIDTH)),
            once((RANK, MODEL_WIDTH)),
            once((RANK, MODEL_WIDTH)),
            once((MODEL_WIDTH, LANES)),
        ],
        out_shape=[
            jax.ShapeDtypeStruct((length, MODEL_WIDTH), bf16),
            jax.ShapeDtypeStruct((length, MODEL_WIDTH), f32),
            jax.ShapeDtypeStruct((MODEL_WIDTH, length), bf16),
            jax.ShapeDtypeStruct((8, MODEL_WIDTH), f32),
            low_rank,
            low_rank,
            low_rank,
            jax.ShapeDtypeStruct((MODEL_WIDTH, LANES), f32),
        ],
        scratch_shapes=[pltpu.VMEM((PADDED, MODEL_WIDTH), bf16)],
        cost_estimate=pl.CostEstimate(
            flops=5 * length * MODEL_WIDTH * PADDED,
            bytes_accessed=32 * length * MODEL_WIDTH,
            transcendentals=0,
        ),
        compiler_params=pltpu.CompilerParams(vmem_limit_bytes=60 * MIB),
        name="after_feed",
    )(
        final,
        dsecond,
        tokens,
        cotangent,
        branch,
        second,
        dfinal,
        mixed,
        middles,
        mods,
        weight,
        up_proj,
        down_proj,
        down_expand,
        up_shrink,
        bias,
    )


def leave_kernel(
    dqkv_ref,
    token_ref,
    dresidual_ref,
    hidden_ref,
    middle_ref,
    mod_ref,
    weight_ref,
    up_ref,
    down_ref,
    token_grad_ref,
    sums_ref,
    up_grad,
    down_grad,
    weight_aug,
):
    bf16 = jnp.bfloat16
    @pl.when(pl.program_id(0) == 0)
    def _():
        weight_aug[:MODEL_WIDTH, :] = weight_ref[...]
        weight_aug[MODEL_WIDTH:, :] = up_ref[...]

    tile = token_ref.shape[0]
    middle_t = transposed(middle_ref[...])[:RANK].astype(bf16)
    joined = jnp.zeros((tile, PADDED), jnp.float32)
    up_grads = []
    for part in range(3):
        columns = slice(part * MODEL_WIDTH, (part + 1) * MODEL_WIDTH)
        packed_t = dqkv_ref[part].astype(jnp.float32).reshape(MODEL_WIDTH, tile)
        packed = packed_t.T.astype(bf16)
        joined = joined + nt(packed, weight_aug[:, columns])
        up_grads.append(nn(middle_t, packed))
    dmiddle = joined[:, MODEL_WIDTH:]
    d_hidden = joined[:, :MODEL_WIDTH] + nn(dmiddle.astype(bf16), down_ref[...])
    normed, inverse = standard(token_ref[...].astype(jnp.float32))
    back = back_through(d_hidden * (1.0 + mod_ref[1:2]), normed, inverse)
    token_grad_ref[...] = (dresidual_ref[...] + back).astype(bf16)
    sums = jnp.concatenate(
        [total(d_hidden), total(d_hidden * normed), jnp.zeros((6, MODEL_WIDTH), jnp.float32)], 0
    )
    down = nn(dmiddle.T[:RANK].astype(bf16), hidden_ref[...])

    @pl.when(pl.program_id(0) == 0)
    def _():
        sums_ref[...] = sums
        down_grad[...] = down
        for part in range(3):
            up_grad[:, part * MODEL_WIDTH : (part + 1) * MODEL_WIDTH] = up_grads[part]

    @pl.when(pl.program_id(0) > 0)
    def _():
        sums_ref[...] += sums
        down_grad[...] += down
        for part in range(3):
            up_grad[:, part * MODEL_WIDTH : (part + 1) * MODEL_WIDTH] += up_grads[part]


def leave(dqkv, tokens, dresidual, hidden, middle, mods, weight, up, down, tile=256):
    length = tokens.shape[0]
    bf16, f32 = jnp.bfloat16, jnp.float32
    return pl.pallas_call(
        leave_kernel,
        grid=(length // tile,),
        in_specs=[
            rows_of((3, HEADS, HD, tile), 3),
            rows_of((tile, MODEL_WIDTH), 0),
            rows_of((tile, MODEL_WIDTH), 0),
            rows_of((tile, MODEL_WIDTH), 0),
            rows_of((tile, LANES), 0),
            once(mods.shape),
            once((MODEL_WIDTH, 3 * MODEL_WIDTH)),
            once(up.shape),
            once(down.shape),
        ],
        out_specs=[
            rows_of((tile, MODEL_WIDTH), 0),
            once((8, MODEL_WIDTH)),
            once((RANK, 3 * MODEL_WIDTH)),
            once((RANK, MODEL_WIDTH)),
        ],
        out_shape=[
            jax.ShapeDtypeStruct((length, MODEL_WIDTH), bf16),
            jax.ShapeDtypeStruct((8, MODEL_WIDTH), f32),
            jax.ShapeDtypeStruct((RANK, 3 * MODEL_WIDTH), f32),
            jax.ShapeDtypeStruct((RANK, MODEL_WIDTH), f32),
        ],
        scratch_shapes=[pltpu.VMEM((PADDED, 3 * MODEL_WIDTH), bf16)],
        cost_estimate=pl.CostEstimate(
            flops=7 * length * MODEL_WIDTH * PADDED,
            bytes_accessed=2 * weight.size + 18 * length * MODEL_WIDTH,
            transcendentals=0,
        ),
        compiler_params=pltpu.CompilerParams(vmem_limit_bytes=60 * MIB),
        name="leave",
    )(dqkv, tokens, dresidual, hidden, middle, mods, weight, up, down)


def layout(n_fsdp):
    return [(f // 4, f // 2 % 2, f % 2) for f in range(n_fsdp)]


def moved(n_fsdp, step):
    pairs = []
    for f, (z, x, c) in enumerate(layout(n_fsdp)):
        for y in range(2):
            to_z, to_x, to_c, to_y = step(z, x, c, y)
            pairs.append((2 * f + y, 2 * (4 * to_z + 2 * to_x + to_c) + to_y))
    return pairs


BOTH = ("fsdp", "seq")


def step_z(block, n_fsdp):
    depth = n_fsdp // 4
    by_shift = [block]
    for shift in range(1, depth):
        pairs = moved(n_fsdp, lambda z, x, c, y: ((z + shift) % depth, x, c, y))
        by_shift.append(lax.ppermute(block, BOTH, pairs))
    return jnp.stack(by_shift)


def step_first(block, n_fsdp):
    return lax.ppermute(
        block,
        BOTH,
        moved(n_fsdp, lambda z, x, c, y: (z, x, c, 1 - y) if c else (z, 1 - x, c, y)),
    )


def step_second(block, n_fsdp):
    return lax.ppermute(
        block,
        BOTH,
        moved(n_fsdp, lambda z, x, c, y: (z, 1 - x, c, y) if c else (z, x, c, 1 - y)),
    )


def step_core(block, n_fsdp):
    return lax.ppermute(block, BOTH, moved(n_fsdp, lambda z, x, c, y: (z, x, 1 - c, y)))


def behind(block, *earlier):
    for array in earlier:
        element = lax.slice(array, [n - 1 for n in array.shape], array.shape).reshape(())
        element = element.astype(jnp.float32)
        block = block + jnp.minimum(jnp.abs(element), 0.0).astype(block.dtype)
    return block


def gather_late(block, n_fsdp, place):
    line = step_z(block, n_fsdp)
    near = jnp.stack([line, step_first(line, n_fsdp)])
    far = step_second(near, n_fsdp)
    gathered = assemble(place, near, far, step_core(near, n_fsdp), step_core(far, n_fsdp))
    return gathered.reshape(2, n_fsdp * block.shape[0], block.shape[1])


DOWN_EDGES = (0, 1152, 2304, 3456, 4608, 9216)
UP_EDGES = (0, 6912, 10368, 11520, 16128, 17280)
PIECES = FF // HD


def piece_order(n_fsdp):
    per = PIECES // n_fsdp
    return [f * per + q for q in range(per) for f in range(n_fsdp)]


def unpack_kernel(came_ref, *refs, order, down_chunk, up_chunk):
    bf16 = jnp.bfloat16
    outs, (down_all, up_all, mixed) = refs[:-3], refs[-3:]
    down_outs, up_outs, shrink_t = outs[:4], outs[4:9], outs[9]
    for f in range(came_ref.shape[0]):
        block = came_ref[f].astype(jnp.float32)
        down_all[:, f * down_chunk : (f + 1) * down_chunk] = block[:, :down_chunk]
        up_all[:, f * up_chunk : (f + 1) * up_chunk] = block[:, down_chunk:]
    for target, out in enumerate(down_outs):
        out[...] = jnp.zeros_like(out)
        out[:RANK] = down_all[:, DOWN_EDGES[target] : DOWN_EDGES[target + 1]].astype(bf16)
    mixed[...] = jnp.zeros_like(mixed)
    for target, out in enumerate(up_outs):
        if target == 3:
            for to, piece in enumerate(order):
                at = UP_EDGES[3] + piece * HD
                mixed[:RANK, to * HD : (to + 1) * HD] = up_all[:, at : at + HD]
            out[...] = mixed[...].astype(bf16)
        else:
            out[...] = jnp.zeros_like(out)
            out[:RANK] = up_all[:, UP_EDGES[target] : UP_EDGES[target + 1]].astype(bf16)
    for to, piece in enumerate(order):
        at = DOWN_EDGES[4] + piece * HD
        mixed[:RANK, to * HD : (to + 1) * HD] = down_all[:, at : at + HD]
    for start in range(0, FF, MODEL_WIDTH):
        shrink_t[start : start + MODEL_WIDTH, :] = mixed[:, start : start + MODEL_WIDTH].T.astype(
            bf16
        )


def unpack(came, order, down_chunk, up_chunk):
    bf16 = jnp.bfloat16
    widths = [DOWN_EDGES[t + 1] - DOWN_EDGES[t] for t in range(4)]
    widths += [UP_EDGES[t + 1] - UP_EDGES[t] for t in range(5)]
    return pl.pallas_call(
        functools.partial(
            unpack_kernel, order=order, down_chunk=down_chunk, up_chunk=up_chunk
        ),
        out_shape=[jax.ShapeDtypeStruct((LANES, w), bf16) for w in widths]
        + [jax.ShapeDtypeStruct((FF, LANES), bf16)],
        scratch_shapes=[
            pltpu.VMEM((RANK, DOWN_EDGES[5]), jnp.float32),
            pltpu.VMEM((RANK, UP_EDGES[5]), jnp.float32),
            pltpu.VMEM((LANES, FF), jnp.float32),
        ],
        compiler_params=pltpu.CompilerParams(vmem_limit_bytes=48 * MIB),
        name="unpack",
    )(came)


def pack_kernel(
    leave_ref,
    after_ref,
    middle_ref,
    cond_ref,
    down_ada_ref,
    up_ada_ref,
    down_qkv,
    up_qkv,
    down_proj,
    up_proj,
    down_expand,
    up_expand_low,
    up_expand_high,
    down_shrink_low,
    down_shrink_high,
    up_shrink,
    sent_ref,
    dmod_ref,
    own_ref,
    down_all,
    up_all,
    *,
    order,
    down_chunk,
    up_chunk,
):
    bf16, f32 = jnp.bfloat16, jnp.float32
    width = MODEL_WIDTH
    dmiddle = jnp.zeros((RANK, 1), f32)
    for block in range(6):
        source = leave_ref if block < 2 else after_ref
        line = source[block % 2 if block < 2 else block - 2, :].reshape(1, width)
        line = line.astype(bf16).astype(f32)
        columns = slice(block * width, (block + 1) * width)
        side, at = block // 3, block % 3 * width
        dmod_ref[side : side + 1, at : at + width] = line
        up_all[:, columns] = middle_ref[...] * line
        dmiddle += jnp.sum(up_ada_ref[:RANK, columns].astype(f32) * line, axis=1, keepdims=True)
    dmiddle = dmiddle.astype(bf16).astype(f32)
    down_all[:, :width] = dmiddle * cond_ref[...]
    own_ref[...] = total(dmiddle * down_ada_ref[:RANK].astype(f32))
    down_all[:, width : 2 * width] = down_qkv[...]
    down_all[:, 2 * width : 3 * width] = down_proj[...].T[:RANK]
    down_all[:, 3 * width : 4 * width] = down_expand[...]
    up_all[:, UP_EDGES[1] : UP_EDGES[2]] = up_qkv[...]
    up_all[:, UP_EDGES[2] : UP_EDGES[3]] = up_proj[...]
    up_all[:, UP_EDGES[4] : UP_EDGES[5]] = up_shrink[...]
    half = PIECES // 2
    for at, piece in enumerate(order):
        ups = up_expand_low if at < half else up_expand_high
        downs = down_shrink_low if at < half else down_shrink_high
        columns = slice((at % half) * HD, (at % half + 1) * HD)
        to = UP_EDGES[3] + piece * HD
        up_all[:, to : to + HD] = ups[:, columns]
        to = DOWN_EDGES[4] + piece * HD
        down_all[:, to : to + HD] = downs[:, columns]
    for f in range(sent_ref.shape[0]):
        sent_ref[f, :, :down_chunk] = down_all[:, f * down_chunk : (f + 1) * down_chunk].astype(bf16)
        sent_ref[f, :, down_chunk:] = up_all[:, f * up_chunk : (f + 1) * up_chunk].astype(bf16)


def pack(operands, n_fsdp, order, down_chunk, up_chunk):
    bf16, f32 = jnp.bfloat16, jnp.float32
    return pl.pallas_call(
        functools.partial(pack_kernel, order=order, down_chunk=down_chunk, up_chunk=up_chunk),
        out_shape=[
            jax.ShapeDtypeStruct((n_fsdp, RANK, down_chunk + up_chunk), bf16),
            jax.ShapeDtypeStruct((2, 3 * MODEL_WIDTH), f32),
            jax.ShapeDtypeStruct((1, MODEL_WIDTH), f32),
        ],
        scratch_shapes=[
            pltpu.VMEM((RANK, DOWN_EDGES[5]), f32),
            pltpu.VMEM((RANK, UP_EDGES[5]), f32),
        ],
        compiler_params=pltpu.CompilerParams(vmem_limit_bytes=48 * MIB),
        name="pack",
    )(*operands)


def owners_kernel(ids_ref, place_ref, came_ref, kept_ref, given_ref, sums):
    sums[...] = jnp.zeros_like(sums)
    for f in range(came_ref.shape[0]):
        sums[ids_ref[f]] += came_ref[f].astype(jnp.float32)
    held = kept_ref.shape[0]
    mine = place_ref[3]
    for index in range(held):
        kept_ref[index] = sums[mine * held + index]
        given_ref[index] = sums[(1 - mine) * held + index].astype(jnp.bfloat16)


def owners(ids, place, came):
    held = ADAPTER_COUNT // 2
    shape = (held,) + came.shape[1:]
    return pl.pallas_call(
        owners_kernel,
        in_specs=[
            pl.BlockSpec(memory_space=pltpu.SMEM),
            pl.BlockSpec(memory_space=pltpu.SMEM),
            pl.BlockSpec(memory_space=pltpu.VMEM),
        ],
        out_shape=[
            jax.ShapeDtypeStruct(shape, jnp.float32),
            jax.ShapeDtypeStruct(shape, jnp.bfloat16),
        ],
        scratch_shapes=[pltpu.VMEM((ADAPTER_COUNT,) + came.shape[1:], jnp.float32)],
        compiler_params=pltpu.CompilerParams(vmem_limit_bytes=32 * MIB),
        name="owners",
    )(ids, place, came)


def update_kernel(gradient_ref, squared_ref, *refs):
    down_chunk = refs[0].shape[-1]
    grad_norm = jnp.sqrt(jnp.sum(squared_ref[:, :1], axis=0, keepdims=True))
    clip_factor = jnp.minimum(1.0, clip_limit / (grad_norm + norm_eps))
    ins, outs, norm_ref = refs[:6], refs[6:12], refs[12]
    norm_ref[...] = jnp.broadcast_to(grad_norm, norm_ref.shape)
    for kind in range(2):
        part = slice(0, down_chunk) if kind == 0 else slice(down_chunk, None)
        for index in range(gradient_ref.shape[0]):
            gradient = gradient_ref[index, :, part] * clip_factor
            params = ins[kind][index]
            moment_new = beta_first * ins[2 + kind][index] + (1.0 - beta_first) * gradient
            square_new = (
                beta_second * ins[4 + kind][index] + (1.0 - beta_second) * gradient * gradient
            )
            direction = (
                moment_new
                / (1.0 - beta_first**STEP)
                / (jnp.sqrt(square_new / (1.0 - beta_second**STEP)) + adam_eps)
            )
            outs[kind][index] = params - learn_rate * (direction + decay_rate * params)
            outs[2 + kind][index] = moment_new
            outs[4 + kind][index] = square_new


def update(gradient, squared, states):
    f32 = jnp.float32
    outs = pl.pallas_call(
        update_kernel,
        out_shape=[jax.ShapeDtypeStruct(s.shape, f32) for s in states]
        + [jax.ShapeDtypeStruct((8, LANES), f32)],
        compiler_params=pltpu.CompilerParams(vmem_limit_bytes=32 * MIB),
        name="update",
    )(gradient, squared, *states)
    return outs[:6], outs[6][0, 0]


def fits(mesh):
    return mesh.shape["seq"] == MB and mesh.shape["fsdp"] == 16


def dot(equation, left, right):
    return jnp.einsum(equation, left, right, preferred_element_type=jnp.float32)


def swap(block):
    return lax.ppermute(block, "seq", [(0, 1), (1, 0)])


def by_seq(own, other, mine):
    first = mine == 0
    return jnp.stack([jnp.where(first, own, other), jnp.where(first, other, own)])


def swap_rows(halves, mine):
    kept, came = send_row(halves, mine)
    return by_seq(kept, came, mine)


def send_row(halves, mine):
    sent = lax.dynamic_index_in_dim(halves, 1 - mine, 0, False)
    return lax.dynamic_index_in_dim(halves, mine, 0, False), swap(sent)


def to_all(block):
    return lax.all_to_all(block, ("fsdp", "seq"), split_axis=0, concat_axis=0, tiled=True)


def to_fsdp(block):
    return lax.all_to_all(block, "fsdp", split_axis=0, concat_axis=0, tiled=True)


def fast_shards(
    tokens,
    condition,
    adapter,
    cotangent,
    modulation_weight,
    modulation_bias,
    query_key_value_weight,
    attention_out_weight,
    attention_out_bias,
    widen_weight,
    widen_bias,
    narrow_weight,
    narrow_bias,
    lowrank_down,
    lowrank_up,
    first_moment_down,
    first_moment_up,
    second_moment_down,
    second_moment_up,
):
    bf16 = jnp.bfloat16
    n_fsdp = lax.axis_size("fsdp")
    mine = lax.axis_index("seq")
    row = lax.axis_index("fsdp")
    place = jnp.stack([row // 4, row // 2 % 2, row % 2, mine]).astype(jnp.int32)
    down_chunk, up_chunk = lowrank_down.shape[-1], lowrank_up.shape[-1]
    depth = modulation_weight.shape[0]
    order = piece_order(n_fsdp)
    per = PIECES // n_fsdp

    cond_act_pair = jax.nn.silu(condition).astype(bf16)
    told = jnp.moveaxis(cond_act_pair.reshape(MB, n_fsdp, depth), 1, 0)
    numbers = jnp.broadcast_to(adapter.astype(bf16)[None, :, None], (n_fsdp, MB, 8))
    told = to_fsdp(jnp.concatenate([told, numbers], 2))
    own_ids = lax.dynamic_index_in_dim(told[:, :, depth], mine, 1, False).astype(jnp.int32)

    wide = jnp.moveaxis(widen_weight.reshape(depth, -1, per, HD), 2, 0).reshape(per, depth, HALF)
    narrow = narrow_weight.reshape(per, depth, HALF)

    def whole(block):
        return lax.all_gather(block, "fsdp", axis=0, tiled=True)

    heads = jnp.concatenate([query_key_value_weight, attention_out_weight], 1)
    heads = by_seq(heads, swap(heads), mine)
    cut = query_key_value_weight.shape[1]
    heads_weight = whole(
        jnp.concatenate([heads[0, :, :cut], heads[1, :, :cut], heads[0, :, cut:], heads[1, :, cut:]], 1)
    )
    joined = [jnp.concatenate([wide[q], narrow[q]], 1) for q in range(per)]
    low = jnp.concatenate(joined[: per // 2], 1)
    low = by_seq(low, swap(low), mine)
    low_weight = whole(jnp.concatenate([low[0], low[1]], 1))
    high_weight = gather_late(jnp.concatenate(joined[per // 2 :], 1), n_fsdp, place)

    portions = jnp.concatenate([lowrank_down.astype(bf16), lowrank_up.astype(bf16)], -1)
    others = swap(portions)
    table = by_seq(portions, others, mine).reshape(ADAPTER_COUNT, RANK, -1)
    picks = jax.nn.one_hot(own_ids, ADAPTER_COUNT, dtype=bf16)
    chosen = dot("fa,arc->frc", picks, table).astype(bf16)
    parts = unpack(to_fsdp(chosen), order, down_chunk, up_chunk)
    down_ada, down_qkv, down_proj, down_expand = parts[:4]
    up_ada, up_qkv, up_proj, up_expand, up_shrink = parts[4:9]
    down_shrink_t = parts[9]

    spoken = told[:, :, :depth].reshape(n_fsdp * MB, depth)
    mod_part = to_all(dot("si,io->so", spoken, modulation_weight))
    mod_base = jnp.sum(mod_part.reshape(n_fsdp, MB, -1), axis=0).reshape(1, -1)

    cond_act = lax.dynamic_slice_in_dim(cond_act_pair, mine, 1, 0)
    middle_ada = dot("ti,ri->tr", cond_act, down_ada).astype(bf16)
    modulation = mod_base + modulation_bias + dot("tr,ro->to", middle_ada, up_ada)
    mods = jnp.pad(modulation.reshape(6, MODEL_WIDTH), ((0, 2), (0, 0)))

    length = MB * tokens.shape[1]
    token_rows = swap_rows(tokens, mine).reshape(length, MODEL_WIDTH)
    cot_rows = swap_rows(cotangent, mine).reshape(length, MODEL_WIDTH)

    hidden, middle_qkv, qkv = entry(token_rows, mods, heads_weight, up_qkv, down_qkv)
    mixed_heads, log_total = heads_forward(qkv, step=length)
    mixed = mixed_heads.reshape(MODEL_WIDTH, length)
    second, dfinal, branch, middles = before_feed(
        mixed,
        token_rows,
        cot_rows,
        mods,
        heads_weight,
        up_proj,
        down_proj,
        down_expand,
        up_shrink,
        attention_out_bias[None],
    )
    bias = jnp.moveaxis(widen_bias.reshape(n_fsdp, per, HD), 0, 1).reshape(1, FF)
    cut = FF // 2
    final, dsecond, up_expand_low, down_shrink_low = feed(
        second,
        dfinal,
        middles,
        low_weight,
        up_expand[:, :cut],
        down_shrink_t[:cut],
        bias[:, :cut],
        None,
    )
    final, dsecond, up_expand_high, down_shrink_high = feed(
        second,
        dfinal,
        middles,
        high_weight,
        up_expand[:, cut:],
        down_shrink_t[cut:],
        bias[:, cut:],
        (final, dsecond),
    )
    (
        block_rows,
        d_residual,
        d_mixed,
        after_sums,
        up_shrink_grad,
        down_expand_grad,
        up_proj_grad,
        down_proj_grad,
    ) = after_feed(
        final,
        dsecond,
        token_rows,
        cot_rows,
        branch,
        second,
        dfinal,
        mixed,
        middles,
        mods,
        heads_weight,
        up_proj,
        down_proj,
        down_expand,
        up_shrink,
        narrow_bias[None],
    )
    block_out = swap_rows(block_rows.reshape(tokens.shape), mine)
    d_qkv = heads_back(
        qkv, d_mixed.reshape(HEADS, HD, length), mixed_heads, log_total, step=length
    )
    token_rows_grad, leave_sums, up_qkv_grad, down_qkv_grad = leave(
        d_qkv, token_rows, d_residual, hidden, middle_qkv, mods, heads_weight, up_qkv, down_qkv
    )

    sent, d_modulation, own_cond = pack(
        (
            leave_sums,
            after_sums,
            middle_ada[:, :RANK].astype(jnp.float32).T,
            cond_act.astype(jnp.float32),
            down_ada,
            up_ada,
            down_qkv_grad,
            up_qkv_grad,
            down_proj_grad,
            up_proj_grad,
            down_expand_grad,
            up_expand_low,
            up_expand_high,
            down_shrink_low,
            down_shrink_high,
            up_shrink_grad,
        ),
        n_fsdp,
        order,
        down_chunk,
        up_chunk,
    )
    kept, given = owners(own_ids, place, to_fsdp(sent))
    gradient = kept + swap(given).astype(jnp.float32)
    squared = to_all(jnp.broadcast_to(jnp.sum(gradient * gradient), (n_fsdp * MB, LANES)))

    half_weight = lax.all_gather(
        behind(modulation_weight, second), "fsdp", axis=0, tiled=True
    )
    both_mod = behind(swap_rows(d_modulation.astype(bf16), mine), kept)
    d_cond = dot("so,io->si", both_mod, half_weight)
    d_cond = d_cond + jnp.where(jnp.arange(MB)[:, None] == mine, own_cond, 0.0)
    d_cond = d_cond + swap(d_cond)
    cond_grad = jax.vjp(jax.nn.silu, condition)[1](d_cond)[0]
    token_kept, token_came = send_row(token_rows_grad.reshape(tokens.shape), mine)
    token_grad = by_seq(behind(token_kept, gradient), token_came, mine).astype(jnp.float32)

    states = (
        lowrank_down,
        lowrank_up,
        first_moment_down,
        first_moment_up,
        second_moment_down,
        second_moment_up,
    )
    fresh, grad_norm = update(gradient, squared, states)
    return (block_out, token_grad, cond_grad, grad_norm, *fresh)


def solution(mesh):
    in_specs = (
        P("fsdp", "seq", None),
        P("fsdp", None),
        P("fsdp"),
        P("fsdp", "seq", None),
        P("fsdp", "seq"),
        P(),
        P("fsdp", "seq"),
        P("fsdp", "seq"),
        P(),
        P("fsdp", "seq"),
        P(),
        P("fsdp", "seq"),
        P(),
        P("seq", None, "fsdp"),
        P("seq", None, "fsdp"),
        P("seq", None, "fsdp"),
        P("seq", None, "fsdp"),
        P("seq", None, "fsdp"),
        P("seq", None, "fsdp"),
    )
    out_specs = (
        P("fsdp", "seq", None),
        P("fsdp", "seq", None),
        P("fsdp", None),
        P(),
        P("seq", None, "fsdp"),
        P("seq", None, "fsdp"),
        P("seq", None, "fsdp"),
        P("seq", None, "fsdp"),
        P("seq", None, "fsdp"),
        P("seq", None, "fsdp"),
    )
    body = fast_shards if fits(mesh) else shards
    return jax.shard_map(body, mesh=mesh, in_specs=in_specs, out_specs=out_specs, check_vma=False)
```

```python
import functools

import jax
import jax.numpy as jnp
from jax import lax
from jax.experimental import pallas as pl
from jax.experimental.pallas import tpu as pltpu
from jax.sharding import PartitionSpec as P

MODEL_WIDTH = 1152
HD = 72
FF = 4608
ADAPTER_RANK = 16
ADAPTER_COUNT = 8
MB = 2
SEQ_MB = 1
STEP = 10


beta_first = 0.9
beta_second = 0.999
learn_rate = 0.05
decay_rate = 0.1
adam_eps = 1e-08
clip_limit = 1.0
norm_eps = 1e-06
pair_heads = 2
highest = lax.Precision.HIGHEST


def linear(inputs, weight):
    return jnp.einsum("sti,io->sto", inputs, weight, preferred_element_type=jnp.float32)


def linear_back(gradient, weight):
    return jnp.einsum("sto,io->sti", gradient, weight, preferred_element_type=jnp.float32)


def normalize(stream):
    center = stream - jnp.mean(stream, -1, keepdims=True)
    inverse = lax.rsqrt(jnp.mean(center * center, -1, keepdims=True) + norm_eps)
    return (center * inverse, inverse)


def normalize_back(gradient, normed, inverse):
    return inverse * (
        gradient
        - jnp.mean(gradient, -1, keepdims=True)
        - normed * jnp.mean(gradient * normed, -1, keepdims=True)
    )


def adapt_forward(inputs, down_part, up_part):
    middle = jnp.einsum(
        "sti,sri->str", inputs, down_part, preferred_element_type=jnp.float32
    ).astype(jnp.bfloat16)
    return (middle, jnp.einsum("str,sro->sto", middle, up_part, preferred_element_type=jnp.float32))


def adapt_backward(inputs, middle, gradient, down_part, up_part):
    up_grad = jnp.einsum("str,sto->sro", middle, gradient, preferred_element_type=jnp.float32)
    middle_grad = jnp.einsum(
        "sto,sro->str", gradient, up_part, preferred_element_type=jnp.float32
    ).astype(jnp.bfloat16)
    down_grad = jnp.einsum("str,sti->sri", middle_grad, inputs, preferred_element_type=jnp.float32)
    input_grad = jnp.einsum(
        "str,sri->sti", middle_grad, down_part, preferred_element_type=jnp.float32
    )
    return (input_grad, down_grad, up_grad)


def grouped(matrix):
    seq_count, row_count, col_count = matrix.shape
    return jnp.moveaxis(
        matrix.reshape(seq_count, row_count, col_count // (pair_heads * HD), pair_heads, HD), 2, 0
    )


def ungrouped(stacked):
    moved = jnp.moveaxis(stacked, 0, 2)
    return moved.reshape(moved.shape[0], moved.shape[1], -1)


def attend_group(group_inputs):
    queries, all_keys, all_values = group_inputs
    factor = queries.shape[-1] ** (-0.5)
    scores = (
        jnp.einsum("sqhd,skhd->shqk", queries, all_keys, preferred_element_type=jnp.float32)
        * factor
    )
    row_max = jnp.max(scores, -1, keepdims=True)
    exponent = jnp.exp(scores - row_max)
    row_total = jnp.sum(exponent, -1, keepdims=True)
    weights = (exponent / row_total).astype(jnp.bfloat16)
    mixed_heads = jnp.einsum(
        "shqk,skhd->sqhd", weights, all_values, preferred_element_type=jnp.float32
    )
    return (mixed_heads, row_max + jnp.log(row_total))


def attend_back(group_inputs):
    queries, all_keys, all_values, d_mixed, log_total = group_inputs
    factor = queries.shape[-1] ** (-0.5)
    scores = (
        jnp.einsum("sqhd,skhd->shqk", queries, all_keys, preferred_element_type=jnp.float32)
        * factor
    )
    probable = jnp.exp(scores - log_total)
    d_values = jnp.einsum(
        "shqk,sqhd->skhd",
        probable.astype(jnp.bfloat16),
        d_mixed,
        preferred_element_type=jnp.float32,
    )
    d_weights = jnp.einsum(
        "sqhd,skhd->shqk", d_mixed, all_values, preferred_element_type=jnp.float32
    )
    inner_sum = jnp.sum(d_weights * probable, -1, keepdims=True)
    d_scores = (probable * (d_weights - inner_sum) * factor).astype(jnp.bfloat16)
    d_queries = jnp.einsum(
        "shqk,skhd->sqhd", d_scores, all_keys, preferred_element_type=jnp.float32
    )
    d_keys = jnp.einsum("shqk,sqhd->skhd", d_scores, queries, preferred_element_type=jnp.float32)
    return (d_queries, d_keys, d_values)


def gelu_tanh(inner_act):
    return jax.nn.gelu(inner_act, approximate=True)


def shards(
    tokens,
    condition,
    adapter,
    cotangent,
    modulation_weight,
    modulation_bias,
    query_key_value_weight,
    attention_out_weight,
    attention_out_bias,
    widen_weight,
    widen_bias,
    narrow_weight,
    narrow_bias,
    lowrank_down,
    lowrank_up,
    first_moment_down,
    first_moment_up,
    second_moment_down,
    second_moment_up,
):
    seq_count_axis = lax.axis_size("seq")
    seq_share = 1.0 / seq_count_axis
    down_portion = lowrank_down.astype(jnp.bfloat16)
    up_portion = lowrank_up.astype(jnp.bfloat16)
    down_edges = (
        0,
        MODEL_WIDTH,
        2 * MODEL_WIDTH,
        3 * MODEL_WIDTH,
        4 * MODEL_WIDTH,
        4 * MODEL_WIDTH + FF,
    )
    up_edges = (
        0,
        6 * MODEL_WIDTH,
        9 * MODEL_WIDTH,
        10 * MODEL_WIDTH,
        10 * MODEL_WIDTH + FF,
        11 * MODEL_WIDTH + FF,
    )

    def fetch():
        across = (
            lax.all_gather(modulation_weight, "seq", axis=1, tiled=True),
            lax.all_gather(query_key_value_weight, "seq", axis=1, tiled=True),
            lax.all_gather(attention_out_weight, "seq", axis=1, tiled=True),
            lax.all_gather(widen_weight, "seq", axis=1, tiled=True),
            lax.all_gather(narrow_weight, "seq", axis=1, tiled=True),
            lax.all_gather(down_portion, "seq", axis=0, tiled=True),
            lax.all_gather(up_portion, "seq", axis=0, tiled=True),
        )
        return (
            lax.all_gather(across[0], "fsdp", axis=0, tiled=True),
            lax.all_gather(across[1], "fsdp", axis=0, tiled=True),
            lax.all_gather(across[2], "fsdp", axis=0, tiled=True),
            lax.all_gather(across[3], "fsdp", axis=0, tiled=True),
            lax.all_gather(across[4], "fsdp", axis=0, tiled=True),
            lax.all_gather(across[5], "fsdp", axis=2, tiled=True),
            lax.all_gather(across[6], "fsdp", axis=2, tiled=True),
        )

    def select(gathered_now, picked_adapter):
        down_sel = gathered_now[5][picked_adapter]
        up_sel = gathered_now[6][picked_adapter]
        down_blocks = [
            down_sel[:, :, down_edges[target] : down_edges[target + 1]] for target in range(5)
        ]
        up_blocks = [up_sel[:, :, up_edges[target] : up_edges[target + 1]] for target in range(5)]
        return (
            gathered_now[0],
            gathered_now[1],
            gathered_now[2],
            gathered_now[3],
            gathered_now[4],
            down_blocks,
            up_blocks,
        )

    down_gradient = jnp.zeros((ADAPTER_COUNT, ADAPTER_RANK, down_edges[5]), jnp.float32)
    up_gradient = jnp.zeros((ADAPTER_COUNT, ADAPTER_RANK, up_edges[5]), jnp.float32)
    output_list, token_list, cond_list = ([], [], [])
    for micro_batch in range(MB):
        first_seq = micro_batch * SEQ_MB
        token_rows = tokens[first_seq : first_seq + SEQ_MB].astype(jnp.float32)
        cond_rows = condition[first_seq : first_seq + SEQ_MB]
        picked_adapter = adapter[first_seq : first_seq + SEQ_MB]
        cot_rows = cotangent[first_seq : first_seq + SEQ_MB].astype(jnp.float32)
        batch_seqs = token_rows.shape[0]
        local_rows = token_rows.shape[1]
        gathered = fetch()
        full_ada, full_qkv, full_proj, full_expand, full_shrink, down_blocks, up_blocks = select(
            gathered, picked_adapter
        )
        cond_act = jax.nn.silu(cond_rows).astype(jnp.bfloat16)[:, None, :]
        middle_ada, extra_ada = adapt_forward(cond_act, down_blocks[0], up_blocks[0])
        modulation = linear(cond_act, full_ada) + modulation_bias + extra_ada
        shift_first, scale_first, gate_first, shift_second, scale_second, gate_second = jnp.split(
            modulation, 6, axis=-1
        )
        normed_first, inverse_first = normalize(token_rows)
        hidden = (normed_first * (1.0 + scale_first) + shift_first).astype(jnp.bfloat16)
        middle_qkv, extra_qkv = adapt_forward(hidden, down_blocks[1], up_blocks[1])
        packed = (linear(hidden, full_qkv) + extra_qkv).astype(jnp.bfloat16)
        head_blocks = packed.reshape(
            batch_seqs, local_rows, 3, seq_count_axis, MODEL_WIDTH // seq_count_axis
        )
        by_heads = lax.all_to_all(head_blocks, "seq", split_axis=3, concat_axis=1, tiled=True)
        query_groups = grouped(by_heads[:, :, 0, 0])
        key_groups = grouped(by_heads[:, :, 1, 0])
        value_groups = grouped(by_heads[:, :, 2, 0])
        mixed_groups, log_total = lax.map(attend_group, (query_groups, key_groups, value_groups))
        mixed = lax.all_to_all(
            ungrouped(mixed_groups).astype(jnp.bfloat16),
            "seq",
            split_axis=1,
            concat_axis=2,
            tiled=True,
        )
        middle_proj, extra_proj = adapt_forward(mixed, down_blocks[2], up_blocks[2])
        branch = linear(mixed, full_proj) + attention_out_bias + extra_proj
        residual = token_rows + gate_first * branch
        normed_second, inverse_second = normalize(residual)
        second = (normed_second * (1.0 + scale_second) + shift_second).astype(jnp.bfloat16)
        middle_expand, extra_expand = adapt_forward(second, down_blocks[3], up_blocks[3])
        inner_act = linear(second, full_expand) + widen_bias + extra_expand
        active = gelu_tanh(inner_act).astype(jnp.bfloat16)
        middle_shrink, extra_shrink = adapt_forward(active, down_blocks[4], up_blocks[4])
        final_out = linear(active, full_shrink) + narrow_bias + extra_shrink
        output_list.append((residual + gate_second * final_out).astype(jnp.bfloat16))
        gathered = fetch()
        full_ada, full_qkv, full_proj, full_expand, full_shrink, down_blocks, up_blocks = select(
            gathered, picked_adapter
        )
        d_final = (gate_second * cot_rows).astype(jnp.bfloat16)
        d_gate_second = jnp.sum(cot_rows * final_out, axis=1, keepdims=True)
        d_active, down_shrink, up_shrink = adapt_backward(
            active, middle_shrink, d_final, down_blocks[4], up_blocks[4]
        )
        d_active = d_active + linear_back(d_final, full_shrink)
        d_inner = jax.vjp(gelu_tanh, inner_act)[1](d_active)[0].astype(jnp.bfloat16)
        d_second, down_expand, up_expand = adapt_backward(
            second, middle_expand, d_inner, down_blocks[3], up_blocks[3]
        )
        d_second = d_second + linear_back(d_inner, full_expand)
        d_shift_second = jnp.sum(d_second, axis=1, keepdims=True)
        d_scale_second = jnp.sum(d_second * normed_second, axis=1, keepdims=True)
        d_residual = cot_rows + normalize_back(
            d_second * (1.0 + scale_second), normed_second, inverse_second
        )
        d_branch = (gate_first * d_residual).astype(jnp.bfloat16)
        d_gate_first = jnp.sum(d_residual * branch, axis=1, keepdims=True)
        d_mixed, down_proj, up_proj = adapt_backward(
            mixed, middle_proj, d_branch, down_blocks[2], up_blocks[2]
        )
        d_mixed = (d_mixed + linear_back(d_branch, full_proj)).astype(jnp.bfloat16)
        d_by_heads = lax.all_to_all(d_mixed, "seq", split_axis=2, concat_axis=1, tiled=True)
        dquery_groups, dkey_groups, dvalue_groups = lax.map(
            attend_back, (query_groups, key_groups, value_groups, grouped(d_by_heads), log_total)
        )
        stacked = jnp.stack(
            [
                ungrouped(dquery_groups).astype(jnp.bfloat16),
                ungrouped(dkey_groups).astype(jnp.bfloat16),
                ungrouped(dvalue_groups).astype(jnp.bfloat16),
            ],
            2,
        )[:, :, :, None, :]
        returned = lax.all_to_all(stacked, "seq", split_axis=1, concat_axis=3, tiled=True)
        d_packed = returned.reshape(batch_seqs, local_rows, 3 * MODEL_WIDTH)
        d_hidden, down_qkv, up_qkv = adapt_backward(
            hidden, middle_qkv, d_packed, down_blocks[1], up_blocks[1]
        )
        d_hidden = d_hidden + linear_back(d_packed, full_qkv)
        d_shift_first = jnp.sum(d_hidden, axis=1, keepdims=True)
        d_scale_first = jnp.sum(d_hidden * normed_first, axis=1, keepdims=True)
        token_list.append(
            d_residual + normalize_back(d_hidden * (1.0 + scale_first), normed_first, inverse_first)
        )
        partial_mod = jnp.concatenate(
            [
                d_shift_first,
                d_scale_first,
                d_gate_first,
                d_shift_second,
                d_scale_second,
                d_gate_second,
            ],
            -1,
        )
        d_modulation = lax.psum(partial_mod, "seq").astype(jnp.bfloat16)
        d_cond_act, down_ada, up_ada = adapt_backward(
            cond_act, middle_ada, d_modulation, down_blocks[0], up_blocks[0]
        )
        d_cond_act = d_cond_act + linear_back(d_modulation, full_ada)
        cond_list.append(jax.vjp(jax.nn.silu, cond_rows)[1](d_cond_act[:, 0, :])[0])
        seq_down = jnp.concatenate(
            [down_ada * seq_share, down_qkv, down_proj, down_expand, down_shrink], -1
        )
        seq_up = jnp.concatenate([up_ada * seq_share, up_qkv, up_proj, up_expand, up_shrink], -1)
        selector = jax.nn.one_hot(picked_adapter, ADAPTER_COUNT, dtype=jnp.float32)
        down_gradient = down_gradient + jnp.einsum(
            "sa,src->arc", selector, seq_down, precision=highest
        )
        up_gradient = up_gradient + jnp.einsum("sa,src->arc", selector, seq_up, precision=highest)
    part_down, part_up = (
        lax.psum_scatter(down_gradient, "fsdp", scatter_dimension=2, tiled=True),
        lax.psum_scatter(up_gradient, "fsdp", scatter_dimension=2, tiled=True),
    )
    sequence_down, sequence_up = (
        lax.psum_scatter(
            part_down.astype(jnp.bfloat16), "seq", scatter_dimension=0, tiled=True
        ).astype(jnp.float32),
        lax.psum_scatter(
            part_up.astype(jnp.bfloat16), "seq", scatter_dimension=0, tiled=True
        ).astype(jnp.float32),
    )
    squared = lax.psum(
        jnp.sum(sequence_down * sequence_down) + jnp.sum(sequence_up * sequence_up), ("fsdp", "seq")
    )
    grad_norm = jnp.sqrt(squared)
    clip_factor = jnp.minimum(1.0, clip_limit / (grad_norm + norm_eps))

    def optimizer_update(params, gradient, moment, square):
        gradient = gradient * clip_factor
        moment_new = beta_first * moment + (1.0 - beta_first) * gradient
        square_new = beta_second * square + (1.0 - beta_second) * gradient * gradient
        direction = (
            moment_new
            / (1.0 - beta_first**STEP)
            / (jnp.sqrt(square_new / (1.0 - beta_second**STEP)) + adam_eps)
        )
        return (params - learn_rate * (direction + decay_rate * params), moment_new, square_new)

    stepped_down, next_first_down, next_second_down = optimizer_update(
        lowrank_down, sequence_down, first_moment_down, second_moment_down
    )
    stepped_up, next_first_up, next_second_up = optimizer_update(
        lowrank_up, sequence_up, first_moment_up, second_moment_up
    )
    block_out = jnp.concatenate(output_list, 0)
    token_grad = jnp.concatenate(token_list, 0)
    cond_grad = jnp.concatenate(cond_list, 0)
    return (
        block_out,
        token_grad,
        cond_grad,
        grad_norm,
        stepped_down,
        stepped_up,
        next_first_down,
        next_first_up,
        next_second_down,
        next_second_up,
    )


HEADS = 16
LOG2E = 1.4426950408889634
SCORE_SCALE = HD ** (-0.5)


def tn(left, right):
    return lax.dot_general(left, right, (((0,), (0,)), ((), ())), preferred_element_type=jnp.float32)


def nn(left, right):
    return lax.dot_general(left, right, (((1,), (0,)), ((), ())), preferred_element_type=jnp.float32)


def nt(left, right):
    return lax.dot_general(left, right, (((1,), (1,)), ((), ())), preferred_element_type=jnp.float32)


def heads_kernel(qkv_ref, mixed_ref, log_ref, *, step):
    length = qkv_ref.shape[-1]
    keys = qkv_ref[1, 0].astype(jnp.float32).T.astype(jnp.bfloat16)
    values_t = qkv_ref[2, 0]
    for start in range(0, length, step):
        queries_t = qkv_ref[0, 0, :, start : start + step]
        scores = nn(keys, queries_t) * (SCORE_SCALE * LOG2E)
        top = jnp.max(scores, axis=0, keepdims=True)
        exponent = jnp.exp2(scores - top)
        total = jnp.sum(exponent, axis=0, keepdims=True)
        weights = (exponent * (1.0 / total)).astype(jnp.bfloat16)
        mixed_ref[0, :, start : start + step] = nn(values_t, weights).astype(jnp.bfloat16)
        log_ref[0, :, start : start + step] = top + jnp.log2(total)


def heads_forward(qkv, step=256):
    _, heads, width, length = qkv.shape
    return pl.pallas_call(
        functools.partial(heads_kernel, step=step),
        grid=(heads,),
        in_specs=[pl.BlockSpec((3, 1, width, length), lambda h: (0, h, 0, 0))],
        out_specs=[
            pl.BlockSpec((1, width, length), lambda h: (h, 0, 0)),
            pl.BlockSpec((1, 1, length), lambda h: (h, 0, 0)),
        ],
        out_shape=[
            jax.ShapeDtypeStruct((heads, width, length), jnp.bfloat16),
            jax.ShapeDtypeStruct((heads, 1, length), jnp.float32),
        ],
        cost_estimate=pl.CostEstimate(
            flops=4 * heads * length * length * 256,
            bytes_accessed=10 * heads * width * length,
            transcendentals=heads * length * length,
        ),
        compiler_params=pltpu.CompilerParams(vmem_limit_bytes=48 * 1024 * 1024),
        name="heads_forward",
    )(qkv)


def heads_back_kernel(
    qkv_ref, grad_ref, mixed_ref, log_ref, out_ref, key_acc, value_acc, *, step
):
    length = qkv_ref.shape[-1]
    keys_t = qkv_ref[1, 0]
    keys = keys_t.astype(jnp.float32).T.astype(jnp.bfloat16)
    values = qkv_ref[2, 0].astype(jnp.float32).T.astype(jnp.bfloat16)
    for start in range(0, length, step):
        queries_t = qkv_ref[0, 0, :, start : start + step]
        grad_t = grad_ref[0, :, start : start + step]
        queries = queries_t.astype(jnp.float32).T.astype(jnp.bfloat16)
        grad = grad_t.astype(jnp.float32).T.astype(jnp.bfloat16)
        scores = nn(keys, queries_t) * (SCORE_SCALE * LOG2E)
        probable = jnp.exp2(scores - log_ref[0, :, start : start + step])
        d_weights = nn(values, grad_t)
        inner_sum = jnp.sum(
            grad_t.astype(jnp.float32) * mixed_ref[0, :, start : start + step].astype(jnp.float32),
            axis=0,
            keepdims=True,
        )
        d_scores = (probable * (d_weights - inner_sum)).astype(jnp.bfloat16)
        d_values = nn(probable.astype(jnp.bfloat16), grad)
        d_keys = nn(d_scores, queries)
        if start == 0:
            value_acc[...] = d_values
            key_acc[...] = d_keys
        else:
            value_acc[...] += d_values
            key_acc[...] += d_keys
        out_ref[0, 0, :, start : start + step] = (nn(keys_t, d_scores) * SCORE_SCALE).astype(
            jnp.bfloat16
        )
    out_ref[1, 0] = (key_acc[...] * SCORE_SCALE).T.astype(jnp.bfloat16)
    out_ref[2, 0] = value_acc[...].T.astype(jnp.bfloat16)


def heads_back(qkv, grad, mixed, log_total, step=256):
    _, heads, width, length = qkv.shape
    return pl.pallas_call(
        functools.partial(heads_back_kernel, step=step),
        grid=(heads,),
        in_specs=[
            pl.BlockSpec((3, 1, width, length), lambda h: (0, h, 0, 0)),
            pl.BlockSpec((1, width, length), lambda h: (h, 0, 0)),
            pl.BlockSpec((1, width, length), lambda h: (h, 0, 0)),
            pl.BlockSpec((1, 1, length), lambda h: (h, 0, 0)),
        ],
        out_specs=pl.BlockSpec((3, 1, width, length), lambda h: (0, h, 0, 0)),
        out_shape=jax.ShapeDtypeStruct((3, heads, width, length), jnp.bfloat16),
        scratch_shapes=[
            pltpu.VMEM((length, width), jnp.float32),
            pltpu.VMEM((length, width), jnp.float32),
        ],
        cost_estimate=pl.CostEstimate(
            flops=10 * heads * length * length * 256,
            bytes_accessed=16 * heads * width * length,
            transcendentals=heads * length * length,
        ),
        compiler_params=pltpu.CompilerParams(vmem_limit_bytes=60 * 1024 * 1024),
        name="heads_back",
    )(qkv, grad, mixed, log_total)


RANK = ADAPTER_RANK
LANES = 128
PADDED = MODEL_WIDTH + LANES
HALF = MODEL_WIDTH // 2
MIB = 1024 * 1024


def transposed(block):
    return block.astype(jnp.float32).T


def once(shape):
    return pl.BlockSpec(shape, lambda *_: (0,) * len(shape), pipeline_mode=pl.Buffered(1))


def rows_of(shape, axis):
    return pl.BlockSpec(shape, lambda i: tuple(i if a == axis else 0 for a in range(len(shape))))


def standard(stream):
    center = stream - jnp.mean(stream, -1, keepdims=True)
    inverse = lax.rsqrt(jnp.mean(center * center, -1, keepdims=True) + norm_eps)
    return (center * inverse, inverse)


def assemble_kernel(place_ref, near_ref, far_ref, next_near_ref, next_far_ref, out_ref, sems):
    z, x, core, y = (place_ref[i] for i in range(4))
    depth = out_ref.shape[1]
    copies = []
    for side, pair in enumerate(((near_ref, far_ref), (next_near_ref, next_far_ref))):
        source = core if side == 0 else 1 - core
        for stage, ref in enumerate(pair):
            for hop in range(2):
                by_x = jnp.where(source == 0, hop, stage)
                by_y = hop + stage - by_x
                for shift in range(depth):
                    target = out_ref.at[
                        lax.rem(y + by_y, 2),
                        lax.rem(z + depth - shift, depth),
                        lax.rem(x + by_x, 2),
                        source,
                    ]
                    copy = pltpu.make_async_copy(
                        ref.at[hop, shift], target, sems.at[len(copies)]
                    )
                    copy.start()
                    copies.append(copy)
    for copy in copies:
        copy.wait()


def assemble(place, near, far, next_near, next_far):
    _, depth, rows, columns = near.shape
    return pl.pallas_call(
        assemble_kernel,
        in_specs=[pl.BlockSpec(memory_space=pltpu.SMEM)]
        + [pl.BlockSpec(memory_space=pltpu.VMEM)] * 4,
        out_specs=pl.BlockSpec(memory_space=pl.ANY),
        out_shape=jax.ShapeDtypeStruct((2, depth, 2, 2, rows, columns), near.dtype),
        scratch_shapes=[pltpu.SemaphoreType.DMA((8 * depth,))],
        cost_estimate=pl.CostEstimate(
            flops=0, bytes_accessed=16 * near.size, transcendentals=0
        ),
        compiler_params=pltpu.CompilerParams(vmem_limit_bytes=32 * MIB),
        name="assemble",
    )(place, near, far, next_near, next_far)


def entry_kernel(
    token_ref, mod_ref, weight_ref, up_ref, down_ref, hidden_ref, middle_ref, qkv_ref, weight_aug
):
    @pl.when(pl.program_id(0) == 0)
    def _():
        weight_aug[:MODEL_WIDTH, :] = weight_ref[...]
        weight_aug[MODEL_WIDTH:, :] = up_ref[...]

    normed, _ = standard(token_ref[...].astype(jnp.float32))
    hidden = (normed * (1.0 + mod_ref[1:2]) + mod_ref[0:1]).astype(jnp.bfloat16)
    middle = nt(hidden, down_ref[...]).astype(jnp.bfloat16)
    hidden_ref[...] = hidden
    middle_ref[...] = middle
    joined = jnp.concatenate([hidden, middle], 1)
    for part in range(3):
        columns = slice(part * MODEL_WIDTH, (part + 1) * MODEL_WIDTH)
        packed = nn(joined, weight_aug[:, columns])
        qkv_ref[part] = packed.T.reshape(qkv_ref.shape[1:]).astype(jnp.bfloat16)


def entry(tokens, mods, weight, up, down, tile=256):
    length = tokens.shape[0]
    bf16 = jnp.bfloat16
    return pl.pallas_call(
        entry_kernel,
        grid=(length // tile,),
        in_specs=[
            rows_of((tile, MODEL_WIDTH), 0),
            once(mods.shape),
            once((MODEL_WIDTH, 3 * MODEL_WIDTH)),
            once(up.shape),
            once(down.shape),
        ],
        out_specs=[
            rows_of((tile, MODEL_WIDTH), 0),
            rows_of((tile, LANES), 0),
            rows_of((3, HEADS, HD, tile), 3),
        ],
        out_shape=[
            jax.ShapeDtypeStruct((length, MODEL_WIDTH), bf16),
            jax.ShapeDtypeStruct((length, LANES), bf16),
            jax.ShapeDtypeStruct((3, HEADS, HD, length), bf16),
        ],
        scratch_shapes=[pltpu.VMEM((PADDED, 3 * MODEL_WIDTH), bf16)],
        cost_estimate=pl.CostEstimate(
            flops=6 * length * MODEL_WIDTH * PADDED,
            bytes_accessed=2 * weight.size + 12 * length * MODEL_WIDTH,
            transcendentals=0,
        ),
        compiler_params=pltpu.CompilerParams(vmem_limit_bytes=56 * MIB),
        name="entry",
    )(tokens, mods, weight, up, down)


def load_proj(proj_aug, weight_ref, up_ref):
    @pl.when(pl.program_id(0) == 0)
    def _():
        proj_aug[:MODEL_WIDTH, :] = weight_ref[...]
        proj_aug[MODEL_WIDTH:, :] = up_ref[...]


def before_kernel(
    mixed_ref,
    token_ref,
    cot_ref,
    mod_ref,
    weight_ref,
    up_proj_ref,
    down_proj_ref,
    down_expand_ref,
    up_shrink_ref,
    bias_ref,
    second_ref,
    dfinal_ref,
    branch_ref,
    middle_ref,
    proj_aug,
):
    bf16 = jnp.bfloat16
    load_proj(proj_aug, weight_ref, up_proj_ref)
    mixed = transposed(mixed_ref[...]).astype(bf16)
    middle_proj = nt(mixed, down_proj_ref[...])
    branch = nn(jnp.concatenate([mixed, middle_proj.astype(bf16)], 1), proj_aug[...])
    branch = branch + bias_ref[...]
    branch_ref[...] = branch
    residual = token_ref[...].astype(jnp.float32) + mod_ref[2:3] * branch
    normed, _ = standard(residual)
    second = (normed * (1.0 + mod_ref[4:5]) + mod_ref[3:4]).astype(bf16)
    middle_expand = nt(second, down_expand_ref[...])
    second_ref[:, :MODEL_WIDTH] = second
    second_ref[:, MODEL_WIDTH:] = middle_expand.astype(bf16)
    d_final = (mod_ref[5:6] * cot_ref[...].astype(jnp.float32)).astype(bf16)
    dmiddle_shrink = nt(d_final, up_shrink_ref[...])
    dfinal_ref[:, :MODEL_WIDTH] = d_final
    dfinal_ref[:, MODEL_WIDTH:] = dmiddle_shrink.astype(bf16)
    middle_ref[0] = middle_proj.T[:RANK].astype(bf16)
    middle_ref[1] = middle_expand.T[:RANK].astype(bf16)
    middle_ref[2] = dmiddle_shrink.T[:RANK].astype(bf16)


def before_feed(
    mixed, tokens, cotangent, mods, weight, up_proj, down_proj, down_expand, up_shrink, bias, tile=256
):
    length = tokens.shape[0]
    bf16 = jnp.bfloat16
    return pl.pallas_call(
        before_kernel,
        grid=(length // tile,),
        in_specs=[
            rows_of((MODEL_WIDTH, tile), 1),
            rows_of((tile, MODEL_WIDTH), 0),
            rows_of((tile, MODEL_WIDTH), 0),
            once(mods.shape),
            pl.BlockSpec(
                (MODEL_WIDTH, MODEL_WIDTH), lambda *_: (0, 3), pipeline_mode=pl.Buffered(1)
            ),
            once(up_proj.shape),
            once(down_proj.shape),
            once(down_expand.shape),
            once(up_shrink.shape),
            once(bias.shape),
        ],
        out_specs=[
            rows_of((tile, PADDED), 0),
            rows_of((tile, PADDED), 0),
            rows_of((tile, MODEL_WIDTH), 0),
            rows_of((3, RANK, tile), 2),
        ],
        out_shape=[
            jax.ShapeDtypeStruct((length, PADDED), bf16),
            jax.ShapeDtypeStruct((length, PADDED), bf16),
            jax.ShapeDtypeStruct((length, MODEL_WIDTH), jnp.float32),
            jax.ShapeDtypeStruct((3, RANK, length), bf16),
        ],
        scratch_shapes=[pltpu.VMEM((PADDED, MODEL_WIDTH), bf16)],
        cost_estimate=pl.CostEstimate(
            flops=4 * length * MODEL_WIDTH * PADDED,
            bytes_accessed=16 * length * MODEL_WIDTH,
            transcendentals=0,
        ),
        compiler_params=pltpu.CompilerParams(vmem_limit_bytes=48 * MIB),
        name="before_feed",
    )(mixed, tokens, cotangent, mods, weight, up_proj, down_proj, down_expand, up_shrink, bias)


GELU_RATE = 0.7978845608
GELU_CUBE = 0.044715


def gelu_pair(inner, d_active):
    square = inner * inner
    tanh = jnp.tanh(inner * (GELU_RATE + (GELU_RATE * GELU_CUBE) * square))
    half = 0.5 + 0.5 * tanh
    slope = half + inner * (half * (1.0 - tanh)) * (
        GELU_RATE + (3.0 * GELU_CUBE * GELU_RATE) * square
    )
    return (inner * half).astype(jnp.bfloat16), (d_active * slope).astype(jnp.bfloat16)


def feed_kernel(
    second_ref, dfinal_ref, middle_ref, left_ref, right_ref, up_ref, down_ref, bias_ref,
    final_in_ref, dsecond_in_ref, final_ref, dsecond_ref, up_grad_ref, down_grad_ref,
    widen_aug, narrow_aug, *, rows, first, sub,
):
    width = MODEL_WIDTH
    chunks = left_ref.shape[-1] // width
    for chunk in range(chunks):
        rows_now = slice(chunk * width, (chunk + 1) * width)
        for side, ref in enumerate((left_ref, right_ref)):
            at = chunk * width + side * HALF
            widen_aug[:width, at : at + HALF] = ref[:, chunk * width : chunk * width + HALF]
            narrow_aug[rows_now, side * HALF : (side + 1) * HALF] = ref[
                :, chunk * width + HALF : (chunk + 1) * width
            ]
    widen_aug[width:, :] = up_ref[...]
    narrow_aug[:, width:] = down_ref[...]
    length = second_ref.shape[0]
    for index in range(chunks * width // sub):
        cols = slice(index * sub, (index + 1) * sub)
        for start in range(0, length, rows):
            at = slice(start, start + rows)
            inner = nn(second_ref[at, :], widen_aug[:, cols]) + bias_ref[:, cols]
            active, d_inner = gelu_pair(inner, nt(dfinal_ref[at, :], narrow_aug[cols, :]))
            final = nn(active, narrow_aug[cols, :])
            dsecond = nt(d_inner, widen_aug[:, cols])
            if index == 0 and first:
                final_ref[at, :] = final
                dsecond_ref[at, :] = dsecond
            elif index == 0:
                final_ref[at, :] = final_in_ref[at, :] + final
                dsecond_ref[at, :] = dsecond_in_ref[at, :] + dsecond
            else:
                final_ref[at, :] += final
                dsecond_ref[at, :] += dsecond
            up_grad = nn(middle_ref[1, :, at], d_inner)
            down_grad = nn(middle_ref[2, :, at], active)
            if start == 0:
                up_grad_ref[:, cols] = up_grad
                down_grad_ref[:, cols] = down_grad
            else:
                up_grad_ref[:, cols] += up_grad
                down_grad_ref[:, cols] += down_grad


def side_of(weight, side):
    width = weight.size // (2 * MODEL_WIDTH)
    if weight.ndim == 2:
        return pl.BlockSpec(
            (MODEL_WIDTH, width), lambda *_: (0, side), pipeline_mode=pl.Buffered(1)
        )
    return pl.BlockSpec(
        (None, MODEL_WIDTH, width), lambda *_: (side, 0, 0), pipeline_mode=pl.Buffered(1)
    )


def feed(second, dfinal, middles, weight, up, down, bias, sums, rows=1024, sub=768):
    length, padded = second.shape
    hidden = weight.size // (2 * MODEL_WIDTH)
    first = sums is None
    if first:
        sums = (jnp.zeros((8, LANES), jnp.float32),) * 2
    return pl.pallas_call(
        functools.partial(feed_kernel, rows=rows, first=first, sub=sub),
        grid=(1,),
        in_specs=[
            once((length, padded)), once((length, padded)), once(middles.shape),
            *(side_of(weight, side) for side in range(2)),
            once(up.shape), once(down.shape), once(bias.shape),
            once(sums[0].shape), once(sums[1].shape),
        ],
        out_specs=[once((length, padded)), once((length, padded)), once((RANK, hidden)), once((RANK, hidden))],
        out_shape=[
            jax.ShapeDtypeStruct((length, padded), jnp.float32),
            jax.ShapeDtypeStruct((length, padded), jnp.float32),
            jax.ShapeDtypeStruct((RANK, hidden), jnp.float32),
            jax.ShapeDtypeStruct((RANK, hidden), jnp.float32),
        ],
        scratch_shapes=[pltpu.VMEM((padded, hidden), jnp.bfloat16), pltpu.VMEM((hidden, padded), jnp.bfloat16)],
        input_output_aliases={} if first else {8: 0, 9: 1},
        cost_estimate=pl.CostEstimate(
            flops=8 * length * padded * hidden,
            bytes_accessed=weight.size + 12 * length * padded,
            transcendentals=length * hidden,
        ),
        compiler_params=pltpu.CompilerParams(vmem_limit_bytes=63 * MIB),
        name="feed",
    )(second, dfinal, middles, weight, weight, up, down, bias, *sums)


def back_through(gradient, normed, inverse):
    return inverse * (
        gradient
        - jnp.mean(gradient, -1, keepdims=True)
        - normed * jnp.mean(gradient * normed, -1, keepdims=True)
    )


def total(values):
    return jnp.sum(values, axis=0, keepdims=True)


def after_kernel(
    final_ref,
    dsecond_ref,
    token_ref,
    cot_ref,
    branch_ref,
    second_ref,
    dfinal_ref,
    mixed_ref,
    middle_ref,
    mod_ref,
    weight_ref,
    up_proj_ref,
    down_proj_ref,
    down_expand_ref,
    up_shrink_ref,
    bias_ref,
    block_ref,
    dresidual_ref,
    dmixed_ref,
    sums_ref,
    up_shrink_grad,
    down_expand_grad,
    up_proj_grad,
    down_proj_grad,
    proj_aug,
):
    bf16 = jnp.bfloat16
    load_proj(proj_aug, weight_ref, up_proj_ref)
    cot = cot_ref[...].astype(jnp.float32)
    branch = branch_ref[...]
    residual = token_ref[...].astype(jnp.float32) + mod_ref[2:3] * branch
    normed, inverse = standard(residual)
    middle_shrink = final_ref[:, MODEL_WIDTH:]
    final = final_ref[:, :MODEL_WIDTH] + bias_ref[...]
    final = final + nn(middle_shrink.astype(bf16), up_shrink_ref[...])
    block_ref[...] = (residual + mod_ref[5:6] * final).astype(bf16)
    dmiddle_expand = dsecond_ref[:, MODEL_WIDTH:]
    d_second = dsecond_ref[:, :MODEL_WIDTH] + nn(dmiddle_expand.astype(bf16), down_expand_ref[...])
    d_residual = cot + back_through(d_second * (1.0 + mod_ref[4:5]), normed, inverse)
    dresidual_ref[...] = d_residual
    d_branch = (mod_ref[2:3] * d_residual).astype(bf16)
    joined = nt(d_branch, proj_aug[...])
    dmiddle_proj = joined[:, MODEL_WIDTH:].astype(bf16)
    d_mixed = joined[:, :MODEL_WIDTH] + nn(dmiddle_proj, down_proj_ref[...])
    dmixed_ref[...] = d_mixed.T.astype(bf16)
    sums = jnp.concatenate(
        [
            total(d_residual * branch),
            total(d_second),
            total(d_second * normed),
            total(cot * final),
            jnp.zeros((4, MODEL_WIDTH), jnp.float32),
        ],
        0,
    )
    grads = (
        nn(middle_shrink.T[:RANK].astype(bf16), dfinal_ref[...]),
        nn(dmiddle_expand.T[:RANK].astype(bf16), second_ref[...]),
        nn(middle_ref[0], d_branch),
        nn(mixed_ref[...], dmiddle_proj),
    )
    refs = (up_shrink_grad, down_expand_grad, up_proj_grad, down_proj_grad)

    @pl.when(pl.program_id(0) == 0)
    def _():
        sums_ref[...] = sums
        for ref, grad in zip(refs, grads):
            ref[...] = grad

    @pl.when(pl.program_id(0) > 0)
    def _():
        sums_ref[...] += sums
        for ref, grad in zip(refs, grads):
            ref[...] += grad


def after_feed(
    final,
    dsecond,
    tokens,
    cotangent,
    branch,
    second,
    dfinal,
    mixed,
    middles,
    mods,
    weight,
    up_proj,
    down_proj,
    down_expand,
    up_shrink,
    bias,
    tile=256,
):
    length = tokens.shape[0]
    bf16, f32 = jnp.bfloat16, jnp.float32
    low_rank = jax.ShapeDtypeStruct((RANK, MODEL_WIDTH), f32)
    return pl.pallas_call(
        after_kernel,
        grid=(length // tile,),
        in_specs=[
            rows_of((tile, PADDED), 0),
            rows_of((tile, PADDED), 0),
            rows_of((tile, MODEL_WIDTH), 0),
            rows_of((tile, MODEL_WIDTH), 0),
            rows_of((tile, MODEL_WIDTH), 0),
            rows_of((tile, MODEL_WIDTH), 0),
            rows_of((tile, MODEL_WIDTH), 0),
            rows_of((MODEL_WIDTH, tile), 1),
            rows_of((3, RANK, tile), 2),
            once(mods.shape),
            pl.BlockSpec(
                (MODEL_WIDTH, MODEL_WIDTH), lambda *_: (0, 3), pipeline_mode=pl.Buffered(1)
            ),
            once(up_proj.shape),
            once(down_proj.shape),
            once(down_expand.shape),
            once(up_shrink.shape),
            once(bias.shape),
        ],
        out_specs=[
            rows_of((tile, MODEL_WIDTH), 0),
            rows_of((tile, MODEL_WIDTH), 0),
            rows_of((MODEL_WIDTH, tile), 1),
            once((8, MODEL_WIDTH)),
            once((RANK, MODEL_WIDTH)),
            once((RANK, MODEL_WIDTH)),
            once((RANK, MODEL_WIDTH)),
            once((MODEL_WIDTH, LANES)),
        ],
        out_shape=[
            jax.ShapeDtypeStruct((length, MODEL_WIDTH), bf16),
            jax.ShapeDtypeStruct((length, MODEL_WIDTH), f32),
            jax.ShapeDtypeStruct((MODEL_WIDTH, length), bf16),
            jax.ShapeDtypeStruct((8, MODEL_WIDTH), f32),
            low_rank,
            low_rank,
            low_rank,
            jax.ShapeDtypeStruct((MODEL_WIDTH, LANES), f32),
        ],
        scratch_shapes=[pltpu.VMEM((PADDED, MODEL_WIDTH), bf16)],
        cost_estimate=pl.CostEstimate(
            flops=5 * length * MODEL_WIDTH * PADDED,
            bytes_accessed=32 * length * MODEL_WIDTH,
            transcendentals=0,
        ),
        compiler_params=pltpu.CompilerParams(vmem_limit_bytes=60 * MIB),
        name="after_feed",
    )(
        final,
        dsecond,
        tokens,
        cotangent,
        branch,
        second,
        dfinal,
        mixed,
        middles,
        mods,
        weight,
        up_proj,
        down_proj,
        down_expand,
        up_shrink,
        bias,
    )


def leave_kernel(
    dqkv_ref,
    token_ref,
    dresidual_ref,
    hidden_ref,
    middle_ref,
    mod_ref,
    weight_ref,
    up_ref,
    down_ref,
    token_grad_ref,
    sums_ref,
    up_grad,
    down_grad,
    weight_aug,
):
    bf16 = jnp.bfloat16
    @pl.when(pl.program_id(0) == 0)
    def _():
        weight_aug[:MODEL_WIDTH, :] = weight_ref[...]
        weight_aug[MODEL_WIDTH:, :] = up_ref[...]

    tile = token_ref.shape[0]
    middle_t = transposed(middle_ref[...])[:RANK].astype(bf16)
    joined = jnp.zeros((tile, PADDED), jnp.float32)
    up_grads = []
    for part in range(3):
        columns = slice(part * MODEL_WIDTH, (part + 1) * MODEL_WIDTH)
        packed_t = dqkv_ref[part].astype(jnp.float32).reshape(MODEL_WIDTH, tile)
        packed = packed_t.T.astype(bf16)
        joined = joined + nt(packed, weight_aug[:, columns])
        up_grads.append(nn(middle_t, packed))
    dmiddle = joined[:, MODEL_WIDTH:]
    d_hidden = joined[:, :MODEL_WIDTH] + nn(dmiddle.astype(bf16), down_ref[...])
    normed, inverse = standard(token_ref[...].astype(jnp.float32))
    back = back_through(d_hidden * (1.0 + mod_ref[1:2]), normed, inverse)
    token_grad_ref[...] = (dresidual_ref[...] + back).astype(bf16)
    sums = jnp.concatenate(
        [total(d_hidden), total(d_hidden * normed), jnp.zeros((6, MODEL_WIDTH), jnp.float32)], 0
    )
    down = nn(dmiddle.T[:RANK].astype(bf16), hidden_ref[...])

    @pl.when(pl.program_id(0) == 0)
    def _():
        sums_ref[...] = sums
        down_grad[...] = down
        for part in range(3):
            up_grad[:, part * MODEL_WIDTH : (part + 1) * MODEL_WIDTH] = up_grads[part]

    @pl.when(pl.program_id(0) > 0)
    def _():
        sums_ref[...] += sums
        down_grad[...] += down
        for part in range(3):
            up_grad[:, part * MODEL_WIDTH : (part + 1) * MODEL_WIDTH] += up_grads[part]


def leave(dqkv, tokens, dresidual, hidden, middle, mods, weight, up, down, tile=256):
    length = tokens.shape[0]
    bf16, f32 = jnp.bfloat16, jnp.float32
    return pl.pallas_call(
        leave_kernel,
        grid=(length // tile,),
        in_specs=[
            rows_of((3, HEADS, HD, tile), 3),
            rows_of((tile, MODEL_WIDTH), 0),
            rows_of((tile, MODEL_WIDTH), 0),
            rows_of((tile, MODEL_WIDTH), 0),
            rows_of((tile, LANES), 0),
            once(mods.shape),
            once((MODEL_WIDTH, 3 * MODEL_WIDTH)),
            once(up.shape),
            once(down.shape),
        ],
        out_specs=[
            rows_of((tile, MODEL_WIDTH), 0),
            once((8, MODEL_WIDTH)),
            once((RANK, 3 * MODEL_WIDTH)),
            once((RANK, MODEL_WIDTH)),
        ],
        out_shape=[
            jax.ShapeDtypeStruct((length, MODEL_WIDTH), bf16),
            jax.ShapeDtypeStruct((8, MODEL_WIDTH), f32),
            jax.ShapeDtypeStruct((RANK, 3 * MODEL_WIDTH), f32),
            jax.ShapeDtypeStruct((RANK, MODEL_WIDTH), f32),
        ],
        scratch_shapes=[pltpu.VMEM((PADDED, 3 * MODEL_WIDTH), bf16)],
        cost_estimate=pl.CostEstimate(
            flops=7 * length * MODEL_WIDTH * PADDED,
            bytes_accessed=2 * weight.size + 18 * length * MODEL_WIDTH,
            transcendentals=0,
        ),
        compiler_params=pltpu.CompilerParams(vmem_limit_bytes=60 * MIB),
        name="leave",
    )(dqkv, tokens, dresidual, hidden, middle, mods, weight, up, down)


def layout(n_fsdp):
    return [(f // 4, f // 2 % 2, f % 2) for f in range(n_fsdp)]


def moved(n_fsdp, step):
    pairs = []
    for f, (z, x, c) in enumerate(layout(n_fsdp)):
        for y in range(2):
            to_z, to_x, to_c, to_y = step(z, x, c, y)
            pairs.append((2 * f + y, 2 * (4 * to_z + 2 * to_x + to_c) + to_y))
    return pairs


BOTH = ("fsdp", "seq")


def step_z(block, n_fsdp):
    depth = n_fsdp // 4
    by_shift = [block]
    for shift in range(1, depth):
        pairs = moved(n_fsdp, lambda z, x, c, y: ((z + shift) % depth, x, c, y))
        by_shift.append(lax.ppermute(block, BOTH, pairs))
    return jnp.stack(by_shift)


def step_first(block, n_fsdp):
    return lax.ppermute(
        block,
        BOTH,
        moved(n_fsdp, lambda z, x, c, y: (z, x, c, 1 - y) if c else (z, 1 - x, c, y)),
    )


def step_second(block, n_fsdp):
    return lax.ppermute(
        block,
        BOTH,
        moved(n_fsdp, lambda z, x, c, y: (z, 1 - x, c, y) if c else (z, x, c, 1 - y)),
    )


def step_core(block, n_fsdp):
    return lax.ppermute(block, BOTH, moved(n_fsdp, lambda z, x, c, y: (z, x, 1 - c, y)))


def behind(block, *earlier):
    for array in earlier:
        element = lax.slice(array, [n - 1 for n in array.shape], array.shape).reshape(())
        element = element.astype(jnp.float32)
        block = block + jnp.minimum(jnp.abs(element), 0.0).astype(block.dtype)
    return block


def gather_late(block, n_fsdp, place, told):
    line = behind(step_z(block, n_fsdp), told)
    near = jnp.stack([line, step_first(line, n_fsdp)])
    far = step_second(near, n_fsdp)
    gathered = assemble(place, near, far, step_core(near, n_fsdp), step_core(far, n_fsdp))
    return gathered.reshape(2, n_fsdp * block.shape[0], block.shape[1])


DOWN_EDGES = (0, 1152, 2304, 3456, 4608, 9216)
UP_EDGES = (0, 6912, 10368, 11520, 16128, 17280)
PIECES = FF // HD


def piece_order(n_fsdp):
    per = PIECES // n_fsdp
    return [f * per + q for q in range(per) for f in range(n_fsdp)]


def unpack_kernel(came_ref, cond_ref, base_ref, *refs, order, down_chunk, up_chunk):
    bf16 = jnp.bfloat16
    outs, (down_all, up_all, mixed) = refs[:-3], refs[-3:]
    down_outs, up_outs, shrink_t, mod_ref, middle_ref = outs[:4], outs[4:9], *outs[9:]
    for f in range(came_ref.shape[0]):
        block = came_ref[f].astype(jnp.float32)
        down_all[:, f * down_chunk : (f + 1) * down_chunk] = block[:, :down_chunk]
        up_all[:, f * up_chunk : (f + 1) * up_chunk] = block[:, down_chunk:]
    middle = jnp.sum(down_all[:, :MODEL_WIDTH] * cond_ref[...], axis=1, keepdims=True)
    middle = middle.astype(bf16).astype(jnp.float32)
    middle_ref[...] = middle
    mod_ref[...] = jnp.zeros_like(mod_ref)
    for block in range(6):
        columns = slice(block * MODEL_WIDTH, (block + 1) * MODEL_WIDTH)
        mod_ref[block : block + 1] = base_ref[:, columns] + total(middle * up_all[:, columns])
    for target, out in enumerate(down_outs):
        out[...] = jnp.zeros_like(out)
        out[:RANK] = down_all[:, DOWN_EDGES[target] : DOWN_EDGES[target + 1]].astype(bf16)
    mixed[...] = jnp.zeros_like(mixed)
    for target, out in enumerate(up_outs):
        if target == 3:
            for to, piece in enumerate(order):
                at = UP_EDGES[3] + piece * HD
                mixed[:RANK, to * HD : (to + 1) * HD] = up_all[:, at : at + HD]
            out[...] = mixed[...].astype(bf16)
        else:
            out[...] = jnp.zeros_like(out)
            out[:RANK] = up_all[:, UP_EDGES[target] : UP_EDGES[target + 1]].astype(bf16)
    for to, piece in enumerate(order):
        at = DOWN_EDGES[4] + piece * HD
        mixed[:RANK, to * HD : (to + 1) * HD] = down_all[:, at : at + HD]
    for start in range(0, FF, MODEL_WIDTH):
        shrink_t[start : start + MODEL_WIDTH, :] = mixed[:, start : start + MODEL_WIDTH].T.astype(
            bf16
        )


def unpack(came, cond, base, order, down_chunk, up_chunk):
    bf16 = jnp.bfloat16
    widths = [DOWN_EDGES[t + 1] - DOWN_EDGES[t] for t in range(4)]
    widths += [UP_EDGES[t + 1] - UP_EDGES[t] for t in range(5)]
    return pl.pallas_call(
        functools.partial(
            unpack_kernel, order=order, down_chunk=down_chunk, up_chunk=up_chunk
        ),
        out_shape=[jax.ShapeDtypeStruct((LANES, w), bf16) for w in widths]
        + [
            jax.ShapeDtypeStruct((FF, LANES), bf16),
            jax.ShapeDtypeStruct((8, MODEL_WIDTH), jnp.float32),
            jax.ShapeDtypeStruct((RANK, 1), jnp.float32),
        ],
        scratch_shapes=[
            pltpu.VMEM((RANK, DOWN_EDGES[5]), jnp.float32),
            pltpu.VMEM((RANK, UP_EDGES[5]), jnp.float32),
            pltpu.VMEM((LANES, FF), jnp.float32),
        ],
        compiler_params=pltpu.CompilerParams(vmem_limit_bytes=48 * MIB),
        name="unpack",
    )(came, cond, base)


def pack_kernel(
    leave_ref,
    after_ref,
    middle_ref,
    cond_ref,
    down_ada_ref,
    up_ada_ref,
    down_qkv,
    up_qkv,
    down_proj,
    up_proj,
    down_expand,
    up_expand_low,
    up_expand_high,
    down_shrink_low,
    down_shrink_high,
    up_shrink,
    sent_ref,
    dmod_ref,
    own_ref,
    down_all,
    up_all,
    *,
    order,
    down_chunk,
    up_chunk,
):
    bf16, f32 = jnp.bfloat16, jnp.float32
    width = MODEL_WIDTH
    dmiddle = jnp.zeros((RANK, 1), f32)
    for block in range(6):
        source = leave_ref if block < 2 else after_ref
        line = source[block % 2 if block < 2 else block - 2, :].reshape(1, width)
        line = line.astype(bf16).astype(f32)
        columns = slice(block * width, (block + 1) * width)
        side, at = block // 3, block % 3 * width
        dmod_ref[side : side + 1, at : at + width] = line
        up_all[:, columns] = middle_ref[...] * line
        dmiddle += jnp.sum(up_ada_ref[:RANK, columns].astype(f32) * line, axis=1, keepdims=True)
    dmiddle = dmiddle.astype(bf16).astype(f32)
    down_all[:, :width] = dmiddle * cond_ref[...]
    own_ref[...] = total(dmiddle * down_ada_ref[:RANK].astype(f32))
    down_all[:, width : 2 * width] = down_qkv[...]
    down_all[:, 2 * width : 3 * width] = down_proj[...].T[:RANK]
    down_all[:, 3 * width : 4 * width] = down_expand[...]
    up_all[:, UP_EDGES[1] : UP_EDGES[2]] = up_qkv[...]
    up_all[:, UP_EDGES[2] : UP_EDGES[3]] = up_proj[...]
    up_all[:, UP_EDGES[4] : UP_EDGES[5]] = up_shrink[...]
    half = PIECES // 2
    for at, piece in enumerate(order):
        ups = up_expand_low if at < half else up_expand_high
        downs = down_shrink_low if at < half else down_shrink_high
        columns = slice((at % half) * HD, (at % half + 1) * HD)
        to = UP_EDGES[3] + piece * HD
        up_all[:, to : to + HD] = ups[:, columns]
        to = DOWN_EDGES[4] + piece * HD
        down_all[:, to : to + HD] = downs[:, columns]
    for f in range(sent_ref.shape[0]):
        sent_ref[f, :, :down_chunk] = down_all[:, f * down_chunk : (f + 1) * down_chunk].astype(bf16)
        sent_ref[f, :, down_chunk:] = up_all[:, f * up_chunk : (f + 1) * up_chunk].astype(bf16)


def pack(operands, n_fsdp, order, down_chunk, up_chunk):
    bf16, f32 = jnp.bfloat16, jnp.float32
    return pl.pallas_call(
        functools.partial(pack_kernel, order=order, down_chunk=down_chunk, up_chunk=up_chunk),
        out_shape=[
            jax.ShapeDtypeStruct((n_fsdp, RANK, down_chunk + up_chunk), bf16),
            jax.ShapeDtypeStruct((2, 3 * MODEL_WIDTH), f32),
            jax.ShapeDtypeStruct((1, MODEL_WIDTH), f32),
        ],
        scratch_shapes=[
            pltpu.VMEM((RANK, DOWN_EDGES[5]), f32),
            pltpu.VMEM((RANK, UP_EDGES[5]), f32),
        ],
        compiler_params=pltpu.CompilerParams(vmem_limit_bytes=48 * MIB),
        name="pack",
    )(*operands)


def owners_kernel(ids_ref, place_ref, came_ref, kept_ref, given_ref, sums):
    sums[...] = jnp.zeros_like(sums)
    for f in range(came_ref.shape[0]):
        sums[ids_ref[f]] += came_ref[f].astype(jnp.float32)
    held = kept_ref.shape[0]
    mine = place_ref[3]
    for index in range(held):
        kept_ref[index] = sums[mine * held + index]
        given_ref[index] = sums[(1 - mine) * held + index].astype(jnp.bfloat16)


def owners(ids, place, came):
    held = ADAPTER_COUNT // 2
    shape = (held,) + came.shape[1:]
    return pl.pallas_call(
        owners_kernel,
        in_specs=[
            pl.BlockSpec(memory_space=pltpu.SMEM),
            pl.BlockSpec(memory_space=pltpu.SMEM),
            pl.BlockSpec(memory_space=pltpu.VMEM),
        ],
        out_shape=[
            jax.ShapeDtypeStruct(shape, jnp.float32),
            jax.ShapeDtypeStruct(shape, jnp.bfloat16),
        ],
        scratch_shapes=[pltpu.VMEM((ADAPTER_COUNT,) + came.shape[1:], jnp.float32)],
        compiler_params=pltpu.CompilerParams(vmem_limit_bytes=32 * MIB),
        name="owners",
    )(ids, place, came)


def update_kernel(gradient_ref, squared_ref, *refs):
    down_chunk = refs[0].shape[-1]
    grad_norm = jnp.sqrt(jnp.sum(squared_ref[:, :1], axis=0, keepdims=True))
    clip_factor = jnp.minimum(1.0, clip_limit / (grad_norm + norm_eps))
    ins, outs, norm_ref = refs[:6], refs[6:12], refs[12]
    norm_ref[...] = jnp.broadcast_to(grad_norm, norm_ref.shape)
    for kind in range(2):
        part = slice(0, down_chunk) if kind == 0 else slice(down_chunk, None)
        for index in range(gradient_ref.shape[0]):
            gradient = gradient_ref[index, :, part] * clip_factor
            params = ins[kind][index]
            moment_new = beta_first * ins[2 + kind][index] + (1.0 - beta_first) * gradient
            square_new = (
                beta_second * ins[4 + kind][index] + (1.0 - beta_second) * gradient * gradient
            )
            direction = (
                moment_new
                / (1.0 - beta_first**STEP)
                / (jnp.sqrt(square_new / (1.0 - beta_second**STEP)) + adam_eps)
            )
            outs[kind][index] = params - learn_rate * (direction + decay_rate * params)
            outs[2 + kind][index] = moment_new
            outs[4 + kind][index] = square_new


def update(gradient, squared, states):
    f32 = jnp.float32
    outs = pl.pallas_call(
        update_kernel,
        out_shape=[jax.ShapeDtypeStruct(s.shape, f32) for s in states]
        + [jax.ShapeDtypeStruct((8, LANES), f32)],
        compiler_params=pltpu.CompilerParams(vmem_limit_bytes=32 * MIB),
        name="update",
    )(gradient, squared, *states)
    return outs[:6], outs[6][0, 0]


def fits(mesh):
    return mesh.shape["seq"] == MB and mesh.shape["fsdp"] == 16


def dot(equation, left, right):
    return jnp.einsum(equation, left, right, preferred_element_type=jnp.float32)


def swap(block):
    return lax.ppermute(block, "seq", [(0, 1), (1, 0)])


def by_seq(own, other, mine):
    first = mine == 0
    return jnp.stack([jnp.where(first, own, other), jnp.where(first, other, own)])


def swap_rows(halves, mine):
    kept, came = send_row(halves, mine)
    return by_seq(kept, came, mine)


def send_row(halves, mine):
    sent = lax.dynamic_index_in_dim(halves, 1 - mine, 0, False)
    return lax.dynamic_index_in_dim(halves, mine, 0, False), swap(sent)


def to_all(block):
    return lax.all_to_all(block, ("fsdp", "seq"), split_axis=0, concat_axis=0, tiled=True)


def to_fsdp(block):
    return lax.all_to_all(block, "fsdp", split_axis=0, concat_axis=0, tiled=True)


def fast_shards(
    tokens,
    condition,
    adapter,
    cotangent,
    modulation_weight,
    modulation_bias,
    query_key_value_weight,
    attention_out_weight,
    attention_out_bias,
    widen_weight,
    widen_bias,
    narrow_weight,
    narrow_bias,
    lowrank_down,
    lowrank_up,
    first_moment_down,
    first_moment_up,
    second_moment_down,
    second_moment_up,
):
    bf16 = jnp.bfloat16
    n_fsdp = lax.axis_size("fsdp")
    mine = lax.axis_index("seq")
    row = lax.axis_index("fsdp")
    place = jnp.stack([row // 4, row // 2 % 2, row % 2, mine]).astype(jnp.int32)
    down_chunk, up_chunk = lowrank_down.shape[-1], lowrank_up.shape[-1]
    depth = modulation_weight.shape[0]
    order = piece_order(n_fsdp)
    per = PIECES // n_fsdp

    cond_act_pair = jax.nn.silu(condition).astype(bf16)
    told = jnp.moveaxis(cond_act_pair.reshape(MB, n_fsdp, depth), 1, 0)
    numbers = jnp.broadcast_to(adapter.astype(bf16)[None, :, None], (n_fsdp, MB, 8))
    told = to_fsdp(jnp.concatenate([told, numbers], 2))
    own_ids = lax.dynamic_index_in_dim(told[:, :, depth], mine, 1, False).astype(jnp.int32)

    wide = jnp.moveaxis(widen_weight.reshape(depth, -1, per, HD), 2, 0).reshape(per, depth, HALF)
    narrow = narrow_weight.reshape(per, depth, HALF)

    def whole(block):
        return lax.all_gather(block, "fsdp", axis=0, tiled=True)

    heads = jnp.concatenate([query_key_value_weight, attention_out_weight], 1)
    heads = by_seq(heads, swap(heads), mine)
    cut = query_key_value_weight.shape[1]
    heads_weight = whole(
        jnp.concatenate([heads[0, :, :cut], heads[1, :, :cut], heads[0, :, cut:], heads[1, :, cut:]], 1)
    )
    joined = [jnp.concatenate([wide[q], narrow[q]], 1) for q in range(per)]
    low = jnp.concatenate(joined[: per // 2], 1)
    low = by_seq(low, swap(low), mine)
    low_weight = whole(jnp.concatenate([low[0], low[1]], 1))
    high_weight = gather_late(jnp.concatenate(joined[per // 2 :], 1), n_fsdp, place, told)

    portions = jnp.concatenate([lowrank_down.astype(bf16), lowrank_up.astype(bf16)], -1)
    others = swap(portions)
    table = by_seq(portions, others, mine).reshape(ADAPTER_COUNT, RANK, -1)
    picks = jax.nn.one_hot(own_ids, ADAPTER_COUNT, dtype=bf16)
    chosen = dot("fa,arc->frc", picks, table).astype(bf16)
    spoken = told[:, :, :depth].reshape(n_fsdp * MB, depth)
    mod_part = to_all(dot("si,io->so", spoken, modulation_weight))
    mod_base = jnp.sum(mod_part.reshape(n_fsdp, MB, -1), axis=0).reshape(1, -1)
    cond_act = lax.dynamic_slice_in_dim(cond_act_pair, mine, 1, 0).astype(jnp.float32)
    parts = unpack(
        to_fsdp(chosen), cond_act, mod_base + modulation_bias, order, down_chunk, up_chunk
    )
    down_ada, down_qkv, down_proj, down_expand = parts[:4]
    up_ada, up_qkv, up_proj, up_expand, up_shrink = parts[4:9]
    down_shrink_t, mods, middle_ada = parts[9:]

    length = MB * tokens.shape[1]
    token_rows = swap_rows(tokens, mine).reshape(length, MODEL_WIDTH)
    cot_rows = swap_rows(cotangent, mine).reshape(length, MODEL_WIDTH)

    hidden, middle_qkv, qkv = entry(token_rows, mods, heads_weight, up_qkv, down_qkv)
    mixed_heads, log_total = heads_forward(qkv, step=length)
    mixed = mixed_heads.reshape(MODEL_WIDTH, length)
    second, dfinal, branch, middles = before_feed(
        mixed,
        token_rows,
        cot_rows,
        mods,
        heads_weight,
        up_proj,
        down_proj,
        down_expand,
        up_shrink,
        attention_out_bias[None],
    )
    bias = jnp.moveaxis(widen_bias.reshape(n_fsdp, per, HD), 0, 1).reshape(1, FF)
    cut = FF // 2
    final, dsecond, up_expand_low, down_shrink_low = feed(
        second,
        dfinal,
        middles,
        low_weight,
        up_expand[:, :cut],
        down_shrink_t[:cut],
        bias[:, :cut],
        None,
    )
    final, dsecond, up_expand_high, down_shrink_high = feed(
        second,
        dfinal,
        middles,
        high_weight,
        up_expand[:, cut:],
        down_shrink_t[cut:],
        bias[:, cut:],
        (final, dsecond),
    )
    (
        block_rows,
        d_residual,
        d_mixed,
        after_sums,
        up_shrink_grad,
        down_expand_grad,
        up_proj_grad,
        down_proj_grad,
    ) = after_feed(
        final,
        dsecond,
        token_rows,
        cot_rows,
        branch,
        second,
        dfinal,
        mixed,
        middles,
        mods,
        heads_weight,
        up_proj,
        down_proj,
        down_expand,
        up_shrink,
        narrow_bias[None],
    )
    block_out = swap_rows(block_rows.reshape(tokens.shape), mine)
    d_qkv = heads_back(
        qkv, d_mixed.reshape(HEADS, HD, length), mixed_heads, log_total, step=length
    )
    token_rows_grad, leave_sums, up_qkv_grad, down_qkv_grad = leave(
        d_qkv, token_rows, d_residual, hidden, middle_qkv, mods, heads_weight, up_qkv, down_qkv
    )

    sent, d_modulation, own_cond = pack(
        (
            leave_sums,
            after_sums,
            middle_ada,
            cond_act,
            down_ada,
            up_ada,
            down_qkv_grad,
            up_qkv_grad,
            down_proj_grad,
            up_proj_grad,
            down_expand_grad,
            up_expand_low,
            up_expand_high,
            down_shrink_low,
            down_shrink_high,
            up_shrink_grad,
        ),
        n_fsdp,
        order,
        down_chunk,
        up_chunk,
    )
    kept, given = owners(own_ids, place, to_fsdp(sent))
    gradient = kept + swap(given).astype(jnp.float32)
    squared = to_all(jnp.broadcast_to(jnp.sum(gradient * gradient), (n_fsdp * MB, LANES)))

    half_weight = lax.all_gather(
        behind(modulation_weight, second), "fsdp", axis=0, tiled=True
    )
    both_mod = behind(swap_rows(d_modulation.astype(bf16), mine), kept)
    d_cond = dot("so,io->si", both_mod, half_weight)
    d_cond = d_cond + jnp.where(jnp.arange(MB)[:, None] == mine, own_cond, 0.0)
    d_cond = d_cond + swap(d_cond)
    cond_grad = jax.vjp(jax.nn.silu, condition)[1](d_cond)[0]
    token_kept, token_came = send_row(token_rows_grad.reshape(tokens.shape), mine)
    token_grad = by_seq(behind(token_kept, gradient), token_came, mine).astype(jnp.float32)

    states = (
        lowrank_down,
        lowrank_up,
        first_moment_down,
        first_moment_up,
        second_moment_down,
        second_moment_up,
    )
    fresh, grad_norm = update(gradient, squared, states)
    return (block_out, token_grad, cond_grad, grad_norm, *fresh)


def solution(mesh):
    in_specs = (
        P("fsdp", "seq", None),
        P("fsdp", None),
        P("fsdp"),
        P("fsdp", "seq", None),
        P("fsdp", "seq"),
        P(),
        P("fsdp", "seq"),
        P("fsdp", "seq"),
        P(),
        P("fsdp", "seq"),
        P(),
        P("fsdp", "seq"),
        P(),
        P("seq", None, "fsdp"),
        P("seq", None, "fsdp"),
        P("seq", None, "fsdp"),
        P("seq", None, "fsdp"),
        P("seq", None, "fsdp"),
        P("seq", None, "fsdp"),
    )
    out_specs = (
        P("fsdp", "seq", None),
        P("fsdp", "seq", None),
        P("fsdp", None),
        P(),
        P("seq", None, "fsdp"),
        P("seq", None, "fsdp"),
        P("seq", None, "fsdp"),
        P("seq", None, "fsdp"),
        P("seq", None, "fsdp"),
        P("seq", None, "fsdp"),
    )
    body = fast_shards if fits(mesh) else shards
    return jax.shard_map(body, mesh=mesh, in_specs=in_specs, out_specs=out_specs, check_vma=False)
```

```python
import functools

import jax
import jax.numpy as jnp
from jax import lax
from jax.experimental import pallas as pl
from jax.experimental.pallas import tpu as pltpu
from jax.sharding import PartitionSpec as P

MODEL_WIDTH = 1152
HD = 72
FF = 4608
ADAPTER_RANK = 16
ADAPTER_COUNT = 8
MB = 2
SEQ_MB = 1
STEP = 10


beta_first = 0.9
beta_second = 0.999
learn_rate = 0.05
decay_rate = 0.1
adam_eps = 1e-08
clip_limit = 1.0
norm_eps = 1e-06
pair_heads = 2
highest = lax.Precision.HIGHEST


def linear(inputs, weight):
    return jnp.einsum("sti,io->sto", inputs, weight, preferred_element_type=jnp.float32)


def linear_back(gradient, weight):
    return jnp.einsum("sto,io->sti", gradient, weight, preferred_element_type=jnp.float32)


def normalize(stream):
    center = stream - jnp.mean(stream, -1, keepdims=True)
    inverse = lax.rsqrt(jnp.mean(center * center, -1, keepdims=True) + norm_eps)
    return (center * inverse, inverse)


def normalize_back(gradient, normed, inverse):
    return inverse * (
        gradient
        - jnp.mean(gradient, -1, keepdims=True)
        - normed * jnp.mean(gradient * normed, -1, keepdims=True)
    )


def adapt_forward(inputs, down_part, up_part):
    middle = jnp.einsum(
        "sti,sri->str", inputs, down_part, preferred_element_type=jnp.float32
    ).astype(jnp.bfloat16)
    return (middle, jnp.einsum("str,sro->sto", middle, up_part, preferred_element_type=jnp.float32))


def adapt_backward(inputs, middle, gradient, down_part, up_part):
    up_grad = jnp.einsum("str,sto->sro", middle, gradient, preferred_element_type=jnp.float32)
    middle_grad = jnp.einsum(
        "sto,sro->str", gradient, up_part, preferred_element_type=jnp.float32
    ).astype(jnp.bfloat16)
    down_grad = jnp.einsum("str,sti->sri", middle_grad, inputs, preferred_element_type=jnp.float32)
    input_grad = jnp.einsum(
        "str,sri->sti", middle_grad, down_part, preferred_element_type=jnp.float32
    )
    return (input_grad, down_grad, up_grad)


def grouped(matrix):
    seq_count, row_count, col_count = matrix.shape
    return jnp.moveaxis(
        matrix.reshape(seq_count, row_count, col_count // (pair_heads * HD), pair_heads, HD), 2, 0
    )


def ungrouped(stacked):
    moved = jnp.moveaxis(stacked, 0, 2)
    return moved.reshape(moved.shape[0], moved.shape[1], -1)


def attend_group(group_inputs):
    queries, all_keys, all_values = group_inputs
    factor = queries.shape[-1] ** (-0.5)
    scores = (
        jnp.einsum("sqhd,skhd->shqk", queries, all_keys, preferred_element_type=jnp.float32)
        * factor
    )
    row_max = jnp.max(scores, -1, keepdims=True)
    exponent = jnp.exp(scores - row_max)
    row_total = jnp.sum(exponent, -1, keepdims=True)
    weights = (exponent / row_total).astype(jnp.bfloat16)
    mixed_heads = jnp.einsum(
        "shqk,skhd->sqhd", weights, all_values, preferred_element_type=jnp.float32
    )
    return (mixed_heads, row_max + jnp.log(row_total))


def attend_back(group_inputs):
    queries, all_keys, all_values, d_mixed, log_total = group_inputs
    factor = queries.shape[-1] ** (-0.5)
    scores = (
        jnp.einsum("sqhd,skhd->shqk", queries, all_keys, preferred_element_type=jnp.float32)
        * factor
    )
    probable = jnp.exp(scores - log_total)
    d_values = jnp.einsum(
        "shqk,sqhd->skhd",
        probable.astype(jnp.bfloat16),
        d_mixed,
        preferred_element_type=jnp.float32,
    )
    d_weights = jnp.einsum(
        "sqhd,skhd->shqk", d_mixed, all_values, preferred_element_type=jnp.float32
    )
    inner_sum = jnp.sum(d_weights * probable, -1, keepdims=True)
    d_scores = (probable * (d_weights - inner_sum) * factor).astype(jnp.bfloat16)
    d_queries = jnp.einsum(
        "shqk,skhd->sqhd", d_scores, all_keys, preferred_element_type=jnp.float32
    )
    d_keys = jnp.einsum("shqk,sqhd->skhd", d_scores, queries, preferred_element_type=jnp.float32)
    return (d_queries, d_keys, d_values)


def gelu_tanh(inner_act):
    return jax.nn.gelu(inner_act, approximate=True)


def shards(
    tokens,
    condition,
    adapter,
    cotangent,
    modulation_weight,
    modulation_bias,
    query_key_value_weight,
    attention_out_weight,
    attention_out_bias,
    widen_weight,
    widen_bias,
    narrow_weight,
    narrow_bias,
    lowrank_down,
    lowrank_up,
    first_moment_down,
    first_moment_up,
    second_moment_down,
    second_moment_up,
):
    seq_count_axis = lax.axis_size("seq")
    seq_share = 1.0 / seq_count_axis
    down_portion = lowrank_down.astype(jnp.bfloat16)
    up_portion = lowrank_up.astype(jnp.bfloat16)
    down_edges = (
        0,
        MODEL_WIDTH,
        2 * MODEL_WIDTH,
        3 * MODEL_WIDTH,
        4 * MODEL_WIDTH,
        4 * MODEL_WIDTH + FF,
    )
    up_edges = (
        0,
        6 * MODEL_WIDTH,
        9 * MODEL_WIDTH,
        10 * MODEL_WIDTH,
        10 * MODEL_WIDTH + FF,
        11 * MODEL_WIDTH + FF,
    )

    def fetch():
        across = (
            lax.all_gather(modulation_weight, "seq", axis=1, tiled=True),
            lax.all_gather(query_key_value_weight, "seq", axis=1, tiled=True),
            lax.all_gather(attention_out_weight, "seq", axis=1, tiled=True),
            lax.all_gather(widen_weight, "seq", axis=1, tiled=True),
            lax.all_gather(narrow_weight, "seq", axis=1, tiled=True),
            lax.all_gather(down_portion, "seq", axis=0, tiled=True),
            lax.all_gather(up_portion, "seq", axis=0, tiled=True),
        )
        return (
            lax.all_gather(across[0], "fsdp", axis=0, tiled=True),
            lax.all_gather(across[1], "fsdp", axis=0, tiled=True),
            lax.all_gather(across[2], "fsdp", axis=0, tiled=True),
            lax.all_gather(across[3], "fsdp", axis=0, tiled=True),
            lax.all_gather(across[4], "fsdp", axis=0, tiled=True),
            lax.all_gather(across[5], "fsdp", axis=2, tiled=True),
            lax.all_gather(across[6], "fsdp", axis=2, tiled=True),
        )

    def select(gathered_now, picked_adapter):
        down_sel = gathered_now[5][picked_adapter]
        up_sel = gathered_now[6][picked_adapter]
        down_blocks = [
            down_sel[:, :, down_edges[target] : down_edges[target + 1]] for target in range(5)
        ]
        up_blocks = [up_sel[:, :, up_edges[target] : up_edges[target + 1]] for target in range(5)]
        return (
            gathered_now[0],
            gathered_now[1],
            gathered_now[2],
            gathered_now[3],
            gathered_now[4],
            down_blocks,
            up_blocks,
        )

    down_gradient = jnp.zeros((ADAPTER_COUNT, ADAPTER_RANK, down_edges[5]), jnp.float32)
    up_gradient = jnp.zeros((ADAPTER_COUNT, ADAPTER_RANK, up_edges[5]), jnp.float32)
    output_list, token_list, cond_list = ([], [], [])
    for micro_batch in range(MB):
        first_seq = micro_batch * SEQ_MB
        token_rows = tokens[first_seq : first_seq + SEQ_MB].astype(jnp.float32)
        cond_rows = condition[first_seq : first_seq + SEQ_MB]
        picked_adapter = adapter[first_seq : first_seq + SEQ_MB]
        cot_rows = cotangent[first_seq : first_seq + SEQ_MB].astype(jnp.float32)
        batch_seqs = token_rows.shape[0]
        local_rows = token_rows.shape[1]
        gathered = fetch()
        full_ada, full_qkv, full_proj, full_expand, full_shrink, down_blocks, up_blocks = select(
            gathered, picked_adapter
        )
        cond_act = jax.nn.silu(cond_rows).astype(jnp.bfloat16)[:, None, :]
        middle_ada, extra_ada = adapt_forward(cond_act, down_blocks[0], up_blocks[0])
        modulation = linear(cond_act, full_ada) + modulation_bias + extra_ada
        shift_first, scale_first, gate_first, shift_second, scale_second, gate_second = jnp.split(
            modulation, 6, axis=-1
        )
        normed_first, inverse_first = normalize(token_rows)
        hidden = (normed_first * (1.0 + scale_first) + shift_first).astype(jnp.bfloat16)
        middle_qkv, extra_qkv = adapt_forward(hidden, down_blocks[1], up_blocks[1])
        packed = (linear(hidden, full_qkv) + extra_qkv).astype(jnp.bfloat16)
        head_blocks = packed.reshape(
            batch_seqs, local_rows, 3, seq_count_axis, MODEL_WIDTH // seq_count_axis
        )
        by_heads = lax.all_to_all(head_blocks, "seq", split_axis=3, concat_axis=1, tiled=True)
        query_groups = grouped(by_heads[:, :, 0, 0])
        key_groups = grouped(by_heads[:, :, 1, 0])
        value_groups = grouped(by_heads[:, :, 2, 0])
        mixed_groups, log_total = lax.map(attend_group, (query_groups, key_groups, value_groups))
        mixed = lax.all_to_all(
            ungrouped(mixed_groups).astype(jnp.bfloat16),
            "seq",
            split_axis=1,
            concat_axis=2,
            tiled=True,
        )
        middle_proj, extra_proj = adapt_forward(mixed, down_blocks[2], up_blocks[2])
        branch = linear(mixed, full_proj) + attention_out_bias + extra_proj
        residual = token_rows + gate_first * branch
        normed_second, inverse_second = normalize(residual)
        second = (normed_second * (1.0 + scale_second) + shift_second).astype(jnp.bfloat16)
        middle_expand, extra_expand = adapt_forward(second, down_blocks[3], up_blocks[3])
        inner_act = linear(second, full_expand) + widen_bias + extra_expand
        active = gelu_tanh(inner_act).astype(jnp.bfloat16)
        middle_shrink, extra_shrink = adapt_forward(active, down_blocks[4], up_blocks[4])
        final_out = linear(active, full_shrink) + narrow_bias + extra_shrink
        output_list.append((residual + gate_second * final_out).astype(jnp.bfloat16))
        gathered = fetch()
        full_ada, full_qkv, full_proj, full_expand, full_shrink, down_blocks, up_blocks = select(
            gathered, picked_adapter
        )
        d_final = (gate_second * cot_rows).astype(jnp.bfloat16)
        d_gate_second = jnp.sum(cot_rows * final_out, axis=1, keepdims=True)
        d_active, down_shrink, up_shrink = adapt_backward(
            active, middle_shrink, d_final, down_blocks[4], up_blocks[4]
        )
        d_active = d_active + linear_back(d_final, full_shrink)
        d_inner = jax.vjp(gelu_tanh, inner_act)[1](d_active)[0].astype(jnp.bfloat16)
        d_second, down_expand, up_expand = adapt_backward(
            second, middle_expand, d_inner, down_blocks[3], up_blocks[3]
        )
        d_second = d_second + linear_back(d_inner, full_expand)
        d_shift_second = jnp.sum(d_second, axis=1, keepdims=True)
        d_scale_second = jnp.sum(d_second * normed_second, axis=1, keepdims=True)
        d_residual = cot_rows + normalize_back(
            d_second * (1.0 + scale_second), normed_second, inverse_second
        )
        d_branch = (gate_first * d_residual).astype(jnp.bfloat16)
        d_gate_first = jnp.sum(d_residual * branch, axis=1, keepdims=True)
        d_mixed, down_proj, up_proj = adapt_backward(
            mixed, middle_proj, d_branch, down_blocks[2], up_blocks[2]
        )
        d_mixed = (d_mixed + linear_back(d_branch, full_proj)).astype(jnp.bfloat16)
        d_by_heads = lax.all_to_all(d_mixed, "seq", split_axis=2, concat_axis=1, tiled=True)
        dquery_groups, dkey_groups, dvalue_groups = lax.map(
            attend_back, (query_groups, key_groups, value_groups, grouped(d_by_heads), log_total)
        )
        stacked = jnp.stack(
            [
                ungrouped(dquery_groups).astype(jnp.bfloat16),
                ungrouped(dkey_groups).astype(jnp.bfloat16),
                ungrouped(dvalue_groups).astype(jnp.bfloat16),
            ],
            2,
        )[:, :, :, None, :]
        returned = lax.all_to_all(stacked, "seq", split_axis=1, concat_axis=3, tiled=True)
        d_packed = returned.reshape(batch_seqs, local_rows, 3 * MODEL_WIDTH)
        d_hidden, down_qkv, up_qkv = adapt_backward(
            hidden, middle_qkv, d_packed, down_blocks[1], up_blocks[1]
        )
        d_hidden = d_hidden + linear_back(d_packed, full_qkv)
        d_shift_first = jnp.sum(d_hidden, axis=1, keepdims=True)
        d_scale_first = jnp.sum(d_hidden * normed_first, axis=1, keepdims=True)
        token_list.append(
            d_residual + normalize_back(d_hidden * (1.0 + scale_first), normed_first, inverse_first)
        )
        partial_mod = jnp.concatenate(
            [
                d_shift_first,
                d_scale_first,
                d_gate_first,
                d_shift_second,
                d_scale_second,
                d_gate_second,
            ],
            -1,
        )
        d_modulation = lax.psum(partial_mod, "seq").astype(jnp.bfloat16)
        d_cond_act, down_ada, up_ada = adapt_backward(
            cond_act, middle_ada, d_modulation, down_blocks[0], up_blocks[0]
        )
        d_cond_act = d_cond_act + linear_back(d_modulation, full_ada)
        cond_list.append(jax.vjp(jax.nn.silu, cond_rows)[1](d_cond_act[:, 0, :])[0])
        seq_down = jnp.concatenate(
            [down_ada * seq_share, down_qkv, down_proj, down_expand, down_shrink], -1
        )
        seq_up = jnp.concatenate([up_ada * seq_share, up_qkv, up_proj, up_expand, up_shrink], -1)
        selector = jax.nn.one_hot(picked_adapter, ADAPTER_COUNT, dtype=jnp.float32)
        down_gradient = down_gradient + jnp.einsum(
            "sa,src->arc", selector, seq_down, precision=highest
        )
        up_gradient = up_gradient + jnp.einsum("sa,src->arc", selector, seq_up, precision=highest)
    part_down, part_up = (
        lax.psum_scatter(down_gradient, "fsdp", scatter_dimension=2, tiled=True),
        lax.psum_scatter(up_gradient, "fsdp", scatter_dimension=2, tiled=True),
    )
    sequence_down, sequence_up = (
        lax.psum_scatter(
            part_down.astype(jnp.bfloat16), "seq", scatter_dimension=0, tiled=True
        ).astype(jnp.float32),
        lax.psum_scatter(
            part_up.astype(jnp.bfloat16), "seq", scatter_dimension=0, tiled=True
        ).astype(jnp.float32),
    )
    squared = lax.psum(
        jnp.sum(sequence_down * sequence_down) + jnp.sum(sequence_up * sequence_up), ("fsdp", "seq")
    )
    grad_norm = jnp.sqrt(squared)
    clip_factor = jnp.minimum(1.0, clip_limit / (grad_norm + norm_eps))

    def optimizer_update(params, gradient, moment, square):
        gradient = gradient * clip_factor
        moment_new = beta_first * moment + (1.0 - beta_first) * gradient
        square_new = beta_second * square + (1.0 - beta_second) * gradient * gradient
        direction = (
            moment_new
            / (1.0 - beta_first**STEP)
            / (jnp.sqrt(square_new / (1.0 - beta_second**STEP)) + adam_eps)
        )
        return (params - learn_rate * (direction + decay_rate * params), moment_new, square_new)

    stepped_down, next_first_down, next_second_down = optimizer_update(
        lowrank_down, sequence_down, first_moment_down, second_moment_down
    )
    stepped_up, next_first_up, next_second_up = optimizer_update(
        lowrank_up, sequence_up, first_moment_up, second_moment_up
    )
    block_out = jnp.concatenate(output_list, 0)
    token_grad = jnp.concatenate(token_list, 0)
    cond_grad = jnp.concatenate(cond_list, 0)
    return (
        block_out,
        token_grad,
        cond_grad,
        grad_norm,
        stepped_down,
        stepped_up,
        next_first_down,
        next_first_up,
        next_second_down,
        next_second_up,
    )


HEADS = 16
LOG2E = 1.4426950408889634
SCORE_SCALE = HD ** (-0.5)


def tn(left, right):
    return lax.dot_general(left, right, (((0,), (0,)), ((), ())), preferred_element_type=jnp.float32)


def nn(left, right):
    return lax.dot_general(left, right, (((1,), (0,)), ((), ())), preferred_element_type=jnp.float32)


def nt(left, right):
    return lax.dot_general(left, right, (((1,), (1,)), ((), ())), preferred_element_type=jnp.float32)


def heads_kernel(qkv_ref, mixed_ref, log_ref, *, step):
    length = qkv_ref.shape[-1]
    keys = qkv_ref[1, 0].astype(jnp.float32).T.astype(jnp.bfloat16)
    values_t = qkv_ref[2, 0]
    for start in range(0, length, step):
        queries_t = qkv_ref[0, 0, :, start : start + step]
        scores = nn(keys, queries_t) * (SCORE_SCALE * LOG2E)
        top = jnp.max(scores, axis=0, keepdims=True)
        exponent = jnp.exp2(scores - top)
        total = jnp.sum(exponent, axis=0, keepdims=True)
        weights = (exponent * (1.0 / total)).astype(jnp.bfloat16)
        mixed_ref[0, :, start : start + step] = nn(values_t, weights).astype(jnp.bfloat16)
        log_ref[0, :, start : start + step] = top + jnp.log2(total)


def heads_forward(qkv, step=256):
    _, heads, width, length = qkv.shape
    return pl.pallas_call(
        functools.partial(heads_kernel, step=step),
        grid=(heads,),
        in_specs=[pl.BlockSpec((3, 1, width, length), lambda h: (0, h, 0, 0))],
        out_specs=[
            pl.BlockSpec((1, width, length), lambda h: (h, 0, 0)),
            pl.BlockSpec((1, 1, length), lambda h: (h, 0, 0)),
        ],
        out_shape=[
            jax.ShapeDtypeStruct((heads, width, length), jnp.bfloat16),
            jax.ShapeDtypeStruct((heads, 1, length), jnp.float32),
        ],
        cost_estimate=pl.CostEstimate(
            flops=4 * heads * length * length * 256,
            bytes_accessed=10 * heads * width * length,
            transcendentals=heads * length * length,
        ),
        compiler_params=pltpu.CompilerParams(vmem_limit_bytes=48 * 1024 * 1024),
        name="heads_forward",
    )(qkv)


def heads_back_kernel(
    qkv_ref, grad_ref, mixed_ref, log_ref, out_ref, key_acc, value_acc, *, step
):
    length = qkv_ref.shape[-1]
    keys_t = qkv_ref[1, 0]
    keys = keys_t.astype(jnp.float32).T.astype(jnp.bfloat16)
    values = qkv_ref[2, 0].astype(jnp.float32).T.astype(jnp.bfloat16)
    for start in range(0, length, step):
        queries_t = qkv_ref[0, 0, :, start : start + step]
        grad_t = grad_ref[0, :, start : start + step]
        queries = queries_t.astype(jnp.float32).T.astype(jnp.bfloat16)
        grad = grad_t.astype(jnp.float32).T.astype(jnp.bfloat16)
        scores = nn(keys, queries_t) * (SCORE_SCALE * LOG2E)
        probable = jnp.exp2(scores - log_ref[0, :, start : start + step])
        d_weights = nn(values, grad_t)
        inner_sum = jnp.sum(
            grad_t.astype(jnp.float32) * mixed_ref[0, :, start : start + step].astype(jnp.float32),
            axis=0,
            keepdims=True,
        )
        d_scores = (probable * (d_weights - inner_sum)).astype(jnp.bfloat16)
        d_values = nn(probable.astype(jnp.bfloat16), grad)
        d_keys = nn(d_scores, queries)
        if start == 0:
            value_acc[...] = d_values
            key_acc[...] = d_keys
        else:
            value_acc[...] += d_values
            key_acc[...] += d_keys
        out_ref[0, 0, :, start : start + step] = (nn(keys_t, d_scores) * SCORE_SCALE).astype(
            jnp.bfloat16
        )
    out_ref[1, 0] = (key_acc[...] * SCORE_SCALE).T.astype(jnp.bfloat16)
    out_ref[2, 0] = value_acc[...].T.astype(jnp.bfloat16)


def heads_back(qkv, grad, mixed, log_total, step=256):
    _, heads, width, length = qkv.shape
    return pl.pallas_call(
        functools.partial(heads_back_kernel, step=step),
        grid=(heads,),
        in_specs=[
            pl.BlockSpec((3, 1, width, length), lambda h: (0, h, 0, 0)),
            pl.BlockSpec((1, width, length), lambda h: (h, 0, 0)),
            pl.BlockSpec((1, width, length), lambda h: (h, 0, 0)),
            pl.BlockSpec((1, 1, length), lambda h: (h, 0, 0)),
        ],
        out_specs=pl.BlockSpec((3, 1, width, length), lambda h: (0, h, 0, 0)),
        out_shape=jax.ShapeDtypeStruct((3, heads, width, length), jnp.bfloat16),
        scratch_shapes=[
            pltpu.VMEM((length, width), jnp.float32),
            pltpu.VMEM((length, width), jnp.float32),
        ],
        cost_estimate=pl.CostEstimate(
            flops=10 * heads * length * length * 256,
            bytes_accessed=16 * heads * width * length,
            transcendentals=heads * length * length,
        ),
        compiler_params=pltpu.CompilerParams(vmem_limit_bytes=60 * 1024 * 1024),
        name="heads_back",
    )(qkv, grad, mixed, log_total)


RANK = ADAPTER_RANK
LANES = 128
PADDED = MODEL_WIDTH + LANES
HALF = MODEL_WIDTH // 2
MIB = 1024 * 1024


def transposed(block):
    return block.astype(jnp.float32).T


def once(shape):
    return pl.BlockSpec(shape, lambda *_: (0,) * len(shape), pipeline_mode=pl.Buffered(1))


def rows_of(shape, axis):
    return pl.BlockSpec(shape, lambda i: tuple(i if a == axis else 0 for a in range(len(shape))))


def standard(stream):
    center = stream - jnp.mean(stream, -1, keepdims=True)
    inverse = lax.rsqrt(jnp.mean(center * center, -1, keepdims=True) + norm_eps)
    return (center * inverse, inverse)


def assemble_kernel(place_ref, near_ref, far_ref, next_near_ref, next_far_ref, out_ref, sems):
    z, x, core, y = (place_ref[i] for i in range(4))
    depth = out_ref.shape[1]
    copies = []
    for side, pair in enumerate(((near_ref, far_ref), (next_near_ref, next_far_ref))):
        source = core if side == 0 else 1 - core
        for stage, ref in enumerate(pair):
            for hop in range(2):
                by_x = jnp.where(source == 0, hop, stage)
                by_y = hop + stage - by_x
                for shift in range(depth):
                    target = out_ref.at[
                        lax.rem(y + by_y, 2),
                        lax.rem(z + depth - shift, depth),
                        lax.rem(x + by_x, 2),
                        source,
                    ]
                    copy = pltpu.make_async_copy(
                        ref.at[hop, shift], target, sems.at[len(copies)]
                    )
                    copy.start()
                    copies.append(copy)
    for copy in copies:
        copy.wait()


def assemble(place, near, far, next_near, next_far):
    _, depth, rows, columns = near.shape
    return pl.pallas_call(
        assemble_kernel,
        in_specs=[pl.BlockSpec(memory_space=pltpu.SMEM)]
        + [pl.BlockSpec(memory_space=pltpu.VMEM)] * 4,
        out_specs=pl.BlockSpec(memory_space=pl.ANY),
        out_shape=jax.ShapeDtypeStruct((2, depth, 2, 2, rows, columns), near.dtype),
        scratch_shapes=[pltpu.SemaphoreType.DMA((8 * depth,))],
        cost_estimate=pl.CostEstimate(
            flops=0, bytes_accessed=16 * near.size, transcendentals=0
        ),
        compiler_params=pltpu.CompilerParams(vmem_limit_bytes=32 * MIB),
        name="assemble",
    )(place, near, far, next_near, next_far)


def entry_kernel(
    token_ref, mod_ref, weight_ref, up_ref, down_ref, hidden_ref, middle_ref, qkv_ref, weight_aug
):
    @pl.when(pl.program_id(0) == 0)
    def _():
        weight_aug[:MODEL_WIDTH, :] = weight_ref[...]
        weight_aug[MODEL_WIDTH:, :] = up_ref[...]

    normed, _ = standard(token_ref[...].astype(jnp.float32))
    hidden = (normed * (1.0 + mod_ref[1:2]) + mod_ref[0:1]).astype(jnp.bfloat16)
    middle = nt(hidden, down_ref[...]).astype(jnp.bfloat16)
    hidden_ref[...] = hidden
    middle_ref[...] = middle
    joined = jnp.concatenate([hidden, middle], 1)
    for part in range(3):
        columns = slice(part * MODEL_WIDTH, (part + 1) * MODEL_WIDTH)
        packed = nn(joined, weight_aug[:, columns])
        qkv_ref[part] = packed.T.reshape(qkv_ref.shape[1:]).astype(jnp.bfloat16)


def entry(tokens, mods, weight, up, down, tile=256):
    length = tokens.shape[0]
    bf16 = jnp.bfloat16
    return pl.pallas_call(
        entry_kernel,
        grid=(length // tile,),
        in_specs=[
            rows_of((tile, MODEL_WIDTH), 0),
            once(mods.shape),
            once((MODEL_WIDTH, 3 * MODEL_WIDTH)),
            once(up.shape),
            once(down.shape),
        ],
        out_specs=[
            rows_of((tile, MODEL_WIDTH), 0),
            rows_of((tile, LANES), 0),
            rows_of((3, HEADS, HD, tile), 3),
        ],
        out_shape=[
            jax.ShapeDtypeStruct((length, MODEL_WIDTH), bf16),
            jax.ShapeDtypeStruct((length, LANES), bf16),
            jax.ShapeDtypeStruct((3, HEADS, HD, length), bf16),
        ],
        scratch_shapes=[pltpu.VMEM((PADDED, 3 * MODEL_WIDTH), bf16)],
        cost_estimate=pl.CostEstimate(
            flops=6 * length * MODEL_WIDTH * PADDED,
            bytes_accessed=2 * weight.size + 12 * length * MODEL_WIDTH,
            transcendentals=0,
        ),
        compiler_params=pltpu.CompilerParams(vmem_limit_bytes=56 * MIB),
        name="entry",
    )(tokens, mods, weight, up, down)


def load_proj(proj_aug, weight_ref, up_ref):
    @pl.when(pl.program_id(0) == 0)
    def _():
        proj_aug[:MODEL_WIDTH, :] = weight_ref[...]
        proj_aug[MODEL_WIDTH:, :] = up_ref[...]


def before_kernel(
    mixed_ref,
    token_ref,
    cot_ref,
    mod_ref,
    weight_ref,
    up_proj_ref,
    down_proj_ref,
    down_expand_ref,
    up_shrink_ref,
    bias_ref,
    second_ref,
    dfinal_ref,
    branch_ref,
    middle_ref,
    proj_aug,
):
    bf16 = jnp.bfloat16
    load_proj(proj_aug, weight_ref, up_proj_ref)
    mixed = transposed(mixed_ref[...]).astype(bf16)
    middle_proj = nt(mixed, down_proj_ref[...])
    branch = nn(jnp.concatenate([mixed, middle_proj.astype(bf16)], 1), proj_aug[...])
    branch = branch + bias_ref[...]
    branch_ref[...] = branch
    residual = token_ref[...].astype(jnp.float32) + mod_ref[2:3] * branch
    normed, _ = standard(residual)
    second = (normed * (1.0 + mod_ref[4:5]) + mod_ref[3:4]).astype(bf16)
    middle_expand = nt(second, down_expand_ref[...])
    second_ref[:, :MODEL_WIDTH] = second
    second_ref[:, MODEL_WIDTH:] = middle_expand.astype(bf16)
    d_final = (mod_ref[5:6] * cot_ref[...].astype(jnp.float32)).astype(bf16)
    dmiddle_shrink = nt(d_final, up_shrink_ref[...])
    dfinal_ref[:, :MODEL_WIDTH] = d_final
    dfinal_ref[:, MODEL_WIDTH:] = dmiddle_shrink.astype(bf16)
    middle_ref[0] = middle_proj.T[:RANK].astype(bf16)
    middle_ref[1] = middle_expand.T[:RANK].astype(bf16)
    middle_ref[2] = dmiddle_shrink.T[:RANK].astype(bf16)


def before_feed(
    mixed, tokens, cotangent, mods, weight, up_proj, down_proj, down_expand, up_shrink, bias, tile=256
):
    length = tokens.shape[0]
    bf16 = jnp.bfloat16
    return pl.pallas_call(
        before_kernel,
        grid=(length // tile,),
        in_specs=[
            rows_of((MODEL_WIDTH, tile), 1),
            rows_of((tile, MODEL_WIDTH), 0),
            rows_of((tile, MODEL_WIDTH), 0),
            once(mods.shape),
            pl.BlockSpec(
                (MODEL_WIDTH, MODEL_WIDTH), lambda *_: (0, 3), pipeline_mode=pl.Buffered(1)
            ),
            once(up_proj.shape),
            once(down_proj.shape),
            once(down_expand.shape),
            once(up_shrink.shape),
            once(bias.shape),
        ],
        out_specs=[
            rows_of((tile, PADDED), 0),
            rows_of((tile, PADDED), 0),
            rows_of((tile, MODEL_WIDTH), 0),
            rows_of((3, RANK, tile), 2),
        ],
        out_shape=[
            jax.ShapeDtypeStruct((length, PADDED), bf16),
            jax.ShapeDtypeStruct((length, PADDED), bf16),
            jax.ShapeDtypeStruct((length, MODEL_WIDTH), jnp.float32),
            jax.ShapeDtypeStruct((3, RANK, length), bf16),
        ],
        scratch_shapes=[pltpu.VMEM((PADDED, MODEL_WIDTH), bf16)],
        cost_estimate=pl.CostEstimate(
            flops=4 * length * MODEL_WIDTH * PADDED,
            bytes_accessed=16 * length * MODEL_WIDTH,
            transcendentals=0,
        ),
        compiler_params=pltpu.CompilerParams(vmem_limit_bytes=48 * MIB),
        name="before_feed",
    )(mixed, tokens, cotangent, mods, weight, up_proj, down_proj, down_expand, up_shrink, bias)


GELU_RATE = 0.7978845608
GELU_CUBE = 0.044715


def gelu_pair(inner, d_active):
    square = inner * inner
    tanh = jnp.tanh(inner * (GELU_RATE + (GELU_RATE * GELU_CUBE) * square))
    half = 0.5 + 0.5 * tanh
    slope = half + inner * (half * (1.0 - tanh)) * (
        GELU_RATE + (3.0 * GELU_CUBE * GELU_RATE) * square
    )
    return (inner * half).astype(jnp.bfloat16), (d_active * slope).astype(jnp.bfloat16)


def feed_kernel(
    second_ref, dfinal_ref, middle_ref, left_ref, right_ref, up_ref, down_ref, bias_ref,
    final_in_ref, dsecond_in_ref, final_ref, dsecond_ref, up_grad_ref, down_grad_ref,
    widen_aug, narrow_aug, *, rows, first, sub,
):
    width = MODEL_WIDTH
    chunks = left_ref.shape[-1] // width
    for chunk in range(chunks):
        rows_now = slice(chunk * width, (chunk + 1) * width)
        for side, ref in enumerate((left_ref, right_ref)):
            at = chunk * width + side * HALF
            widen_aug[:width, at : at + HALF] = ref[:, chunk * width : chunk * width + HALF]
            narrow_aug[rows_now, side * HALF : (side + 1) * HALF] = ref[
                :, chunk * width + HALF : (chunk + 1) * width
            ]
    widen_aug[width:, :] = up_ref[...]
    narrow_aug[:, width:] = down_ref[...]
    length = second_ref.shape[0]
    for index in range(chunks * width // sub):
        cols = slice(index * sub, (index + 1) * sub)
        for start in range(0, length, rows):
            at = slice(start, start + rows)
            inner = nn(second_ref[at, :], widen_aug[:, cols]) + bias_ref[:, cols]
            active, d_inner = gelu_pair(inner, nt(dfinal_ref[at, :], narrow_aug[cols, :]))
            final = nn(active, narrow_aug[cols, :])
            dsecond = nt(d_inner, widen_aug[:, cols])
            if index == 0 and first:
                final_ref[at, :] = final
                dsecond_ref[at, :] = dsecond
            elif index == 0:
                final_ref[at, :] = final_in_ref[at, :] + final
                dsecond_ref[at, :] = dsecond_in_ref[at, :] + dsecond
            else:
                final_ref[at, :] += final
                dsecond_ref[at, :] += dsecond
            up_grad = nn(middle_ref[1, :, at], d_inner)
            down_grad = nn(middle_ref[2, :, at], active)
            if start == 0:
                up_grad_ref[:, cols] = up_grad
                down_grad_ref[:, cols] = down_grad
            else:
                up_grad_ref[:, cols] += up_grad
                down_grad_ref[:, cols] += down_grad


def side_of(weight, side):
    width = weight.size // (2 * MODEL_WIDTH)
    if weight.ndim == 2:
        return pl.BlockSpec(
            (MODEL_WIDTH, width), lambda *_: (0, side), pipeline_mode=pl.Buffered(1)
        )
    return pl.BlockSpec(
        (None, MODEL_WIDTH, width), lambda *_: (side, 0, 0), pipeline_mode=pl.Buffered(1)
    )


def feed(second, dfinal, middles, weight, up, down, bias, sums, rows=1024, sub=768):
    length, padded = second.shape
    hidden = weight.size // (2 * MODEL_WIDTH)
    first = sums is None
    if first:
        sums = (jnp.zeros((8, LANES), jnp.float32),) * 2
    return pl.pallas_call(
        functools.partial(feed_kernel, rows=rows, first=first, sub=sub),
        grid=(1,),
        in_specs=[
            once((length, padded)), once((length, padded)), once(middles.shape),
            *(side_of(weight, side) for side in range(2)),
            once(up.shape), once(down.shape), once(bias.shape),
            once(sums[0].shape), once(sums[1].shape),
        ],
        out_specs=[once((length, padded)), once((length, padded)), once((RANK, hidden)), once((RANK, hidden))],
        out_shape=[
            jax.ShapeDtypeStruct((length, padded), jnp.float32),
            jax.ShapeDtypeStruct((length, padded), jnp.float32),
            jax.ShapeDtypeStruct((RANK, hidden), jnp.float32),
            jax.ShapeDtypeStruct((RANK, hidden), jnp.float32),
        ],
        scratch_shapes=[pltpu.VMEM((padded, hidden), jnp.bfloat16), pltpu.VMEM((hidden, padded), jnp.bfloat16)],
        input_output_aliases={} if first else {8: 0, 9: 1},
        cost_estimate=pl.CostEstimate(
            flops=8 * length * padded * hidden,
            bytes_accessed=weight.size + 12 * length * padded,
            transcendentals=length * hidden,
        ),
        compiler_params=pltpu.CompilerParams(vmem_limit_bytes=63 * MIB),
        name="feed",
    )(second, dfinal, middles, weight, weight, up, down, bias, *sums)


def back_through(gradient, normed, inverse):
    return inverse * (
        gradient
        - jnp.mean(gradient, -1, keepdims=True)
        - normed * jnp.mean(gradient * normed, -1, keepdims=True)
    )


def total(values):
    return jnp.sum(values, axis=0, keepdims=True)


def after_kernel(
    final_ref,
    dsecond_ref,
    token_ref,
    cot_ref,
    branch_ref,
    second_ref,
    dfinal_ref,
    mixed_ref,
    middle_ref,
    mod_ref,
    weight_ref,
    up_proj_ref,
    down_proj_ref,
    down_expand_ref,
    up_shrink_ref,
    bias_ref,
    block_ref,
    dresidual_ref,
    dmixed_ref,
    sums_ref,
    up_shrink_grad,
    down_expand_grad,
    up_proj_grad,
    down_proj_grad,
    proj_aug,
):
    bf16 = jnp.bfloat16
    load_proj(proj_aug, weight_ref, up_proj_ref)
    cot = cot_ref[...].astype(jnp.float32)
    branch = branch_ref[...]
    residual = token_ref[...].astype(jnp.float32) + mod_ref[2:3] * branch
    normed, inverse = standard(residual)
    middle_shrink = final_ref[:, MODEL_WIDTH:]
    final = final_ref[:, :MODEL_WIDTH] + bias_ref[...]
    final = final + nn(middle_shrink.astype(bf16), up_shrink_ref[...])
    block_ref[...] = (residual + mod_ref[5:6] * final).astype(bf16)
    dmiddle_expand = dsecond_ref[:, MODEL_WIDTH:]
    d_second = dsecond_ref[:, :MODEL_WIDTH] + nn(dmiddle_expand.astype(bf16), down_expand_ref[...])
    d_residual = cot + back_through(d_second * (1.0 + mod_ref[4:5]), normed, inverse)
    dresidual_ref[...] = d_residual
    d_branch = (mod_ref[2:3] * d_residual).astype(bf16)
    joined = nt(d_branch, proj_aug[...])
    dmiddle_proj = joined[:, MODEL_WIDTH:].astype(bf16)
    d_mixed = joined[:, :MODEL_WIDTH] + nn(dmiddle_proj, down_proj_ref[...])
    dmixed_ref[...] = d_mixed.T.astype(bf16)
    sums = jnp.concatenate(
        [
            total(d_residual * branch),
            total(d_second),
            total(d_second * normed),
            total(cot * final),
            jnp.zeros((4, MODEL_WIDTH), jnp.float32),
        ],
        0,
    )
    grads = (
        nn(middle_shrink.T[:RANK].astype(bf16), dfinal_ref[...]),
        nn(dmiddle_expand.T[:RANK].astype(bf16), second_ref[...]),
        nn(middle_ref[0], d_branch),
        nn(mixed_ref[...], dmiddle_proj),
    )
    refs = (up_shrink_grad, down_expand_grad, up_proj_grad, down_proj_grad)

    @pl.when(pl.program_id(0) == 0)
    def _():
        sums_ref[...] = sums
        for ref, grad in zip(refs, grads):
            ref[...] = grad

    @pl.when(pl.program_id(0) > 0)
    def _():
        sums_ref[...] += sums
        for ref, grad in zip(refs, grads):
            ref[...] += grad


def after_feed(
    final,
    dsecond,
    tokens,
    cotangent,
    branch,
    second,
    dfinal,
    mixed,
    middles,
    mods,
    weight,
    up_proj,
    down_proj,
    down_expand,
    up_shrink,
    bias,
    tile=256,
):
    length = tokens.shape[0]
    bf16, f32 = jnp.bfloat16, jnp.float32
    low_rank = jax.ShapeDtypeStruct((RANK, MODEL_WIDTH), f32)
    return pl.pallas_call(
        after_kernel,
        grid=(length // tile,),
        in_specs=[
            rows_of((tile, PADDED), 0),
            rows_of((tile, PADDED), 0),
            rows_of((tile, MODEL_WIDTH), 0),
            rows_of((tile, MODEL_WIDTH), 0),
            rows_of((tile, MODEL_WIDTH), 0),
            rows_of((tile, MODEL_WIDTH), 0),
            rows_of((tile, MODEL_WIDTH), 0),
            rows_of((MODEL_WIDTH, tile), 1),
            rows_of((3, RANK, tile), 2),
            once(mods.shape),
            pl.BlockSpec(
                (MODEL_WIDTH, MODEL_WIDTH), lambda *_: (0, 3), pipeline_mode=pl.Buffered(1)
            ),
            once(up_proj.shape),
            once(down_proj.shape),
            once(down_expand.shape),
            once(up_shrink.shape),
            once(bias.shape),
        ],
        out_specs=[
            rows_of((tile, MODEL_WIDTH), 0),
            rows_of((tile, MODEL_WIDTH), 0),
            rows_of((MODEL_WIDTH, tile), 1),
            once((8, MODEL_WIDTH)),
            once((RANK, MODEL_WIDTH)),
            once((RANK, MODEL_WIDTH)),
            once((RANK, MODEL_WIDTH)),
            once((MODEL_WIDTH, LANES)),
        ],
        out_shape=[
            jax.ShapeDtypeStruct((length, MODEL_WIDTH), bf16),
            jax.ShapeDtypeStruct((length, MODEL_WIDTH), f32),
            jax.ShapeDtypeStruct((MODEL_WIDTH, length), bf16),
            jax.ShapeDtypeStruct((8, MODEL_WIDTH), f32),
            low_rank,
            low_rank,
            low_rank,
            jax.ShapeDtypeStruct((MODEL_WIDTH, LANES), f32),
        ],
        scratch_shapes=[pltpu.VMEM((PADDED, MODEL_WIDTH), bf16)],
        cost_estimate=pl.CostEstimate(
            flops=5 * length * MODEL_WIDTH * PADDED,
            bytes_accessed=32 * length * MODEL_WIDTH,
            transcendentals=0,
        ),
        compiler_params=pltpu.CompilerParams(vmem_limit_bytes=60 * MIB),
        name="after_feed",
    )(
        final,
        dsecond,
        tokens,
        cotangent,
        branch,
        second,
        dfinal,
        mixed,
        middles,
        mods,
        weight,
        up_proj,
        down_proj,
        down_expand,
        up_shrink,
        bias,
    )


def leave_kernel(
    dqkv_ref,
    token_ref,
    dresidual_ref,
    hidden_ref,
    middle_ref,
    mod_ref,
    weight_ref,
    up_ref,
    down_ref,
    token_grad_ref,
    sums_ref,
    up_grad,
    down_grad,
    weight_aug,
):
    bf16 = jnp.bfloat16
    @pl.when(pl.program_id(0) == 0)
    def _():
        weight_aug[:MODEL_WIDTH, :] = weight_ref[...]
        weight_aug[MODEL_WIDTH:, :] = up_ref[...]

    tile = token_ref.shape[0]
    middle_t = transposed(middle_ref[...])[:RANK].astype(bf16)
    joined = jnp.zeros((tile, PADDED), jnp.float32)
    up_grads = []
    for part in range(3):
        columns = slice(part * MODEL_WIDTH, (part + 1) * MODEL_WIDTH)
        packed_t = dqkv_ref[part].astype(jnp.float32).reshape(MODEL_WIDTH, tile)
        packed = packed_t.T.astype(bf16)
        joined = joined + nt(packed, weight_aug[:, columns])
        up_grads.append(nn(middle_t, packed))
    dmiddle = joined[:, MODEL_WIDTH:]
    d_hidden = joined[:, :MODEL_WIDTH] + nn(dmiddle.astype(bf16), down_ref[...])
    normed, inverse = standard(token_ref[...].astype(jnp.float32))
    back = back_through(d_hidden * (1.0 + mod_ref[1:2]), normed, inverse)
    token_grad_ref[...] = (dresidual_ref[...] + back).astype(bf16)
    sums = jnp.concatenate(
        [total(d_hidden), total(d_hidden * normed), jnp.zeros((6, MODEL_WIDTH), jnp.float32)], 0
    )
    down = nn(dmiddle.T[:RANK].astype(bf16), hidden_ref[...])

    @pl.when(pl.program_id(0) == 0)
    def _():
        sums_ref[...] = sums
        down_grad[...] = down
        for part in range(3):
            up_grad[:, part * MODEL_WIDTH : (part + 1) * MODEL_WIDTH] = up_grads[part]

    @pl.when(pl.program_id(0) > 0)
    def _():
        sums_ref[...] += sums
        down_grad[...] += down
        for part in range(3):
            up_grad[:, part * MODEL_WIDTH : (part + 1) * MODEL_WIDTH] += up_grads[part]


def leave(dqkv, tokens, dresidual, hidden, middle, mods, weight, up, down, tile=256):
    length = tokens.shape[0]
    bf16, f32 = jnp.bfloat16, jnp.float32
    return pl.pallas_call(
        leave_kernel,
        grid=(length // tile,),
        in_specs=[
            rows_of((3, HEADS, HD, tile), 3),
            rows_of((tile, MODEL_WIDTH), 0),
            rows_of((tile, MODEL_WIDTH), 0),
            rows_of((tile, MODEL_WIDTH), 0),
            rows_of((tile, LANES), 0),
            once(mods.shape),
            once((MODEL_WIDTH, 3 * MODEL_WIDTH)),
            once(up.shape),
            once(down.shape),
        ],
        out_specs=[
            rows_of((tile, MODEL_WIDTH), 0),
            once((8, MODEL_WIDTH)),
            once((RANK, 3 * MODEL_WIDTH)),
            once((RANK, MODEL_WIDTH)),
        ],
        out_shape=[
            jax.ShapeDtypeStruct((length, MODEL_WIDTH), bf16),
            jax.ShapeDtypeStruct((8, MODEL_WIDTH), f32),
            jax.ShapeDtypeStruct((RANK, 3 * MODEL_WIDTH), f32),
            jax.ShapeDtypeStruct((RANK, MODEL_WIDTH), f32),
        ],
        scratch_shapes=[pltpu.VMEM((PADDED, 3 * MODEL_WIDTH), bf16)],
        cost_estimate=pl.CostEstimate(
            flops=7 * length * MODEL_WIDTH * PADDED,
            bytes_accessed=2 * weight.size + 18 * length * MODEL_WIDTH,
            transcendentals=0,
        ),
        compiler_params=pltpu.CompilerParams(vmem_limit_bytes=60 * MIB),
        name="leave",
    )(dqkv, tokens, dresidual, hidden, middle, mods, weight, up, down)


def layout(n_fsdp):
    return [(f // 4, f // 2 % 2, f % 2) for f in range(n_fsdp)]


def moved(n_fsdp, step):
    pairs = []
    for f, (z, x, c) in enumerate(layout(n_fsdp)):
        for y in range(2):
            to_z, to_x, to_c, to_y = step(z, x, c, y)
            pairs.append((2 * f + y, 2 * (4 * to_z + 2 * to_x + to_c) + to_y))
    return pairs


BOTH = ("fsdp", "seq")


def step_z(block, n_fsdp):
    depth = n_fsdp // 4
    by_shift = [block]
    for shift in range(1, depth):
        pairs = moved(n_fsdp, lambda z, x, c, y: ((z + shift) % depth, x, c, y))
        by_shift.append(lax.ppermute(block, BOTH, pairs))
    return jnp.stack(by_shift)


def step_first(block, n_fsdp):
    return lax.ppermute(
        block,
        BOTH,
        moved(n_fsdp, lambda z, x, c, y: (z, x, c, 1 - y) if c else (z, 1 - x, c, y)),
    )


def step_second(block, n_fsdp):
    return lax.ppermute(
        block,
        BOTH,
        moved(n_fsdp, lambda z, x, c, y: (z, 1 - x, c, y) if c else (z, x, c, 1 - y)),
    )


def step_core(block, n_fsdp):
    return lax.ppermute(block, BOTH, moved(n_fsdp, lambda z, x, c, y: (z, x, 1 - c, y)))


def behind(block, *earlier):
    for array in earlier:
        element = lax.slice(array, [n - 1 for n in array.shape], array.shape).reshape(())
        element = element.astype(jnp.float32)
        block = block + jnp.minimum(jnp.abs(element), 0.0).astype(block.dtype)
    return block


def gather_late(block, n_fsdp, place):
    line = step_z(block, n_fsdp)
    near = jnp.stack([line, step_first(line, n_fsdp)])
    far = step_second(near, n_fsdp)
    gathered = assemble(place, near, far, step_core(near, n_fsdp), step_core(far, n_fsdp))
    return gathered.reshape(2, n_fsdp * block.shape[0], block.shape[1])


DOWN_EDGES = (0, 1152, 2304, 3456, 4608, 9216)
UP_EDGES = (0, 6912, 10368, 11520, 16128, 17280)
PIECES = FF // HD


def piece_order(n_fsdp):
    per = PIECES // n_fsdp
    return [f * per + q for q in range(per) for f in range(n_fsdp)]


def unpack_kernel(came_ref, *refs, order, down_chunk, up_chunk):
    bf16 = jnp.bfloat16
    outs, (down_all, up_all, mixed) = refs[:-3], refs[-3:]
    down_outs, up_outs, shrink_t = outs[:4], outs[4:9], outs[9]
    for f in range(came_ref.shape[0]):
        block = came_ref[f].astype(jnp.float32)
        down_all[:, f * down_chunk : (f + 1) * down_chunk] = block[:, :down_chunk]
        up_all[:, f * up_chunk : (f + 1) * up_chunk] = block[:, down_chunk:]
    for target, out in enumerate(down_outs):
        out[...] = jnp.zeros_like(out)
        out[:RANK] = down_all[:, DOWN_EDGES[target] : DOWN_EDGES[target + 1]].astype(bf16)
    mixed[...] = jnp.zeros_like(mixed)
    for target, out in enumerate(up_outs):
        if target == 3:
            for to, piece in enumerate(order):
                at = UP_EDGES[3] + piece * HD
                mixed[:RANK, to * HD : (to + 1) * HD] = up_all[:, at : at + HD]
            out[...] = mixed[...].astype(bf16)
        else:
            out[...] = jnp.zeros_like(out)
            out[:RANK] = up_all[:, UP_EDGES[target] : UP_EDGES[target + 1]].astype(bf16)
    for to, piece in enumerate(order):
        at = DOWN_EDGES[4] + piece * HD
        mixed[:RANK, to * HD : (to + 1) * HD] = down_all[:, at : at + HD]
    for start in range(0, FF, MODEL_WIDTH):
        shrink_t[start : start + MODEL_WIDTH, :] = mixed[:, start : start + MODEL_WIDTH].T.astype(
            bf16
        )


def unpack(came, order, down_chunk, up_chunk):
    bf16 = jnp.bfloat16
    widths = [DOWN_EDGES[t + 1] - DOWN_EDGES[t] for t in range(4)]
    widths += [UP_EDGES[t + 1] - UP_EDGES[t] for t in range(5)]
    return pl.pallas_call(
        functools.partial(
            unpack_kernel, order=order, down_chunk=down_chunk, up_chunk=up_chunk
        ),
        out_shape=[jax.ShapeDtypeStruct((LANES, w), bf16) for w in widths]
        + [jax.ShapeDtypeStruct((FF, LANES), bf16)],
        scratch_shapes=[
            pltpu.VMEM((RANK, DOWN_EDGES[5]), jnp.float32),
            pltpu.VMEM((RANK, UP_EDGES[5]), jnp.float32),
            pltpu.VMEM((LANES, FF), jnp.float32),
        ],
        compiler_params=pltpu.CompilerParams(vmem_limit_bytes=48 * MIB),
        name="unpack",
    )(came)


def pack_kernel(
    leave_ref,
    after_ref,
    middle_ref,
    cond_ref,
    down_ada_ref,
    up_ada_ref,
    down_qkv,
    up_qkv,
    down_proj,
    up_proj,
    down_expand,
    up_expand_low,
    up_expand_high,
    down_shrink_low,
    down_shrink_high,
    up_shrink,
    sent_ref,
    dmod_ref,
    own_ref,
    down_all,
    up_all,
    *,
    order,
    down_chunk,
    up_chunk,
):
    bf16, f32 = jnp.bfloat16, jnp.float32
    width = MODEL_WIDTH
    dmiddle = jnp.zeros((RANK, 1), f32)
    for block in range(6):
        source = leave_ref if block < 2 else after_ref
        line = source[block % 2 if block < 2 else block - 2, :].reshape(1, width)
        line = line.astype(bf16).astype(f32)
        columns = slice(block * width, (block + 1) * width)
        side, at = block // 3, block % 3 * width
        dmod_ref[side : side + 1, at : at + width] = line
        up_all[:, columns] = middle_ref[...] * line
        dmiddle += jnp.sum(up_ada_ref[:RANK, columns].astype(f32) * line, axis=1, keepdims=True)
    dmiddle = dmiddle.astype(bf16).astype(f32)
    down_all[:, :width] = dmiddle * cond_ref[...]
    own_ref[...] = total(dmiddle * down_ada_ref[:RANK].astype(f32))
    down_all[:, width : 2 * width] = down_qkv[...]
    down_all[:, 2 * width : 3 * width] = down_proj[...].T[:RANK]
    down_all[:, 3 * width : 4 * width] = down_expand[...]
    up_all[:, UP_EDGES[1] : UP_EDGES[2]] = up_qkv[...]
    up_all[:, UP_EDGES[2] : UP_EDGES[3]] = up_proj[...]
    up_all[:, UP_EDGES[4] : UP_EDGES[5]] = up_shrink[...]
    half = PIECES // 2
    for at, piece in enumerate(order):
        ups = up_expand_low if at < half else up_expand_high
        downs = down_shrink_low if at < half else down_shrink_high
        columns = slice((at % half) * HD, (at % half + 1) * HD)
        to = UP_EDGES[3] + piece * HD
        up_all[:, to : to + HD] = ups[:, columns]
        to = DOWN_EDGES[4] + piece * HD
        down_all[:, to : to + HD] = downs[:, columns]
    for f in range(sent_ref.shape[0]):
        sent_ref[f, :, :down_chunk] = down_all[:, f * down_chunk : (f + 1) * down_chunk].astype(bf16)
        sent_ref[f, :, down_chunk:] = up_all[:, f * up_chunk : (f + 1) * up_chunk].astype(bf16)


def pack(operands, n_fsdp, order, down_chunk, up_chunk):
    bf16, f32 = jnp.bfloat16, jnp.float32
    return pl.pallas_call(
        functools.partial(pack_kernel, order=order, down_chunk=down_chunk, up_chunk=up_chunk),
        out_shape=[
            jax.ShapeDtypeStruct((n_fsdp, RANK, down_chunk + up_chunk), bf16),
            jax.ShapeDtypeStruct((2, 3 * MODEL_WIDTH), f32),
            jax.ShapeDtypeStruct((1, MODEL_WIDTH), f32),
        ],
        scratch_shapes=[
            pltpu.VMEM((RANK, DOWN_EDGES[5]), f32),
            pltpu.VMEM((RANK, UP_EDGES[5]), f32),
        ],
        compiler_params=pltpu.CompilerParams(vmem_limit_bytes=48 * MIB),
        name="pack",
    )(*operands)


def owners_kernel(ids_ref, place_ref, came_ref, kept_ref, given_ref, sums):
    sums[...] = jnp.zeros_like(sums)
    for f in range(came_ref.shape[0]):
        sums[ids_ref[f]] += came_ref[f].astype(jnp.float32)
    held = kept_ref.shape[0]
    mine = place_ref[3]
    for index in range(held):
        kept_ref[index] = sums[mine * held + index]
        given_ref[index] = sums[(1 - mine) * held + index].astype(jnp.bfloat16)


def owners(ids, place, came):
    held = ADAPTER_COUNT // 2
    shape = (held,) + came.shape[1:]
    return pl.pallas_call(
        owners_kernel,
        in_specs=[
            pl.BlockSpec(memory_space=pltpu.SMEM),
            pl.BlockSpec(memory_space=pltpu.SMEM),
            pl.BlockSpec(memory_space=pltpu.VMEM),
        ],
        out_shape=[
            jax.ShapeDtypeStruct(shape, jnp.float32),
            jax.ShapeDtypeStruct(shape, jnp.bfloat16),
        ],
        scratch_shapes=[pltpu.VMEM((ADAPTER_COUNT,) + came.shape[1:], jnp.float32)],
        compiler_params=pltpu.CompilerParams(vmem_limit_bytes=32 * MIB),
        name="owners",
    )(ids, place, came)


def update_kernel(gradient_ref, squared_ref, *refs):
    down_chunk = refs[0].shape[-1]
    grad_norm = jnp.sqrt(jnp.sum(squared_ref[:, :1], axis=0, keepdims=True))
    clip_factor = jnp.minimum(1.0, clip_limit / (grad_norm + norm_eps))
    ins, outs, norm_ref = refs[:6], refs[6:12], refs[12]
    norm_ref[...] = jnp.broadcast_to(grad_norm, norm_ref.shape)
    for kind in range(2):
        part = slice(0, down_chunk) if kind == 0 else slice(down_chunk, None)
        for index in range(gradient_ref.shape[0]):
            gradient = gradient_ref[index, :, part] * clip_factor
            params = ins[kind][index]
            moment_new = beta_first * ins[2 + kind][index] + (1.0 - beta_first) * gradient
            square_new = (
                beta_second * ins[4 + kind][index] + (1.0 - beta_second) * gradient * gradient
            )
            direction = (
                moment_new
                / (1.0 - beta_first**STEP)
                / (jnp.sqrt(square_new / (1.0 - beta_second**STEP)) + adam_eps)
            )
            outs[kind][index] = params - learn_rate * (direction + decay_rate * params)
            outs[2 + kind][index] = moment_new
            outs[4 + kind][index] = square_new


def update(gradient, squared, states):
    f32 = jnp.float32
    outs = pl.pallas_call(
        update_kernel,
        out_shape=[jax.ShapeDtypeStruct(s.shape, f32) for s in states]
        + [jax.ShapeDtypeStruct((8, LANES), f32)],
        compiler_params=pltpu.CompilerParams(vmem_limit_bytes=32 * MIB),
        name="update",
    )(gradient, squared, *states)
    return outs[:6], outs[6][0, 0]


def fits(mesh):
    return mesh.shape["seq"] == MB and mesh.shape["fsdp"] == 16


def dot(equation, left, right):
    return jnp.einsum(equation, left, right, preferred_element_type=jnp.float32)


def swap(block):
    return lax.ppermute(block, "seq", [(0, 1), (1, 0)])


def by_seq(own, other, mine):
    first = mine == 0
    return jnp.stack([jnp.where(first, own, other), jnp.where(first, other, own)])


def swap_rows(halves, mine):
    kept, came = send_row(halves, mine)
    return by_seq(kept, came, mine)


def send_row(halves, mine):
    sent = lax.dynamic_index_in_dim(halves, 1 - mine, 0, False)
    return lax.dynamic_index_in_dim(halves, mine, 0, False), swap(sent)


def to_all(block):
    return lax.all_to_all(block, ("fsdp", "seq"), split_axis=0, concat_axis=0, tiled=True)


def to_fsdp(block):
    return lax.all_to_all(block, "fsdp", split_axis=0, concat_axis=0, tiled=True)


def fast_shards(
    tokens,
    condition,
    adapter,
    cotangent,
    modulation_weight,
    modulation_bias,
    query_key_value_weight,
    attention_out_weight,
    attention_out_bias,
    widen_weight,
    widen_bias,
    narrow_weight,
    narrow_bias,
    lowrank_down,
    lowrank_up,
    first_moment_down,
    first_moment_up,
    second_moment_down,
    second_moment_up,
):
    bf16 = jnp.bfloat16
    n_fsdp = lax.axis_size("fsdp")
    mine = lax.axis_index("seq")
    row = lax.axis_index("fsdp")
    place = jnp.stack([row // 4, row // 2 % 2, row % 2, mine]).astype(jnp.int32)
    down_chunk, up_chunk = lowrank_down.shape[-1], lowrank_up.shape[-1]
    depth = modulation_weight.shape[0]
    order = piece_order(n_fsdp)
    per = PIECES // n_fsdp

    cond_act_pair = jax.nn.silu(condition).astype(bf16)
    told = jnp.moveaxis(cond_act_pair.reshape(MB, n_fsdp, depth), 1, 0)
    numbers = jnp.broadcast_to(adapter.astype(bf16)[None, :, None], (n_fsdp, MB, 8))
    told = to_fsdp(jnp.concatenate([told, numbers], 2))
    own_ids = lax.dynamic_index_in_dim(told[:, :, depth], mine, 1, False).astype(jnp.int32)

    wide = jnp.moveaxis(widen_weight.reshape(depth, -1, per, HD), 2, 0).reshape(per, depth, HALF)
    narrow = narrow_weight.reshape(per, depth, HALF)

    def whole(block):
        return lax.all_gather(block, "fsdp", axis=0, tiled=True)

    heads = jnp.concatenate([query_key_value_weight, attention_out_weight], 1)
    heads = by_seq(heads, swap(heads), mine)
    cut = query_key_value_weight.shape[1]
    heads_weight = whole(
        jnp.concatenate([heads[0, :, :cut], heads[1, :, :cut], heads[0, :, cut:], heads[1, :, cut:]], 1)
    )
    joined = [jnp.concatenate([wide[q], narrow[q]], 1) for q in range(per)]
    low = jnp.concatenate(joined[: per // 2], 1)
    low = by_seq(low, swap(low), mine)
    low_weight = whole(jnp.concatenate([low[0], low[1]], 1))
    high_weight = gather_late(jnp.concatenate(joined[per // 2 :], 1), n_fsdp, place)

    portions = jnp.concatenate([lowrank_down.astype(bf16), lowrank_up.astype(bf16)], -1)
    others = swap(portions)
    table = by_seq(portions, others, mine).reshape(ADAPTER_COUNT, RANK, -1)
    picks = jax.nn.one_hot(own_ids, ADAPTER_COUNT, dtype=bf16)
    chosen = dot("fa,arc->frc", picks, table).astype(bf16)
    parts = unpack(to_fsdp(chosen), order, down_chunk, up_chunk)
    down_ada, down_qkv, down_proj, down_expand = parts[:4]
    up_ada, up_qkv, up_proj, up_expand, up_shrink = parts[4:9]
    down_shrink_t = parts[9]

    spoken = told[:, :, :depth].reshape(n_fsdp * MB, depth)
    mod_part = to_all(dot("si,io->so", spoken, modulation_weight))
    mod_base = jnp.sum(mod_part.reshape(n_fsdp, MB, -1), axis=0).reshape(1, -1)

    cond_act = lax.dynamic_slice_in_dim(cond_act_pair, mine, 1, 0)
    middle_ada = dot("ti,ri->tr", cond_act, down_ada).astype(bf16)
    modulation = mod_base + modulation_bias + dot("tr,ro->to", middle_ada, up_ada)
    mods = jnp.pad(modulation.reshape(6, MODEL_WIDTH), ((0, 2), (0, 0)))

    length = MB * tokens.shape[1]
    token_rows = swap_rows(tokens, mine).reshape(length, MODEL_WIDTH)
    cot_rows = swap_rows(cotangent, mine).reshape(length, MODEL_WIDTH)

    hidden, middle_qkv, qkv = entry(token_rows, mods, heads_weight, up_qkv, down_qkv)
    mixed_heads, log_total = heads_forward(qkv, step=length)
    mixed = mixed_heads.reshape(MODEL_WIDTH, length)
    second, dfinal, branch, middles = before_feed(
        mixed,
        token_rows,
        cot_rows,
        mods,
        heads_weight,
        up_proj,
        down_proj,
        down_expand,
        up_shrink,
        attention_out_bias[None],
    )
    bias = jnp.moveaxis(widen_bias.reshape(n_fsdp, per, HD), 0, 1).reshape(1, FF)
    cut = FF // 2
    final, dsecond, up_expand_low, down_shrink_low = feed(
        second,
        dfinal,
        middles,
        low_weight,
        up_expand[:, :cut],
        down_shrink_t[:cut],
        bias[:, :cut],
        None,
    )
    final, dsecond, up_expand_high, down_shrink_high = feed(
        second,
        dfinal,
        middles,
        high_weight,
        up_expand[:, cut:],
        down_shrink_t[cut:],
        bias[:, cut:],
        (final, dsecond),
    )
    (
        block_rows,
        d_residual,
        d_mixed,
        after_sums,
        up_shrink_grad,
        down_expand_grad,
        up_proj_grad,
        down_proj_grad,
    ) = after_feed(
        final,
        dsecond,
        token_rows,
        cot_rows,
        branch,
        second,
        dfinal,
        mixed,
        middles,
        mods,
        heads_weight,
        up_proj,
        down_proj,
        down_expand,
        up_shrink,
        narrow_bias[None],
    )
    block_out = swap_rows(block_rows.reshape(tokens.shape), mine)
    d_qkv = heads_back(
        qkv, d_mixed.reshape(HEADS, HD, length), mixed_heads, log_total, step=length
    )
    token_rows_grad, leave_sums, up_qkv_grad, down_qkv_grad = leave(
        d_qkv, token_rows, d_residual, hidden, middle_qkv, mods, heads_weight, up_qkv, down_qkv
    )

    halves = token_rows_grad.reshape(tokens.shape)
    token_sent = lax.dynamic_index_in_dim(halves, 1 - mine, 0, False)
    token_came = swap(token_sent)
    leave_sums = behind(leave_sums, token_sent)

    sent, d_modulation, own_cond = pack(
        (
            leave_sums,
            after_sums,
            middle_ada[:, :RANK].astype(jnp.float32).T,
            cond_act.astype(jnp.float32),
            down_ada,
            up_ada,
            down_qkv_grad,
            up_qkv_grad,
            down_proj_grad,
            up_proj_grad,
            down_expand_grad,
            up_expand_low,
            up_expand_high,
            down_shrink_low,
            down_shrink_high,
            up_shrink_grad,
        ),
        n_fsdp,
        order,
        down_chunk,
        up_chunk,
    )
    kept, given = owners(own_ids, place, to_fsdp(sent))
    gradient = kept + swap(given).astype(jnp.float32)
    squared = to_all(jnp.broadcast_to(jnp.sum(gradient * gradient), (n_fsdp * MB, LANES)))

    half_weight = lax.all_gather(
        behind(modulation_weight, second), "fsdp", axis=0, tiled=True
    )
    both_mod = behind(swap_rows(d_modulation.astype(bf16), mine), kept)
    d_cond = dot("so,io->si", both_mod, half_weight)
    d_cond = d_cond + jnp.where(jnp.arange(MB)[:, None] == mine, own_cond, 0.0)
    d_cond = d_cond + swap(d_cond)
    cond_grad = jax.vjp(jax.nn.silu, condition)[1](d_cond)[0]
    token_kept, token_came = send_row(token_rows_grad.reshape(tokens.shape), mine)
    token_kept = lax.dynamic_index_in_dim(halves, mine, 0, False)
    token_grad = by_seq(behind(token_kept, gradient), token_came, mine).astype(jnp.float32)

    states = (
        lowrank_down,
        lowrank_up,
        first_moment_down,
        first_moment_up,
        second_moment_down,
        second_moment_up,
    )
    fresh, grad_norm = update(gradient, squared, states)
    return (block_out, token_grad, cond_grad, grad_norm, *fresh)


def solution(mesh):
    in_specs = (
        P("fsdp", "seq", None),
        P("fsdp", None),
        P("fsdp"),
        P("fsdp", "seq", None),
        P("fsdp", "seq"),
        P(),
        P("fsdp", "seq"),
        P("fsdp", "seq"),
        P(),
        P("fsdp", "seq"),
        P(),
        P("fsdp", "seq"),
        P(),
        P("seq", None, "fsdp"),
        P("seq", None, "fsdp"),
        P("seq", None, "fsdp"),
        P("seq", None, "fsdp"),
        P("seq", None, "fsdp"),
        P("seq", None, "fsdp"),
    )
    out_specs = (
        P("fsdp", "seq", None),
        P("fsdp", "seq", None),
        P("fsdp", None),
        P(),
        P("seq", None, "fsdp"),
        P("seq", None, "fsdp"),
        P("seq", None, "fsdp"),
        P("seq", None, "fsdp"),
        P("seq", None, "fsdp"),
        P("seq", None, "fsdp"),
    )
    body = fast_shards if fits(mesh) else shards
    return jax.shard_map(body, mesh=mesh, in_specs=in_specs, out_specs=out_specs, check_vma=False)
```
